128 devices in a mesh: pack: 8 (over z, core), seq: 16 (over x, y).
Axes of the slice: x: 4, y: 4, z: 4, core: 2. Of those that a mesh axis runs over, the one named last changes fastest.
Arguments:
- inputs: bfloat16 [8, 8192, 512], P('pack', 'seq'), may hold values from -6 to 6
- w_query: bfloat16 [512, 512], replicated, may hold values from -0.25 to 0.25
- w_key: bfloat16 [512, 512], replicated, may hold values from -0.25 to 0.25
- w_value: bfloat16 [512, 512], replicated, may hold values from -0.25 to 0.25
- w_output: bfloat16 [512, 512], replicated, may hold values from -6 to 6
- w_up: bfloat16 [512, 2048], replicated, may hold values from -0.25 to 0.25
- w_down: bfloat16 [2048, 512], replicated, may hold values from -0.125 to 0.125
- gain_attn: float32 [512], replicated, may hold values from 0.5 to 1.5
- gain_ffn: float32 [512], replicated, may hold values from 0.5 to 1.5
- random_features: bfloat16 [8, 64, 256], replicated, may hold values from -4 to 4
- doc_ids: int32 [8, 8192], P('pack', 'seq'), may hold values from 0 to 9, as said below
- live_rows: int32 [8, 8192], P('pack', 'seq'), may hold values from 0 to 1, as said below
- cotangent: bfloat16 [8, 8192, 512], P('pack', 'seq'), may hold values from -6 to 6
Outputs:
- outputs: bfloat16 [8, 8192, 512], P('pack', 'seq')
- grad_inputs: bfloat16 [8, 8192, 512], P('pack', 'seq')
- grad_w_query: float32 [512, 512], replicated
- grad_w_key: float32 [512, 512], replicated
- grad_w_value: float32 [512, 512], replicated
- grad_w_output: float32 [512, 512], replicated
- grad_w_up: float32 [512, 2048], replicated
- grad_w_down: float32 [2048, 512], replicated
- grad_gain_attn: float32 [512], replicated
- grad_gain_ffn: float32 [512], replicated
The draws below stay inside these ranges and needn't reach their ends.
Inputs may be any that keep to these rules, and one draw needn't show every extreme that they name: `doc_ids`: document numbers never fall along a pack, and each of the 10 documents of a pack has at least one row. `live_rows`: the first row of every document is live.
All inputs are finite; a program needn't handle non-finite values.
Results may differ from the reference program's by a relative error of at most 0.025.
Values sent between devices are 32-bit elements; how exact they have to be, the bound alone decides.
A program may use at most 128 MiB of HBM per device.

```python
import math
import jax
import jax.numpy as jnp
from jax import lax

D = 512
H = 8
DH = 64
M = 256
FF = 2048
SEGS = 10
TOK_DEV = 512
LENGTH = 8192
PACKS = 8


def boundaries(key):
    pack_keys = jax.random.split(key, PACKS)
    spacing = max(1, TOK_DEV // (2 * SEGS))
    places = (TOK_DEV - 1) // spacing

    def one_pack(pack_key):
        count_key, head_key, tail_key = jax.random.split(pack_key, 3)
        before = jax.random.randint(count_key, (), 0, SEGS)
        head_cut = (jnp.sort(jax.random.permutation(head_key, places)[:SEGS - 1]) + 1) * spacing
        tail_cut = jnp.sort(LENGTH - (jax.random.permutation(tail_key, places)[:SEGS - 1] + 1) * spacing)
        order = jnp.arange(SEGS - 1, dtype=jnp.int32)
        return jnp.where(order < before, head_cut, tail_cut).astype(jnp.int32)
    return jax.vmap(one_pack)(pack_keys)


def draw_doc_ids(key, part):
    cuts = boundaries(key)
    positions = jnp.arange(LENGTH, dtype=jnp.int32)
    passed = (positions[None, :, None] >= cuts[:, None, :]).astype(jnp.int32)
    return jnp.sum(passed, axis=-1).astype(jnp.int32)


def draw_live_rows(key, part):
    cuts = boundaries(key)
    key = jax.random.fold_in(key, 7)
    coins = jax.random.randint(key, (PACKS, LENGTH), 0, 8)
    positions = jnp.arange(LENGTH, dtype=jnp.int32)
    leading = (positions[None, :] == 0) | jnp.any(positions[None, :, None] == cuts[:, None, :], axis=-1)
    return jnp.where(leading | (coins < 7), 1, 0).astype(jnp.int32)


def steps_of(key, dims, cuts, least, high):
    gain = 1.0
    for position, shards_of in cuts:
        draws = jax.random.uniform(jax.random.fold_in(jax.random.fold_in(key, 6), position), (shards_of,), jnp.float32, least / len(cuts), high / len(cuts))
        gain = gain * jnp.repeat(jnp.exp(draws), dims[position] // shards_of).reshape((-1,) + (1,) * (len(dims) - 1 - position))
    return gain


def scatter_about(stream_key, extent, scale, most, shards=(), kind=jnp.bfloat16):
    values = scale * jax.random.normal(stream_key, extent, jnp.float32)
    if shards:
        values = values * steps_of(stream_key, extent, shards, -0.22, 0.18)
    return jnp.clip(values, -most, most).astype(kind)


def setup_inputs(seed: int = 0) -> dict:
    key_list = jax.random.split(jax.random.key(seed), 14)
    return {
        "inputs": scatter_about(key_list[0], (PACKS, LENGTH, D), 1.0, 6.0, ((0, 8), (1, 16))),
        "w_query": scatter_about(key_list[1], (D, D), D ** -0.5, 0.25),
        "w_key": scatter_about(key_list[2], (D, D), D ** -0.5, 0.25),
        "w_value": scatter_about(key_list[3], (D, D), D ** -0.5, 0.25),
        "w_output": scatter_about(key_list[4], (D, D), 1 ** -0.5, 6.0),
        "w_up": scatter_about(key_list[5], (D, FF), D ** -0.5, 0.25),
        "w_down": scatter_about(key_list[6], (FF, D), FF ** -0.5, 0.125),
        "gain_attn": jnp.clip(jax.random.uniform(key_list[7], (D,), jnp.float32, 0.5, 1.5), 0.5, 1.5),
        "gain_ffn": jnp.clip(jax.random.uniform(key_list[8], (D,), jnp.float32, 0.5, 1.5), 0.5, 1.5),
        "random_features": scatter_about(key_list[9], (H, DH, M), 1.0, 4.0),
        "doc_ids": draw_doc_ids(jax.random.fold_in(key_list[13], 71), 0),
        "live_rows": draw_live_rows(jax.random.fold_in(key_list[13], 71), 0),
        "cotangent": scatter_about(key_list[12], (PACKS, LENGTH, D), 1.0, 6.0, ((0, 8), (1, 16))),
    }


epsilon = 1e-05
highest_precision_flag = lax.Precision.HIGHEST

@jax.custom_vjp
def low(v):
    return lax.optimization_barrier(v.astype(jnp.bfloat16)).astype(jnp.float32)

@jax.custom_vjp
def low_back(v):
    return v

def low_keep(v):
    return (low(v), None)

def low_pass(kept, grad):
    return (grad,)

def back_keep(v):
    return (v, None)

def back_low(kept, grad):
    return (low(grad),)
low.defvjp(low_keep, low_pass)
low_back.defvjp(back_keep, back_low)

def rounded(values):
    return low_back(low(values))

def matmul(left_side, right_side):
    return jnp.dot(left_side, right_side, precision=highest_precision_flag, preferred_element_type=jnp.float32)

def layer_norm(values, gain_vec):
    average = lax.optimization_barrier(jnp.mean(values, axis=-1, keepdims=True))
    centred = values - average
    spread = lax.optimization_barrier(jnp.mean(centred * centred, axis=-1, keepdims=True))
    return centred * lax.rsqrt(spread + epsilon) * gain_vec

def feature_map(head_rows, features):
    project = low_back(jnp.einsum('thd,hdm->thm', head_rows, features, precision=highest_precision_flag))
    square = lax.optimization_barrier(jnp.sum(head_rows * head_rows, axis=-1, keepdims=True))
    factor = DH ** (-0.25)
    return jnp.exp(factor * project - 0.5 * factor * factor * square) / math.sqrt(M)

def doc_summaries(phi_key, value_head_rows, onehot):

    def one_doc(mask):
        weighted_value_rows = phi_key * mask[:, None, None]
        return (jnp.einsum('psx,psl->sxl', weighted_value_rows, value_head_rows, precision=highest_precision_flag), lax.optimization_barrier(jnp.sum(weighted_value_rows, axis=0)))
    return lax.map(jax.checkpoint(one_doc), jnp.transpose(onehot))

def doc_reads(phi_query, summary, totals, onehot):
    seq_rows = phi_query.shape[0]

    def one_doc(carry, pieces):
        numerator_rows, denom = carry
        mask, document_summary_state, doc_totals = pieces
        weighted_value_rows = phi_query * mask[:, None, None]
        numerator_rows = numerator_rows + jnp.einsum('sni,nip->snp', weighted_value_rows, document_summary_state, precision=highest_precision_flag)
        denom = denom + jnp.einsum('thm,hm->th', weighted_value_rows, doc_totals, precision=highest_precision_flag)
        return ((numerator_rows, denom), None)
    start = (jnp.zeros((seq_rows, H, DH), jnp.float32), jnp.zeros((seq_rows, H), jnp.float32))
    (numerator_rows, denom), unused = lax.scan(jax.checkpoint(one_doc), start, (jnp.transpose(onehot), summary, totals))
    return (numerator_rows, denom)

def pack_layer(params, rows, features, onehot, live_mask):
    w_query, w_key, w_value, w_output, w_up, w_down, gain_attn, gain_ffn = params
    seq_rows = rows.shape[0]
    normed = rounded(layer_norm(rows, gain_attn))
    query_heads = rounded(matmul(normed, w_query)).reshape(seq_rows, H, DH)
    key_heads = rounded(matmul(normed, w_key)).reshape(seq_rows, H, DH)
    value_head_rows = rounded(matmul(normed, w_value)).reshape(seq_rows, H, DH)
    phi_query = rounded(feature_map(query_heads, features))
    phi_key = rounded(feature_map(key_heads, features) * live_mask[:, None, None])
    summary_sums, totals = doc_summaries(phi_key, value_head_rows, onehot)
    summary = rounded(summary_sums)
    numerator_rows, denominator = doc_reads(phi_query, summary, totals, onehot)
    numerator = low_back(numerator_rows)
    attended = rounded((numerator / denominator[:, :, None]).reshape(seq_rows, D))
    middle = rows + low_back(matmul(attended, w_output))
    hidden = rounded(layer_norm(middle, gain_ffn))
    upward_projection = low_back(matmul(hidden, w_up))
    activated = rounded(jax.nn.gelu(upward_projection))
    return middle + matmul(activated, w_down)

def reference(inputs, w_query, w_key, w_value, w_output, w_up, w_down, gain_attn, gain_ffn, random_features, doc_ids, live_rows, cotangent):
    params = tuple((weight.astype(jnp.float32) for weight in (w_query, w_key, w_value, w_output, w_up, w_down, gain_attn, gain_ffn)))
    features = random_features.astype(jnp.float32)

    def add_up(first, second):
        return first + second

    def one_pack(running, pieces):
        rows, doc_rows, live, cot_rows = pieces
        onehot = (doc_rows[:, None] == jnp.arange(SEGS, dtype=jnp.int32)[None, :]).astype(jnp.float32)
        live_mask = live.astype(jnp.float32)

        def forward(params_in, rows_in):
            return pack_layer(params_in, rows_in, features, onehot, live_mask)
        result, pullback = jax.vjp(forward, params, rows.astype(jnp.float32))
        grad_params, grad_rows = pullback(cot_rows.astype(jnp.float32))
        running = jax.tree.map(add_up, running, grad_params)
        return (running, (result.astype(jnp.bfloat16), grad_rows.astype(jnp.bfloat16)))
    initial = jax.tree.map(jnp.zeros_like, params)
    summed, (outputs, grad_inputs) = lax.scan(one_pack, initial, (inputs, doc_ids, live_rows, cotangent))
    return (outputs, grad_inputs, summed[0], summed[1], summed[2], summed[3], summed[4], summed[5], summed[6], summed[7])
```

```python
import functools
import math

import jax
import jax.numpy as jnp
from jax import lax
from jax.experimental import pallas as pl
from jax.experimental.pallas import tpu as pltpu
from jax.sharding import PartitionSpec as P

SEGS = 10


epsilon = 1e-05
highest_precision_flag = lax.Precision.HIGHEST


def layer_norm(values, gain_vec):
    average = jnp.mean(values, axis=-1, keepdims=True)
    centred = values - average
    spread = jnp.mean(centred * centred, axis=-1, keepdims=True)
    return centred * lax.rsqrt(spread + epsilon) * gain_vec


def feature_exp(project, head_float):
    square = jnp.sum(head_float * head_float, axis=-1, keepdims=True)
    factor = head_float.shape[-1] ** (-0.25)
    return jnp.exp(factor * project - 0.5 * factor * factor * square) / math.sqrt(project.shape[-1])


def contract(left_side, right_side, left_dim, right_dim):
    return lax.dot_general(
        left_side,
        right_side,
        (((left_dim,), (right_dim,)), ((), ())),
        preferred_element_type=jnp.float32,
    )


MESH = pl.DeviceIdType.MESH
SLAB = 136
COLORS = 6
DIM_ORDER = (0, 2, 4, 1, 3, 5)


def place():
    pack, seq = lax.axis_index("pack"), lax.axis_index("seq")
    return pack // 2, pack % 2, seq // 4, seq % 4


def neighbour(dim, z, core, x, y):
    axis = dim // 2
    here = (x, y, z)[axis]
    if dim % 2 == 0:
        there, side = here + 1 - 2 * (here % 2), ((here + 1) // 2) % 2
    else:
        there, side = 3 - here, here // 2
    x = there if axis == 0 else x
    y = there if axis == 1 else y
    z = there if axis == 2 else z
    return (z * 2 + core, x * 4 + y), side


def exchange(out_ref, in_ref, back_ref, got_ref, sems, pack, seq):
    first = []
    for step in range(1, 16):
        peer = lax.rem(seq + step, 16)
        copy = pltpu.make_async_remote_copy(
            src_ref=out_ref.at[peer], dst_ref=in_ref.at[seq],
            send_sem=sems.at[0, step - 1], recv_sem=sems.at[1, step - 1],
            device_id=(pack, peer), device_id_type=MESH)
        copy.start()
        first.append(copy)
    in_ref[seq] = out_ref[seq]
    for copy in first:
        copy.wait()
    carry = jnp.zeros((64, 128), jnp.float32)
    carry_tot = jnp.zeros((1, 128), jnp.float32)
    for dev in range(16):
        if dev > 0:
            whole = in_ref[dev - 1, 130:131] == in_ref[dev - 1, 131:132]
            joins = in_ref[dev - 1, 131:132] == in_ref[dev, 130:131]
            carry = jnp.where(joins, in_ref[dev - 1, 64:128] + jnp.where(whole, carry, 0.0), 0.0)
            carry_tot = jnp.where(joins, in_ref[dev - 1, 129:130] + jnp.where(whole, carry_tot, 0.0), 0.0)
        back_ref[dev, 0:64] = carry
        back_ref[dev, 128:129] = carry_tot
    carry = jnp.zeros((64, 128), jnp.float32)
    carry_tot = jnp.zeros((1, 128), jnp.float32)
    for dev in reversed(range(16)):
        if dev < 15:
            whole = in_ref[dev + 1, 130:131] == in_ref[dev + 1, 131:132]
            joins = in_ref[dev, 131:132] == in_ref[dev + 1, 130:131]
            carry = jnp.where(joins, in_ref[dev + 1, 0:64] + jnp.where(whole, carry, 0.0), 0.0)
            carry_tot = jnp.where(joins, in_ref[dev + 1, 128:129] + jnp.where(whole, carry_tot, 0.0), 0.0)
        back_ref[dev, 64:128] = carry
        back_ref[dev, 129:130] = carry_tot
        back_ref[dev, 130:136] = jnp.zeros((6, 128), jnp.float32)
    second = []
    for step in range(1, 16):
        peer = lax.rem(seq + step, 16)
        copy = pltpu.make_async_remote_copy(
            src_ref=back_ref.at[peer], dst_ref=got_ref.at[seq],
            send_sem=sems.at[2, step - 1], recv_sem=sems.at[3, step - 1],
            device_id=(pack, peer), device_id_type=MESH)
        copy.start()
        second.append(copy)
    got_ref[seq] = back_ref[seq]
    for copy in second:
        copy.wait()


def exchange_kernel(out_ref, got_ref, in_ref, back_ref, sems):
    pack, seq = lax.axis_index("pack"), lax.axis_index("seq")
    barrier = pltpu.get_barrier_semaphore()
    for step in range(1, 16):
        pl.semaphore_signal(barrier, inc=1, device_id=(pack, lax.rem(seq + step, 16)), device_id_type=MESH)
    pl.semaphore_wait(barrier, 15)
    exchange(out_ref, in_ref, back_ref, got_ref, sems, pack, seq)


def document_ends(local_summary, local_totals, doc_rows):
    first, last = doc_rows[0], doc_rows[-1]

    def side(doc):
        return (lax.dynamic_index_in_dim(local_summary, doc, 0, False),
                lax.dynamic_index_in_dim(local_totals, doc, 0, False))

    (sum_f, tot_f), (sum_l, tot_l) = side(first), side(last)
    heads, feats, size = sum_f.shape
    ids = jnp.broadcast_to(jnp.stack([first, last]).astype(jnp.float32)[None, :, None], (heads, 2, feats))
    slab = jnp.concatenate(
        [jnp.swapaxes(sum_f, 1, 2), jnp.swapaxes(sum_l, 1, 2), tot_f[:, None], tot_l[:, None], ids,
         jnp.zeros((heads, 4, feats), jnp.float32)], axis=1)
    slab = slab.reshape(heads, SLAB, 2, 128).swapaxes(1, 2).reshape(heads * 2, SLAB, 128)
    vmem = pltpu.VMEM((16, SLAB, 128), jnp.float32)
    got = pl.pallas_call(
        exchange_kernel,
        out_shape=jax.ShapeDtypeStruct((16, SLAB, 128), jnp.float32),
        in_specs=[pl.BlockSpec(memory_space=pltpu.VMEM)],
        out_specs=pl.BlockSpec(memory_space=pltpu.VMEM),
        scratch_shapes=[vmem, vmem, pltpu.SemaphoreType.DMA((4, 15))],
        compiler_params=pltpu.CompilerParams(collective_id=0, has_side_effects=True, vmem_limit_bytes=32 * 2**20),
    )(slab)
    got = got.reshape(heads, 2, SLAB, 128).swapaxes(1, 2).reshape(heads, SLAB, 256)
    docs = jnp.arange(SEGS, dtype=jnp.int32)
    at_f = (docs == first).astype(jnp.float32)
    at_l = (docs == last).astype(jnp.float32)
    sum_a, sum_b = jnp.swapaxes(got[:, 0:64], 1, 2), jnp.swapaxes(got[:, 64:128], 1, 2)
    tot_a, tot_b = got[:, 128], got[:, 129]
    w = lambda at, v: at.reshape((SEGS,) + (1,) * v.ndim) * v[None]
    return (local_summary + w(at_f, sum_a) + w(at_l, sum_b), local_totals + w(at_f, tot_a) + w(at_l, tot_b))


def add_rows(dst, dst_row, src, src_row, count):
    step = min(64, count)

    def body(i, _):
        dst[pl.ds(pl.multiple_of(dst_row + i * step, 8), step), :] += src[pl.ds(pl.multiple_of(src_row + i * step, 8), step), :]
        return 0

    lax.fori_loop(0, count // step, body, 0)


def weights_kernel(rows, g_hbm, gain_ref, o_hbm, gain_out, g, from_core, from_chip, gain_buf, gain_mid, gain_all, turn, ssem, rsem, gsem, free, lsem):
    z, core, x, y = place()
    pack, seq = lax.axis_index("pack"), lax.axis_index("seq")
    load = pltpu.make_async_copy(g_hbm, g, lsem)
    load.start()
    barrier = pltpu.get_barrier_semaphore()
    sibling = (z * 2 + 1 - core, seq)
    for step in range(1, 16):
        pl.semaphore_signal(barrier, inc=1, device_id=(pack, lax.rem(seq + step, 16)), device_id_type=MESH)
    for step in range(1, 8):
        pl.semaphore_signal(barrier, inc=1, device_id=(lax.rem(pack + step, 8), seq), device_id_type=MESH)
    pl.semaphore_wait(barrier, 22)
    gain_copies = []
    for step in range(1, 8):
        copy = pltpu.make_async_remote_copy(
            src_ref=gain_ref, dst_ref=gain_buf.at[step - 1], send_sem=gsem.at[0, step - 1], recv_sem=gsem.at[1, step - 1],
            device_id=(lax.rem(pack + step, 8), seq), device_id_type=MESH)
        copy.start()
        gain_copies.append(copy)
    load.wait()
    n = rows // 2 // COLORS
    copies = []
    for k in range(COLORS):
        copy = pltpu.make_async_remote_copy(
            src_ref=g.at[pl.ds(pl.multiple_of(k * 2 * n + (1 - core) * n, 8), n)], dst_ref=from_core.at[k],
            send_sem=ssem.at[k, 0], recv_sem=rsem.at[k, 0], device_id=sibling, device_id_type=MESH)
        copy.start()
        copies.append(copy)
    for copy in gain_copies:
        copy.wait()
    total = gain_ref[...]
    for step in range(7):
        total = total + gain_buf[step]
    gain_mid[...] = total
    gain_copies = []
    for step in range(1, 16):
        copy = pltpu.make_async_remote_copy(
            src_ref=gain_mid, dst_ref=gain_all.at[step - 1], send_sem=gsem.at[2, step - 1], recv_sem=gsem.at[3, step - 1],
            device_id=(pack, lax.rem(seq + step, 16)), device_id_type=MESH)
        copy.start()
        gain_copies.append(copy)
    offs = []
    for k in range(COLORS):
        copies[k].wait()
        pl.semaphore_signal(free.at[k, 6], inc=1, device_id=sibling, device_id_type=MESH)
        add_rows(g, k * 2 * n + core * n, from_core.at[k], 0, n)
        offs.append(k * 2 * n + core * n)
    for s in range(6):
        h = n >> (s + 1)
        for k in range(COLORS):
            dev, side = neighbour(DIM_ORDER[(k + s) % 6], z, core, x, y)
            copies[k] = pltpu.make_async_remote_copy(
                src_ref=g.at[pl.ds(pl.multiple_of(offs[k] + (1 - side) * h, 8), h)], dst_ref=from_chip.at[k, pl.ds(n - 2 * h, h)],
                send_sem=ssem.at[k, s + 1], recv_sem=rsem.at[k, s + 1], device_id=dev, device_id_type=MESH)
            copies[k].start()
        for k in range(COLORS):
            dev, side = neighbour(DIM_ORDER[(k + s) % 6], z, core, x, y)
            offs[k] = offs[k] + side * h
            copies[k].wait()
            if s < 5:
                pl.semaphore_signal(free.at[k, s], inc=1, device_id=dev, device_id_type=MESH)
            add_rows(g, offs[k], from_chip.at[k], n - 2 * h, h)
    for s in reversed(range(6)):
        h = n >> (s + 1)
        for k in range(COLORS):
            dev, side = neighbour(DIM_ORDER[(k + s) % 6], z, core, x, y)
            part = g.at[pl.ds(pl.multiple_of(offs[k], 8), h)]
            if s < 5:
                pl.semaphore_wait(free.at[k, s], 1)
            copies[k] = pltpu.make_async_remote_copy(
                src_ref=part, dst_ref=part if s < 5 else turn.at[k], send_sem=ssem.at[k, 7 + s], recv_sem=rsem.at[k, 7 + s], device_id=dev, device_id_type=MESH)
            copies[k].start()
        for k in range(COLORS):
            dev, side = neighbour(DIM_ORDER[(k + s) % 6], z, core, x, y)
            copies[k].wait()
            if s == 5:
                g[pl.ds(pl.multiple_of(offs[k] + (1 - 2 * side) * h, 8), h)] = turn[k]
            offs[k] = offs[k] - side * h
    for k in range(COLORS):
        part = g.at[pl.ds(pl.multiple_of(offs[k], 8), n)]
        pl.semaphore_wait(free.at[k, 6], 1)
        copies[k] = pltpu.make_async_remote_copy(
            src_ref=part, dst_ref=part, send_sem=ssem.at[k, 13], recv_sem=rsem.at[k, 13], device_id=sibling, device_id_type=MESH)
        copies[k].start()
    for copy in gain_copies:
        copy.wait()
    total = gain_mid[...]
    for step in range(15):
        total = total + gain_all[step]
    gain_out[...] = total
    stores = []
    for k in range(COLORS):
        copies[k].wait()
        part = pl.ds(k * 2 * n, 2 * n)
        store = pltpu.make_async_copy(g.at[part], o_hbm.at[part], ssem.at[k, 14])
        store.start()
        stores.append(store)
    for store in stores:
        store.wait()


def sum_weights(grad_w, gains):
    wq, wk, wv, wo, up, down = grad_w
    whole = jnp.concatenate([wq, wk, wv, wo] + [up[:, i * 512:(i + 1) * 512] for i in range(4)] + [down], axis=0)
    rows = whole.shape[0]
    n = rows // 2 // COLORS
    gain = jnp.concatenate(gains).reshape(8, 128)
    whole, gain = pl.pallas_call(
        functools.partial(weights_kernel, rows),
        out_shape=(jax.ShapeDtypeStruct((rows, 512), jnp.float32), jax.ShapeDtypeStruct((8, 128), jnp.float32)),
        in_specs=[pl.BlockSpec(memory_space=pl.ANY), pl.BlockSpec(memory_space=pltpu.VMEM)],
        out_specs=(pl.BlockSpec(memory_space=pl.ANY), pl.BlockSpec(memory_space=pltpu.VMEM)),
        scratch_shapes=[
            pltpu.VMEM((rows, 512), jnp.float32),
            pltpu.VMEM((COLORS, n, 512), jnp.float32),
            pltpu.VMEM((COLORS, n, 512), jnp.float32),
            pltpu.VMEM((7, 8, 128), jnp.float32),
            pltpu.VMEM((8, 128), jnp.float32),
            pltpu.VMEM((15, 8, 128), jnp.float32),
            pltpu.VMEM((COLORS, 8, 512), jnp.float32),
            pltpu.SemaphoreType.DMA((COLORS, 15)),
            pltpu.SemaphoreType.DMA((COLORS, 15)),
            pltpu.SemaphoreType.DMA((4, 15)),
            pltpu.SemaphoreType.REGULAR((COLORS, 7)),
            pltpu.SemaphoreType.DMA,
        ],
        compiler_params=pltpu.CompilerParams(collective_id=1, has_side_effects=True, vmem_limit_bytes=60 * 2**20),
    )(whole, gain)
    block = lambda i: whole[i * 512:(i + 1) * 512]
    flat = gain.reshape(1024)
    return (block(0), block(1), block(2), block(3), jnp.concatenate([block(4 + i) for i in range(4)], axis=1),
            whole[4096:6144], flat[:512], flat[512:])


def per_device(
    inputs,
    w_query,
    w_key,
    w_value,
    w_output,
    w_up,
    w_down,
    gain_attn,
    gain_ffn,
    random_features,
    doc_ids,
    live_rows,
    cotangent,
):
    rows = inputs[0].astype(jnp.float32)
    seq_rows, model_width = rows.shape
    head_count, head_size, feat_count = random_features.shape
    doc_rows = doc_ids[0]
    onehot = (doc_rows[:, None] == jnp.arange(SEGS, dtype=jnp.int32)[None, :]).astype(jnp.bfloat16)
    onehot_float = onehot.astype(jnp.float32)
    onehot_mask = onehot[:, :, None, None]
    live_mask = live_rows[0].astype(jnp.float32)[:, None, None]
    normed_float, norm_pull_attn = jax.vjp(layer_norm, rows, gain_attn)
    normed = normed_float.astype(jnp.bfloat16)
    query_flat = jnp.dot(normed, w_query, preferred_element_type=jnp.float32).astype(jnp.bfloat16)
    key_flat = jnp.dot(normed, w_key, preferred_element_type=jnp.float32).astype(jnp.bfloat16)
    value_flat = jnp.dot(normed, w_value, preferred_element_type=jnp.float32).astype(jnp.bfloat16)
    query_heads = query_flat.reshape(seq_rows, head_count, head_size)
    key_heads = key_flat.reshape(seq_rows, head_count, head_size)
    value_head_rows = value_flat.reshape(seq_rows, head_count, head_size)

    def feature_pass(head_rows):
        project = jnp.einsum(
            "thd,hdm->thm", head_rows, random_features, preferred_element_type=jnp.float32
        )
        return jax.vjp(feature_exp, project, head_rows.astype(jnp.float32))

    phi_query_float, query_pull = feature_pass(query_heads)
    phi_key_float, key_pull = feature_pass(key_heads)
    phi_query = phi_query_float.astype(jnp.bfloat16)
    phi_key = (phi_key_float * live_mask).astype(jnp.bfloat16)
    masked_key = phi_key[:, None, :, :] * onehot_mask
    local_summary = jnp.einsum(
        "tshm,thd->shmd", masked_key, value_head_rows, preferred_element_type=jnp.float32
    )
    local_totals = jnp.einsum("ts,thm->shm", onehot, phi_key, preferred_element_type=jnp.float32)
    summary, totals = document_ends(local_summary, local_totals, doc_rows)
    summary_low = summary.astype(jnp.bfloat16)
    masked_query = phi_query[:, None, :, :] * onehot_mask
    numerator = jnp.einsum(
        "tshm,shmd->thd", masked_query, summary_low, preferred_element_type=jnp.float32
    )
    row_totals = jnp.einsum("ts,shm->thm", onehot_float, totals, precision=highest_precision_flag)
    denominator = jnp.sum(phi_query.astype(jnp.float32) * row_totals, axis=-1)
    attended = (
        (numerator / denominator[:, :, None]).reshape(seq_rows, model_width).astype(jnp.bfloat16)
    )
    middle = rows + jnp.dot(attended, w_output, preferred_element_type=jnp.float32)
    hidden_float, norm_pull_ffn = jax.vjp(layer_norm, middle, gain_ffn)
    hidden = hidden_float.astype(jnp.bfloat16)
    upward_projection = jnp.dot(hidden, w_up, preferred_element_type=jnp.float32)
    activated_float, gelu_pull = jax.vjp(jax.nn.gelu, upward_projection)
    activated = activated_float.astype(jnp.bfloat16)
    outputs = middle + jnp.dot(activated, w_down, preferred_element_type=jnp.float32)
    output_gradient_rows = cotangent[0]
    grad_activated = contract(output_gradient_rows, w_down, 1, 1).astype(jnp.bfloat16)
    grad_w_down = contract(activated, output_gradient_rows, 0, 0)
    (grad_upward_float,) = gelu_pull(grad_activated.astype(jnp.float32))
    grad_upward = grad_upward_float.astype(jnp.bfloat16)
    grad_w_up = contract(hidden, grad_upward, 0, 0)
    grad_hidden = contract(grad_upward, w_up, 1, 1).astype(jnp.bfloat16)
    grad_middle_norm, grad_gain_ffn = norm_pull_ffn(grad_hidden.astype(jnp.float32))
    grad_middle = output_gradient_rows.astype(jnp.float32) + grad_middle_norm
    grad_branch = grad_middle.astype(jnp.bfloat16)
    grad_w_output = contract(attended, grad_branch, 0, 0)
    grad_attended = contract(grad_branch, w_output, 1, 1).astype(jnp.bfloat16).astype(jnp.float32)
    grad_attended = grad_attended.reshape(seq_rows, head_count, head_size)
    grad_numerator = (grad_attended / denominator[:, :, None]).astype(jnp.bfloat16)
    grad_denominator = -jnp.sum(grad_attended * numerator, axis=-1) / (denominator * denominator)
    masked_grad = grad_numerator[:, None, :, :] * onehot_mask
    grad_phi_query = jnp.einsum(
        "tshd,shmd->thm", masked_grad, summary_low, preferred_element_type=jnp.float32
    )
    grad_phi_query = (grad_phi_query + grad_denominator[:, :, None] * row_totals).astype(
        jnp.bfloat16
    )
    local_grad_summary = jnp.einsum(
        "tshm,thd->shmd", masked_query, grad_numerator, preferred_element_type=jnp.float32
    )
    local_grad_totals = jnp.einsum(
        "ts,thm->shm",
        onehot_float,
        phi_query.astype(jnp.float32) * grad_denominator[:, :, None],
        precision=highest_precision_flag,
    )
    grad_summary, grad_totals = document_ends(local_grad_summary, local_grad_totals, doc_rows)
    grad_summary_low = grad_summary.astype(jnp.bfloat16)
    masked_value = value_head_rows[:, None, :, :] * onehot_mask
    grad_phi_key = jnp.einsum(
        "tshd,shmd->thm", masked_value, grad_summary_low, preferred_element_type=jnp.float32
    )
    grad_phi_key = grad_phi_key + jnp.einsum(
        "ts,shm->thm", onehot_float, grad_totals, precision=highest_precision_flag
    )
    grad_phi_key = grad_phi_key.astype(jnp.bfloat16).astype(jnp.float32) * live_mask
    grad_value = jnp.einsum(
        "tshm,shmd->thd", masked_key, grad_summary_low, preferred_element_type=jnp.float32
    ).astype(jnp.bfloat16)

    def heads_back(pull, grad_phi):
        grad_project, grad_square = pull(grad_phi)
        through = jnp.einsum(
            "thm,hdm->thd",
            grad_project.astype(jnp.bfloat16),
            random_features,
            preferred_element_type=jnp.float32,
        )
        return (through + grad_square).astype(jnp.bfloat16)

    grad_query = heads_back(query_pull, grad_phi_query.astype(jnp.float32)).reshape(
        seq_rows, model_width
    )
    grad_key = heads_back(key_pull, grad_phi_key).reshape(seq_rows, model_width)
    grad_value = grad_value.reshape(seq_rows, model_width)
    grad_normed = (
        contract(grad_query, w_query, 1, 1)
        + contract(grad_key, w_key, 1, 1)
        + contract(grad_value, w_value, 1, 1)
    )
    grad_normed = grad_normed.astype(jnp.bfloat16)
    grad_w_query = contract(normed, grad_query, 0, 0)
    grad_w_key = contract(normed, grad_key, 0, 0)
    grad_w_value = contract(normed, grad_value, 0, 0)
    grad_rows_norm, grad_gain_attn = norm_pull_attn(grad_normed.astype(jnp.float32))
    grad_inputs = grad_middle + grad_rows_norm
    summed = sum_weights(
        (grad_w_query, grad_w_key, grad_w_value, grad_w_output, grad_w_up, grad_w_down), (grad_gain_attn, grad_gain_ffn)
    )
    return (
        outputs[None].astype(jnp.bfloat16),
        grad_inputs[None].astype(jnp.bfloat16),
        summed[0],
        summed[1],
        summed[2],
        summed[3],
        summed[4],
        summed[5],
        summed[6],
        summed[7],
    )


def solution(mesh):
    return jax.shard_map(
        per_device,
        mesh=mesh,
        in_specs=(
            P("pack", "seq", None),
            P(),
            P(),
            P(),
            P(),
            P(),
            P(),
            P(),
            P(),
            P(),
            P("pack", "seq"),
            P("pack", "seq"),
            P("pack", "seq", None),
        ),
        out_specs=(
            P("pack", "seq", None),
            P("pack", "seq", None),
            P(),
            P(),
            P(),
            P(),
            P(),
            P(),
            P(),
            P(),
        ),
        check_vma=False,
    )
```

```python
import functools
import math

import jax
import jax.numpy as jnp
from jax import lax
from jax.experimental import pallas as pl
from jax.experimental.pallas import tpu as pltpu
from jax.sharding import PartitionSpec as P

MESH = pl.DeviceIdType.MESH
F32, BF16 = jnp.float32, jnp.bfloat16
T, D, H, DH, M, FF = 512, 512, 8, 64, 256, 2048
SLAB = 136
DIM_ORDER = (0, 2, 4, 1, 3, 5)
EPS = 1e-05
C = DH ** -0.25
ALPHA = C * math.log2(math.e)
GELU_A, GELU_B = math.sqrt(2.0 / math.pi), 0.044715


def dot(a, b):
    return lax.dot_general(a, b, (((1,), (0,)), ((), ())), preferred_element_type=F32)


def dot_nt(a, b):
    return lax.dot_general(a, b, (((1,), (1,)), ((), ())), preferred_element_type=F32)


def dot_tn(a, b):
    return lax.dot_general(a, b, (((0,), (0,)), ((), ())), preferred_element_type=F32)


def iota(shape, dim):
    return lax.broadcasted_iota(jnp.int32, shape, dim)


def place():
    pack, seq = lax.axis_index("pack"), lax.axis_index("seq")
    return pack // 2, pack % 2, seq // 4, seq % 4


def neighbour(dim, z, core, x, y):
    axis = dim // 2
    here = (x, y, z)[axis]
    if dim % 2 == 0:
        there, side = here + 1 - 2 * (here % 2), ((here + 1) // 2) % 2
    else:
        there, side = 3 - here, here // 2
    x = there if axis == 0 else x
    y = there if axis == 1 else y
    z = there if axis == 2 else z
    return (z * 2 + core, x * 4 + y), side


def layer_norm(v):
    centred = v - jnp.mean(v, axis=-1, keepdims=True)
    scale = lax.rsqrt(jnp.mean(centred * centred, axis=-1, keepdims=True) + EPS)
    return centred * scale, scale


def norm_back(n, scale, e):
    return scale * (e - jnp.mean(e, axis=-1, keepdims=True) - n * jnp.mean(e * n, axis=-1, keepdims=True))


def row_loop(step, body, carry=0):
    def run(i, c):
        return body(pl.ds(pl.multiple_of(i * step, step), step), c)

    return lax.fori_loop(0, T // step, run, carry)


def head_loop(body):
    def run(h, c):
        body(h)
        return c

    lax.fori_loop(0, H, run, 0)


class Job:
    def __init__(self, r, where, color, sem, row, lane, width, rows=1024):
        self.r, self.where, self.color, self.sem = r, where, color, sem
        self.row, self.lane, self.width = row, lane, width
        self.n = rows // 2
        self.off = row + where[1] * self.n
        self.step = -1

    def part(self, row, count):
        return self.r.g.at[pl.ds(pl.multiple_of(row, 8), count), pl.ds(self.lane, self.width)]

    def copy(self, src, dst, dev):
        self.now = pltpu.make_async_remote_copy(
            src_ref=src, dst_ref=dst, send_sem=self.r.ssem.at[self.sem, self.step], recv_sem=self.r.rsem.at[self.sem, self.step],
            device_id=dev, device_id_type=MESH)
        self.now.start()

    def add(self, buf, buf_row, count):
        r, lanes, step = self.r, pl.ds(self.lane, self.width), min(64, count)

        def body(i, c):
            at = pl.ds(pl.multiple_of(self.off + i * step, 8), step)
            r.g[at, lanes] += buf[pl.ds(pl.multiple_of(buf_row + i * step, 8), step), lanes]
            return c

        lax.fori_loop(0, count // step, body, 0)

    def tick(self):
        z, core, x, y = self.where
        r, n, lanes = self.r, self.n, pl.ds(self.lane, self.width)
        base = self.row // 2
        sibling = (z * 2 + 1 - core, x * 4 + y)
        s = self.step
        link = lambda k: neighbour(DIM_ORDER[(k + self.color) % 6], z, core, x, y)
        if s >= 0:
            self.now.wait()
        if s == 0:
            pl.semaphore_signal(r.free.at[self.sem, 6], inc=1, device_id=sibling, device_id_type=MESH)
            self.add(r.from_core, base, n)
        elif 1 <= s <= 6:
            dev, side = link(s - 1)
            h = n >> s
            if s < 6:
                pl.semaphore_signal(r.free.at[self.sem, s - 1], inc=1, device_id=dev, device_id_type=MESH)
            self.off = self.off + side * h
            self.add(r.from_chip, base + n - 2 * h, h)
        elif 7 <= s <= 12:
            k = 12 - s
            dev, side = link(k)
            h = n >> (k + 1)
            if k == 5:
                r.g[pl.ds(pl.multiple_of(self.off + (1 - 2 * side) * h, 8), h), lanes] = r.turn[self.sem // 4, :, pl.ds(self.lane if self.width < 512 else 0, self.width)]
            self.off = self.off - side * h
        self.step = s = s + 1
        if s == 0:
            self.copy(self.part(self.row + (1 - core) * n, n), r.from_core.at[pl.ds(base, n), lanes], sibling)
        elif s <= 6:
            dev, side = link(s - 1)
            h = n >> s
            self.copy(self.part(self.off + (1 - side) * h, h), r.from_chip.at[pl.ds(base + n - 2 * h, h), lanes], dev)
        elif s <= 12:
            k = 12 - s
            dev, side = link(k)
            h = n >> (k + 1)
            part = self.part(self.off, h)
            if k == 5:
                self.copy(part, r.turn.at[self.sem // 4, :, pl.ds(self.lane if self.width < 512 else 0, self.width)], dev)
            else:
                pl.semaphore_wait(r.free.at[self.sem, k], 1)
                self.copy(part, part, dev)
        elif s == 13:
            pl.semaphore_wait(r.free.at[self.sem, 6], 1)
            part = self.part(self.off, n)
            self.copy(part, part, sibling)


class Exchange:
    def __init__(self, r, which, pack, seq):
        self.r, self.sems, self.pack, self.seq = r, r.esem.at[which], pack, seq

    def send(self, src, dst, way):
        copies = []
        for step in range(1, 16):
            peer = lax.rem(self.seq + step, 16)
            copy = pltpu.make_async_remote_copy(
                src_ref=src.at[peer], dst_ref=dst.at[self.seq],
                send_sem=self.sems.at[2 * way, step - 1], recv_sem=self.sems.at[2 * way + 1, step - 1],
                device_id=(self.pack, peer), device_id_type=MESH)
            copy.start()
            copies.append(copy)
        dst[self.seq] = src[self.seq]
        self.copies = copies

    def wait(self):
        for copy in self.copies:
            copy.wait()

    def begin(self):
        self.send(self.r.out, self.r.arrived, 0)

    def turn(self):
        self.wait()
        arrived, back = self.r.arrived, self.r.back

        def left(dev, carry):
            total, small = carry
            tail, mine = arrived[dev - 1, 128:136], arrived[dev, 128:136]
            whole = tail[2:3] == tail[3:4]
            joins = tail[3:4] == mine[2:3]
            total = jnp.where(joins, arrived[dev - 1, 64:128] + jnp.where(whole, total, 0.0), 0.0)
            small = jnp.where(joins, tail[1:2] + jnp.where(whole, small, 0.0), 0.0)
            back[dev, 0:64] = total
            back[dev, 128:129] = small
            return total, small

        def right(i, carry):
            dev = 14 - i
            total, small = carry
            tail, mine = arrived[dev + 1, 128:136], arrived[dev, 128:136]
            whole = tail[2:3] == tail[3:4]
            joins = mine[3:4] == tail[2:3]
            total = jnp.where(joins, arrived[dev + 1, 0:64] + jnp.where(whole, total, 0.0), 0.0)
            small = jnp.where(joins, tail[0:1] + jnp.where(whole, small, 0.0), 0.0)
            back[dev, 64:128] = total
            back[dev, 129:130] = small
            return total, small

        none = (jnp.zeros((64, 128), F32), jnp.zeros((1, 128), F32))
        for dev in range(16):
            back[dev, 128:136] = jnp.zeros((8, 128), F32)
        back[0, 0:64] = none[0]
        back[15, 64:128] = none[0]
        lax.fori_loop(1, 16, left, none)
        lax.fori_loop(0, 15, right, none)
        self.send(back, self.r.got, 1)


class Gains:
    def __init__(self, r, pack, seq):
        self.r, self.pack, self.seq = r, pack, seq

    def send(self, src, dst, way, size):
        self.copies = []
        for step in range(1, size):
            dev = (lax.rem(self.pack + step, 8), self.seq) if way == 0 else (self.pack, lax.rem(self.seq + step, 16))
            copy = pltpu.make_async_remote_copy(
                src_ref=src, dst_ref=dst.at[step - 1], send_sem=self.r.gsem.at[2 * way, step - 1],
                recv_sem=self.r.gsem.at[2 * way + 1, step - 1], device_id=dev, device_id_type=MESH)
            copy.start()
            self.copies.append(copy)

    def begin(self):
        self.send(self.r.gain_here, self.r.gain_pack, 0, 8)

    def turn(self):
        for copy in self.copies:
            copy.wait()
        total = self.r.gain_here[...]
        for i in range(7):
            total = total + self.r.gain_pack[i]
        self.r.gain_mid[...] = total
        self.send(self.r.gain_mid, self.r.gain_seq, 1, 16)

    def end(self):
        for copy in self.copies:
            copy.wait()
        total = self.r.gain_mid[...]
        for i in range(15):
            total = total + self.r.gain_seq[i]
        return total


class Refs:
    pass


SCRATCH = [
    ("x", (T, D), BF16), ("cot", (T, D), BF16),
    ("wqkv", (3, D, D), BF16), ("wo", (D, D), BF16),
    ("wup", (4, D, 512), BF16), ("wdown", (4, 512, D), BF16), ("rf", (H, DH, M), BF16),
    ("rx", (4, 256, 512), BF16), ("r80", (H, 80, M), BF16),
    ("nb", (T, D), BF16), ("nT", (D, T), BF16), ("qT", (D, T), BF16), ("kT", (D, T), BF16),
    ("xb", (4, T, 512), BF16),
    ("gup", (4, T, 512), BF16),
    ("vext", (H, 80, T), BF16), ("gext", (H, 80, T), BF16),
    ("phik", (H, T, M), BF16), ("phiq", (H, T, M), BF16),
    ("dcol", (T, T), F32),
    ("num", (H, DH, T), F32), ("den", (H, 8, T), F32),
    ("attT", (D, T), BF16), ("att", (T, D), BF16), ("mid", (T, D), F32), ("hid", (T, D), BF16), ("hidT", (D, T), BF16),
    ("acc", (T, D), F32), ("acc2", (T, D), F32), ("gmid", (T, D), F32), ("gb", (T, D), BF16),
    ("sb1", (H, 144, M), BF16), ("sb2", (H, 144, M), BF16),
    ("gvT", (H, DH, T), F32), ("gT", (3, D, T), BF16),
    ("obf", (T, D), BF16), ("gibf", (T, D), BF16),
    ("out", (16, SLAB, 128), F32), ("arrived", (16, SLAB, 128), F32), ("back", (16, SLAB, 128), F32), ("got", (16, SLAB, 128), F32),
    ("g", (6144, 512), F32), ("from_core", (3072, 512), F32), ("from_chip", (3072, 512), F32), ("turn", (6, 8, 512), F32),
    ("gain_sum", (2, 8, D), F32), ("gain_here", (8, 128), F32), ("gain_pack", (7, 8, 128), F32), ("gain_mid", (8, 128), F32), ("gain_seq", (15, 8, 128), F32),
]
SEMS = [
    ("load", pltpu.SemaphoreType.DMA((20,))), ("store", pltpu.SemaphoreType.DMA((16,))),
    ("esem", pltpu.SemaphoreType.DMA((2, 4, 15))), ("gsem", pltpu.SemaphoreType.DMA((4, 15))),
    ("ssem", pltpu.SemaphoreType.DMA((24, 14))), ("rsem", pltpu.SemaphoreType.DMA((24, 14))),
    ("free", pltpu.SemaphoreType.REGULAR((24, 7))),
]
ROW_DOWN, ROW_UP, ROW_O, ROW_Q, ROW_K, ROW_V = 0, 2048, 4096, 4608, 5120, 5632


def kernel(
    x_h, wq_h, wk_h, wv_h, wo_h, wup_h, wdown_h, rf_h, cot_h, ga_ref, gf_ref, doc_ref, live_ref,
    out_h, gin_h, gwq_h, gwk_h, gwv_h, gwo_h, gwup_h, gwdown_h, gain_ref, *scratch):
    r = Refs()
    for (name, *_), ref in zip(SCRATCH + SEMS, scratch):
        setattr(r, name, ref)
    where = place()
    z, core, px, py = where
    pack, seq = lax.axis_index("pack"), lax.axis_index("seq")

    loads = {}

    def load(name, src, dst):
        copy = pltpu.make_async_copy(src, dst, r.load.at[len(loads)])
        copy.start()
        loads[name] = copy

    load("x", x_h, r.x)
    load("wk", wk_h, r.wqkv.at[1])
    load("wv", wv_h, r.wqkv.at[2])
    load("rf", rf_h, r.rf)
    load("wq", wq_h, r.wqkv.at[0])
    load("wo", wo_h, r.wo)
    for j in range(4):
        load("wup%d" % j, wup_h.at[:, pl.ds(j * 512, 512)], r.wup.at[j])
    load("cot", cot_h, r.cot)
    for j in range(4):
        load("wdown%d" % j, wdown_h.at[pl.ds(j * 512, 512)], r.wdown.at[j])
    barrier = pltpu.get_barrier_semaphore()
    for step in range(1, 16):
        pl.semaphore_signal(barrier, inc=1, device_id=(pack, lax.rem(seq + step, 16)), device_id_type=MESH)
    for step in range(1, 8):
        pl.semaphore_signal(barrier, inc=1, device_id=(lax.rem(pack + step, 8), seq), device_id_type=MESH)

    doc = doc_ref[...].astype(F32)
    doc_f, doc_l = doc[:, 0:1], doc[:, T - 1:T]
    in_f, in_l = doc == doc_f, doc == doc_l
    one_f, one_l = in_f.astype(F32), in_l.astype(F32)
    row16 = iota((16, T), 0)

    def ends(block, tail_f, tail_l):
        zero = jnp.zeros_like(block)
        tail = jnp.where(row16 == 0, tail_f, jnp.where(row16 == 1, tail_l, 0.0))
        return jnp.concatenate(
            [jnp.where(in_f, block, zero).astype(BF16), jnp.where(in_l, block, zero).astype(BF16), tail.astype(BF16)], axis=0)

    dcol = jnp.broadcast_to(doc, (128, T)).T
    for j in range(4):
        r.dcol[:, j * 128:(j + 1) * 128] = dcol
    live = jnp.broadcast_to(live_ref[...].astype(F32), (128, T)).T

    loads["x"].wait()

    def first_norm(rows, c):
        n, _ = layer_norm(r.x[rows, :].astype(F32))
        r.nb[rows, :] = (n * ga_ref[...]).astype(BF16)
        return c

    row_loop(64, first_norm)
    loads["rf"].wait()
    for p in range(4):
        lane, row = iota((256, 512), 1) // 256, iota((256, 512), 0)
        pick = (row >= 128) & (row < 152) & (row % 8 == 2 * p + lane)
        r.rx[p] = jnp.where(pick, 1.0, 0.0).astype(BF16)
        r.rx[p, 0:64, 0:256] = r.rf[2 * p]
        r.rx[p, 64:128, 256:512] = r.rf[2 * p + 1]
    for h in range(H):
        r.r80[h, 0:64] = r.rf[h]
        r.r80[h, 64:80] = jnp.where(iota((16, M), 0) == 0, 1.0, 0.0).astype(BF16)
    pick_heads = ((iota((D, 128), 1) % 8 == iota((D, 128), 0) // DH) & (iota((D, 128), 1) < 24)).astype(BF16)

    def features(w, low, transposed, phi, off, alive):
        flat = dot(r.nb[...], r.wqkv[w]).astype(BF16)
        transposed[...] = flat.T
        square = flat.astype(F32)
        square = square * square
        high = square.astype(BF16)
        rest = (square - high.astype(F32)).astype(BF16)
        size = dot(high, pick_heads) + dot(rest, pick_heads)
        shift = size * (-0.5 * C) - 4.0 / ALPHA
        if alive is not None:
            shift = shift + (alive - 1.0) * 1e30
        first = shift.astype(BF16).astype(F32)
        second = (shift - first).astype(BF16).astype(F32)
        third = shift - first - second
        at = iota((T, 128), 1)
        shift = jnp.where(at < 8, first, jnp.where(at < 16, second, jnp.where(at < 24, third, 0.0))).astype(BF16)
        for p in range(4):
            low[p, :, off:off + 128] = flat[:, p * 128:(p + 1) * 128]
            low[p, :, off + 128:off + 256] = shift

        def one_pair(p, c):
            y = dot(low[p, :, off:off + 256], r.rx[p])
            y = jnp.exp2(y * ALPHA).astype(BF16)
            phi[2 * p] = y[:, 0:256]
            phi[2 * p + 1] = y[:, 256:512]
            return c

        lax.fori_loop(0, 4, one_pair, 0)

    loads["wk"].wait()
    features(1, r.xb, r.kT, r.phik, 0, live)
    loads["wv"].wait()
    vT = dot(r.nb[...], r.wqkv[2]).astype(BF16).T
    for h in range(H):
        r.vext[h, 0:64] = vT[h * 64:(h + 1) * 64]
        r.vext[h, 64:80] = jnp.where(row16 == 0, 1.0, 0.0).astype(BF16)

    def put_slab(h, lhs, phi):
        s = dot(lhs, phi)
        row = iota((8, M), 0)
        tail = jnp.where(row == 2, doc_f, jnp.where(row == 3, doc_l, s[128:136]))
        for half in range(2):
            r.out[2 * h + half, 0:128] = s[0:128, half * 128:(half + 1) * 128]
            r.out[2 * h + half, 128:136] = tail[:, half * 128:(half + 1) * 128]

    def take_slab(h, sb):
        for half in range(2):
            lanes = pl.ds(half * 128, 128)
            sb[h, 0:128, lanes] = r.got[2 * h + half, 0:128].astype(BF16)
            sb[h, 128:144, lanes] = jnp.concatenate(
                [r.got[2 * h + half, 128:136], jnp.zeros((8, 128), F32)], axis=0).astype(BF16)

    def value_ends(h):
        return ends(r.vext[h, 0:64].astype(F32), one_f, one_l)

    head_loop(lambda h: put_slab(h, value_ends(h), r.phik[h]))
    pl.semaphore_wait(barrier, 22)
    exchange = Exchange(r, 0, pack, seq)
    exchange.begin()

    r.nT[...] = r.nb[...].T
    loads["wq"].wait()
    features(0, r.xb, r.qT, r.phiq, 256, None)
    exchange.turn()

    def same(block):
        return jnp.where(r.dcol[...] == doc, block, 0.0).astype(BF16)

    def attend(h):
        local = dot_nt(r.vext[h], same(dot_nt(r.phiq[h], r.phik[h])))
        r.num[h] = local[0:64]
        r.den[h] = local[64:72]

    head_loop(attend)
    exchange.wait()

    def join(h):
        take_slab(h, r.sb1)
        far = dot_nt(r.sb1[h], r.phiq[h])
        num = r.num[h] + jnp.where(in_f, far[0:64], 0.0) + jnp.where(in_l, far[64:128], 0.0)
        den = r.den[h, 0:1] + jnp.where(in_f, far[128:129], 0.0) + jnp.where(in_l, far[129:130], 0.0)
        inv = 1.0 / den
        att = num * inv
        r.num[h] = att
        r.den[h, 0:1] = inv
        r.attT[pl.ds(pl.multiple_of(h * 64, 64), 64)] = att.astype(BF16)

    head_loop(join)
    r.att[...] = r.attT[...].T
    loads["wo"].wait()
    r.mid[...] = dot(r.att[...], r.wo[...])

    def second_norm(rows, c):
        mid = r.x[rows, :].astype(F32) + r.mid[rows, :]
        r.mid[rows, :] = mid
        n, _ = layer_norm(mid)
        r.hid[rows, :] = (n * gf_ref[...]).astype(BF16)
        return c

    row_loop(64, second_norm)

    loads["cot"].wait()
    for j in range(4):
        loads["wup%d" % j].wait()
        loads["wdown%d" % j].wait()

    def feed(j, c):
        r.acc[...] = dot(r.hid[...], r.wup[j])
        r.acc2[...] = dot_nt(r.cot[...], r.wdown[j])

        def gelu(rows, c):
            u = r.acc[rows, :]
            ga = r.acc2[rows, :].astype(BF16).astype(F32)
            sq = u * u
            t = jnp.tanh(u * (GELU_A + GELU_A * GELU_B * sq))
            half = 0.5 * (1.0 + t)
            slope = half + 0.5 * u * (1.0 - t * t) * (GELU_A + 3.0 * GELU_A * GELU_B * sq)
            r.xb[j, rows, :] = (u * half).astype(BF16)
            r.gup[j, rows, :] = (ga * slope).astype(BF16)
            return c

        row_loop(16, gelu)
        back = dot_nt(r.gup[j], r.wup[j])

        @pl.when(j == 0)
        def _():
            r.gmid[...] = back

        @pl.when(j > 0)
        def _():
            r.gmid[...] += back

        return c

    lax.fori_loop(0, 4, feed, 0)

    def add_gain(which, p):
        total = r.gain_sum[which]
        for i in range(8):
            total = total + p[i * 8:(i + 1) * 8]
        r.gain_sum[which] = total

    r.gain_sum[...] = jnp.zeros((2, 8, D), F32)

    def second_back(rows, c):
        gh = r.gmid[rows, :].astype(BF16).astype(F32)
        n, scale = layer_norm(r.mid[rows, :])
        gm = r.cot[rows, :].astype(F32) + norm_back(n, scale, gh * gf_ref[...])
        r.gmid[rows, :] = gm
        r.gb[rows, :] = gm.astype(BF16)
        add_gain(1, gh * n)
        return c

    row_loop(64, second_back)
    r.acc[...] = dot_nt(r.wo[...], r.gb[...])

    def gates(h):
        ga = r.acc[pl.ds(pl.multiple_of(h * 64, 64), 64)].astype(BF16).astype(F32)
        inv = r.den[h, 0:1]
        gn = (ga * inv).astype(BF16)
        gd = -jnp.sum(ga * r.num[h], axis=0, keepdims=True) * inv
        r.gext[h, 0:64] = gn
        r.gext[h, 64:80] = jnp.where(row16 == 0, gd, 0.0).astype(BF16)
        put_slab(h, grad_ends(h), r.phiq[h])

    def grad_ends(h):
        gd = r.gext[h, 64:80].astype(F32)[0:1]
        return ends(r.gext[h, 0:64].astype(F32), one_f * gd, one_l * gd)

    head_loop(gates)
    exchange = Exchange(r, 1, pack, seq)
    exchange.begin()

    jobs = [Job(r, where, k, 4 * k, k * 1024, 0, 512) for k in range(5)]

    def block(row, value):
        r.g[row:row + 512, :] = value

    for k in range(2):
        for j in range(2 * k, 2 * k + 2):
            block(ROW_DOWN + j * 512, dot_tn(r.xb[j], r.cot[...]))
        jobs[k].tick()
    r.hidT[...] = r.hid[...].T
    for k in range(2):
        for j in range(2 * k, 2 * k + 2):
            block(ROW_UP + j * 512, dot(r.hidT[...], r.gup[j]))
        jobs[2 + k].tick()
    for job in jobs[0:2]:
        job.tick()
    block(ROW_O, dot(r.attT[...], r.gb[...]))
    for job in jobs[2:4]:
        job.tick()
    exchange.turn()

    def map_back(h, gphi, phi, flat, which):
        p = (gphi.astype(BF16).astype(F32) * phi.astype(F32)).astype(BF16)
        through = dot_nt(r.r80[h], p)
        rows = pl.ds(pl.multiple_of(h * 64, 64), 64)
        r.gT[which, rows] = (C * through[0:64] - (C * C) * through[64:65] * flat[rows].astype(F32)).astype(BF16)

    def query_back(h):
        gphi = dot(same(dot_tn(r.gext[h], r.vext[h])), r.phik[h]) + dot_tn(grad_ends(h), r.sb1[h])
        map_back(h, gphi, r.phiq[h], r.qT, 0)
        r.gvT[h] = dot(r.gext[h, 0:64], same(dot_nt(r.phiq[h], r.phik[h])))

    head_loop(query_back)
    block(ROW_Q, dot_nt(r.nT[...], r.gT[0]))
    jobs[4].tick()
    for job in jobs[0:4]:
        job.tick()
    stores = []

    def store(src, dst):
        copy = pltpu.make_async_copy(src, dst, r.store.at[len(stores)])
        copy.start()
        stores.append(copy)

    r.acc[...] = dot(r.xb[0], r.wdown[0])
    for j in range(1, 4):
        r.acc[...] += dot(r.xb[j], r.wdown[j])

    def put_out(rows, c):
        r.obf[rows, :] = (r.mid[rows, :] + r.acc[rows, :]).astype(BF16)
        return c

    row_loop(64, put_out)
    store(r.obf, out_h)
    for job in jobs:
        job.tick()
    exchange.wait()

    def key_back(h):
        take_slab(h, r.sb2)
        gphi = dot(same(dot_tn(r.vext[h], r.gext[h])), r.phiq[h]) + dot_tn(value_ends(h), r.sb2[h])
        map_back(h, gphi, r.phik[h], r.kT, 1)
        far = dot_nt(r.sb2[h, 0:128], r.phik[h])
        rows = pl.ds(pl.multiple_of(h * 64, 64), 64)
        r.gT[2, rows] = (r.gvT[h] + jnp.where(in_f, far[0:64], 0.0) + jnp.where(in_l, far[64:128], 0.0)).astype(BF16)

    head_loop(key_back)
    block(ROW_K, dot_nt(r.nT[...], r.gT[1]))
    block(ROW_V, dot_nt(r.nT[...], r.gT[2]))
    last = [Job(r, where, k + 1, 20 + k, 5120, k * 128, 128) for k in range(4)]
    for job in last + jobs:
        job.tick()
    r.acc2[...] = dot(r.wqkv[0], r.gT[0])

    def normed_back(i, c):
        r.acc2[...] += dot(r.wqkv[i], r.gT[i])
        return c

    lax.fori_loop(1, 3, normed_back, 0)
    r.acc[...] = r.acc2[...].T
    for job in last + jobs:
        job.tick()

    def first_back(rows, c):
        gn = r.acc[rows, :].astype(BF16).astype(F32)
        n, scale = layer_norm(r.x[rows, :].astype(F32))
        r.gibf[rows, :] = (r.gmid[rows, :] + norm_back(n, scale, gn * ga_ref[...])).astype(BF16)
        add_gain(0, gn * n)
        return c

    row_loop(64, first_back)
    store(r.gibf, gin_h)
    for which in range(2):
        total = r.gain_sum[which, 0:1]
        for i in range(1, 8):
            total = total + r.gain_sum[which, i:i + 1]
        for j in range(4):
            r.gain_here[4 * which + j:4 * which + j + 1] = total[:, j * 128:(j + 1) * 128]
    gains = Gains(r, pack, seq)
    gains.begin()
    for job in last + jobs:
        job.tick()
    gains.turn()
    while last[0].step < 13 or jobs[4].step < 13:
        for job in last + jobs:
            if job.step < 13:
                job.tick()
    gain_ref[...] = gains.end()
    for job in jobs + last:
        job.now.wait()
    for j in range(4):
        store(r.g.at[pl.ds(ROW_DOWN + j * 512, 512)], gwdown_h.at[pl.ds(j * 512, 512)])
        store(r.g.at[pl.ds(ROW_UP + j * 512, 512)], gwup_h.at[:, pl.ds(j * 512, 512)])
    for row, dst in ((ROW_O, gwo_h), (ROW_Q, gwq_h), (ROW_K, gwk_h), (ROW_V, gwv_h)):
        store(r.g.at[pl.ds(row, 512)], dst)
    for copy in stores:
        copy.wait()


def per_device(
    inputs, w_query, w_key, w_value, w_output, w_up, w_down, gain_attn, gain_ffn, random_features, doc_ids, live_rows, cotangent):
    any_space = pl.BlockSpec(memory_space=pl.ANY)
    vmem = pl.BlockSpec(memory_space=pltpu.VMEM)
    f32 = lambda *shape: jax.ShapeDtypeStruct(shape, F32)
    low = jax.ShapeDtypeStruct((T, D), BF16)
    outs = pl.pallas_call(
        kernel,
        out_shape=(low, low, f32(D, D), f32(D, D), f32(D, D), f32(D, D), f32(D, FF), f32(FF, D), f32(8, 128)),
        in_specs=[any_space] * 9 + [vmem] * 4,
        out_specs=(any_space,) * 8 + (vmem,),
        scratch_shapes=[pltpu.VMEM(shape, dtype) for _, shape, dtype in SCRATCH] + [sem for _, sem in SEMS],
        compiler_params=pltpu.CompilerParams(collective_id=0, has_side_effects=True, vmem_limit_bytes=63 * 2**20),
    )(
        inputs[0], w_query, w_key, w_value, w_output, w_up, w_down, random_features, cotangent[0],
        gain_attn[None], gain_ffn[None], doc_ids, live_rows)
    gain = outs[8].reshape(2 * D)
    return (outs[0][None], outs[1][None]) + tuple(outs[2:8]) + (gain[:D], gain[D:])


def solution(mesh):
    rows = P("pack", "seq", None)
    return jax.shard_map(
        per_device,
        mesh=mesh,
        in_specs=(rows,) + (P(),) * 9 + (P("pack", "seq"), P("pack", "seq"), rows),
        out_specs=(rows, rows) + (P(),) * 8,
        check_vma=False,
    )
```

```python
import functools
import math

import jax
import jax.numpy as jnp
from jax import lax
from jax.experimental import pallas as pl
from jax.experimental.pallas import tpu as pltpu
from jax.sharding import PartitionSpec as P

MESH = pl.DeviceIdType.MESH
F32, BF16 = jnp.float32, jnp.bfloat16
T, D, H, DH, M, FF = 512, 512, 8, 64, 256, 2048
SLAB = 136
EPS = 1e-05
VMEM_LIMIT = 46 * 2**20
C = DH ** -0.25
ALPHA = C * math.log2(math.e)
GELU_A, GELU_B = math.sqrt(2.0 / math.pi), 0.044715


def dot(a, b):
    return lax.dot_general(a, b, (((1,), (0,)), ((), ())), preferred_element_type=F32)


def dot_nt(a, b):
    return lax.dot_general(a, b, (((1,), (1,)), ((), ())), preferred_element_type=F32)


def dot_tn(a, b):
    return lax.dot_general(a, b, (((0,), (0,)), ((), ())), preferred_element_type=F32)


def iota(shape, dim):
    return lax.broadcasted_iota(jnp.int32, shape, dim)


def place():
    pack, seq = lax.axis_index("pack"), lax.axis_index("seq")
    return pack // 2, pack % 2, seq // 4, seq % 4


def layer_norm(v):
    centred = v - jnp.mean(v, axis=-1, keepdims=True)
    scale = lax.rsqrt(jnp.mean(centred * centred, axis=-1, keepdims=True) + EPS)
    return centred * scale, scale


def norm_back(n, scale, e):
    return scale * (e - jnp.mean(e, axis=-1, keepdims=True) - n * jnp.mean(e * n, axis=-1, keepdims=True))


def row_loop(step, body, carry=0):
    def run(i, c):
        return body(pl.ds(pl.multiple_of(i * step, step), step), c)

    return lax.fori_loop(0, T // step, run, carry)


def head_loop(body, start=0, stop=H):
    def run(h, c):
        body(h)
        return c

    lax.fori_loop(start, stop, run, 0)


class Wave:
    def __init__(self, r, where, row, parts, first):
        self.parts = []
        for k, rows in enumerate(parts):
            self.parts.append(Part(r, where, row, rows // 2, k, first + k))
            row += rows
        self.done = False

    def tick(self):
        if self.done:
            return
        for part in self.parts:
            part.finish()
            part.start()
        self.done = self.parts[0].step == 8


class Part:
    def __init__(self, r, where, row, n, color, sem):
        self.r, self.where, self.row, self.n, self.sem = r, where, row, n, sem
        self.axes = [(color + i) % 3 for i in range(3)]
        self.at = row + where[1] * n
        self.buf = row // 2
        self.step = -1
        self.copies = []

    def peers(self, stage):
        z, core, x, y = self.where
        axis = self.axes[stage]
        mine = (x, y, z)[axis]
        devs = []
        for d in range(1, 4):
            there = (mine + d) % 4
            x2, y2, z2 = (there if axis == 0 else x), (there if axis == 1 else y), (there if axis == 2 else z)
            devs.append((there, (z2 * 2 + core, x2 * 4 + y2)))
        return mine, devs

    def sibling(self):
        z, core, x, y = self.where
        return (z * 2 + 1 - core, x * 4 + y)

    def rows(self, at, count):
        return pl.ds(pl.multiple_of(at, 8), count)

    def lanes(self, quarter):
        return pl.ds(pl.multiple_of(quarter * 128, 128), 128)

    def send(self, src, dst, dev, d):
        copy = pltpu.make_async_remote_copy(
            src_ref=src, dst_ref=dst, send_sem=self.r.ssem.at[self.sem, self.step, d], recv_sem=self.r.rsem.at[self.sem, self.step, d],
            device_id=dev, device_id_type=MESH)
        copy.start()
        self.copies.append(copy)

    def free(self, stage):
        for _, dev in self.peers(stage)[1]:
            pl.semaphore_signal(self.r.free.at[self.sem, stage], inc=1, device_id=dev, device_id_type=MESH)

    def add(self, count, buf, slots):
        r, step = self.r, min(32, count)

        def body(i, c):
            at = self.rows(self.at + i * step, step)
            total = r.g[at, :]
            for slot in slots:
                total = total + buf[self.rows(slot + i * step, step), :]
            r.g[at, :] = total
            return c

        lax.fori_loop(0, count // step, body, 0)

    def finish(self):
        r, n, s = self.r, self.n, self.step
        for copy in self.copies:
            copy.wait()
        self.copies = []
        if s == 0:
            pl.semaphore_signal(r.free.at[self.sem, 2], inc=1, device_id=self.sibling(), device_id_type=MESH)
            self.add(n, r.from_core, [self.buf])
        elif s in (1, 2):
            q = n // 4 ** s
            base = self.buf + (0 if s == 1 else 3 * n // 4)
            self.free(s - 1)
            self.at = self.at + self.peers(s - 1)[0] * q
            self.add(q, r.from_chip, [base + d * q for d in range(3)])
        elif s == 3:
            q = n // 16
            at, mine = self.rows(self.at, q), self.lanes(self.peers(2)[0])
            buf = pl.ds(self.buf + 15 * n // 16, q)
            r.g[at, mine] = r.g[at, mine] + r.from_chip[buf, 0:128] + r.from_chip[buf, 128:256] + r.from_chip[buf, 256:384]
        elif s == 4:
            q = n // 16
            at, mine = self.rows(self.at, q), self.peers(2)[0]
            for d in range(3):
                r.g[at, self.lanes((mine + 3 - d) % 4)] = r.turn[d, self.buf // 16:self.buf // 16 + q]
        elif s in (5, 6):
            q = n // 4 ** (7 - s)
            self.at = self.at - self.peers(6 - s)[0] * q

    def start(self):
        r, n = self.r, self.n
        self.step = s = self.step + 1
        if s == 0:
            core = self.where[1]
            self.send(r.g.at[self.rows(self.row + (1 - core) * n, n)], r.from_core.at[pl.ds(self.buf, n)], self.sibling(), 0)
        elif s in (1, 2):
            q = n // 4 ** s
            base = self.buf + (0 if s == 1 else 3 * n // 4)
            for d, (there, dev) in enumerate(self.peers(s - 1)[1]):
                self.send(r.g.at[self.rows(self.at + there * q, q)], r.from_chip.at[pl.ds(base + d * q, q)], dev, d)
        elif s == 3:
            q = n // 16
            at = self.rows(self.at, q)
            for d, (there, dev) in enumerate(self.peers(2)[1]):
                self.send(r.g.at[at, self.lanes(there)], r.from_chip.at[pl.ds(self.buf + 15 * n // 16, q), pl.ds(d * 128, 128)], dev, d)
        elif s == 4:
            q = n // 16
            mine, devs = self.peers(2)
            for d, (there, dev) in enumerate(devs):
                self.send(r.g.at[self.rows(self.at, q), self.lanes(mine)], r.turn.at[d, pl.ds(self.buf // 16, q)], dev, d)
        elif s in (5, 6):
            q = n // 4 ** (7 - s)
            part = r.g.at[self.rows(self.at, q)]
            pl.semaphore_wait(r.free.at[self.sem, 6 - s], 3)
            for d, (there, dev) in enumerate(self.peers(6 - s)[1]):
                self.send(part, part, dev, d)
        elif s == 7:
            part = r.g.at[self.rows(self.at, n)]
            pl.semaphore_wait(r.free.at[self.sem, 2], 1)
            self.send(part, part, self.sibling(), 0)


class Exchange:
    def __init__(self, r, which, pack, seq):
        self.r, self.sems, self.pack, self.seq = r, r.esem.at[which], pack, seq

    def send(self, src, dst, way):
        copies = []
        for step in range(1, 16):
            peer = lax.rem(self.seq + step, 16)
            copy = pltpu.make_async_remote_copy(
                src_ref=src.at[peer], dst_ref=dst.at[self.seq],
                send_sem=self.sems.at[2 * way, step - 1], recv_sem=self.sems.at[2 * way + 1, step - 1],
                device_id=(self.pack, peer), device_id_type=MESH)
            copy.start()
            copies.append(copy)
        dst[self.seq] = src[self.seq]
        self.copies = copies

    def wait(self):
        for copy in self.copies:
            copy.wait()

    def begin(self):
        self.send(self.r.out, self.r.arrived, 0)

    def turn(self):
        self.wait()
        arrived, back = self.r.arrived, self.r.back

        def left(dev, carry):
            total, small = carry
            tail, mine = arrived[dev - 1, 128:136], arrived[dev, 128:136]
            whole = tail[2:3] == tail[3:4]
            joins = tail[3:4] == mine[2:3]
            total = jnp.where(joins, arrived[dev - 1, 64:128] + jnp.where(whole, total, 0.0), 0.0)
            small = jnp.where(joins, tail[1:2] + jnp.where(whole, small, 0.0), 0.0)
            back[dev, 0:64] = total
            back[dev, 128:129] = small
            return total, small

        def right(i, carry):
            dev = 14 - i
            total, small = carry
            tail, mine = arrived[dev + 1, 128:136], arrived[dev, 128:136]
            whole = tail[2:3] == tail[3:4]
            joins = mine[3:4] == tail[2:3]
            total = jnp.where(joins, arrived[dev + 1, 0:64] + jnp.where(whole, total, 0.0), 0.0)
            small = jnp.where(joins, tail[0:1] + jnp.where(whole, small, 0.0), 0.0)
            back[dev, 64:128] = total
            back[dev, 129:130] = small
            return total, small

        none = (jnp.zeros((64, 128), F32), jnp.zeros((1, 128), F32))
        for dev in range(16):
            back[dev, 128:136] = jnp.zeros((8, 128), F32)
        back[0, 0:64] = none[0]
        back[15, 64:128] = none[0]
        lax.fori_loop(1, 16, left, none)
        lax.fori_loop(0, 15, right, none)
        self.send(back, self.r.got, 1)


class Gains:
    def __init__(self, r, pack, seq):
        self.r, self.pack, self.seq = r, pack, seq

    def send(self, src, dst, way, size):
        self.copies = []
        for step in range(1, size):
            dev = (lax.rem(self.pack + step, 8), self.seq) if way == 0 else (self.pack, lax.rem(self.seq + step, 16))
            copy = pltpu.make_async_remote_copy(
                src_ref=src, dst_ref=dst.at[step - 1], send_sem=self.r.gsem.at[2 * way, step - 1],
                recv_sem=self.r.gsem.at[2 * way + 1, step - 1], device_id=dev, device_id_type=MESH)
            copy.start()
            self.copies.append(copy)

    def begin(self):
        self.send(self.r.gain_here, self.r.gain_pack, 0, 8)

    def turn(self):
        for copy in self.copies:
            copy.wait()
        total = self.r.gain_here[...]
        for i in range(7):
            total = total + self.r.gain_pack[i]
        self.r.gain_mid[...] = total
        self.send(self.r.gain_mid, self.r.gain_seq, 1, 16)

    def end(self):
        for copy in self.copies:
            copy.wait()
        total = self.r.gain_mid[...]
        for i in range(15):
            total = total + self.r.gain_seq[i]
        return total


class Refs:
    pass


SCRATCH = [
    ("x", (T, D), BF16), ("cot", (T, D), BF16),
    ("wqkv", (3, D, D), BF16), ("wo", (D, D), BF16),
    ("wup", (4, D, 512), BF16), ("wdown", (4, 512, D), BF16), ("rf", (H, DH, M), BF16),
    ("rx", (4, 256, 512), BF16), ("r80", (H, 80, M), BF16),
    ("nb", (T, D), BF16), ("nT", (D, T), BF16), ("qT", (D, T), BF16), ("kT", (D, T), BF16),
    ("xb", (4, T, 512), BF16),
    ("gup", (4, T, 512), BF16),
    ("vext", (H, 80, T), BF16), ("gext", (H, 80, T), BF16),
    ("phik", (H, T, M), BF16), ("phiq", (H, T, M), BF16),
    ("dcol", (T, T), F32),
    ("num", (H, DH, T), F32), ("den", (H, 8, T), F32),
    ("attT", (D, T), BF16), ("att", (T, D), BF16), ("mid", (T, D), F32), ("hid", (T, D), BF16),
    ("acc", (T, D), F32), ("acc2", (T, D), F32), ("gmid", (T, D), F32),
    ("sb1", (H, 144, M), BF16), ("sb2", (H, 144, M), BF16),
            ("out", (16, SLAB, 128), F32), ("arrived", (16, SLAB, 128), F32), ("got", (16, SLAB, 128), F32),
    ("from_core", (3072, 512), F32), ("from_chip", (3072, 512), F32), ("turn", (3, 192, 128), F32),
    ("gain_sum", (2, 8, D), F32), ("gain_here", (8, 128), F32), ("gain_pack", (7, 8, 128), F32), ("gain_mid", (8, 128), F32), ("gain_seq", (15, 8, 128), F32),
]
SEMS = [
    ("load", pltpu.SemaphoreType.DMA((20,))),
    ("esem", pltpu.SemaphoreType.DMA((2, 4, 15))), ("gsem", pltpu.SemaphoreType.DMA((4, 15))),
    ("ssem", pltpu.SemaphoreType.DMA((9, 8, 3))), ("rsem", pltpu.SemaphoreType.DMA((9, 8, 3))),
    ("free", pltpu.SemaphoreType.REGULAR((9, 3))),
]
ROW_DOWN, ROW_UP, ROW_O, ROW_Q, ROW_K, ROW_V = 0, 2048, 4096, 4608, 5120, 5632


def kernel(
    x_h, wq_h, wk_h, wv_h, wo_h, wup_h, wdown_h, rf_h, cot_h, ga_ref, gf_ref, doc_ref, live_ref,
    obf, gibf, g, gain_ref, *scratch):
    r = Refs()
    r.obf, r.gibf, r.g = obf, gibf, g
    for (name, *_), ref in zip(SCRATCH + SEMS, scratch):
        setattr(r, name, ref)
    r.gb, r.hidT, r.gT, r.back = r.nb, r.att, r.gup, r.out
    where = place()
    z, core, px, py = where
    pack, seq = lax.axis_index("pack"), lax.axis_index("seq")

    loads = {}

    def load(name, src, dst):
        copy = pltpu.make_async_copy(src, dst, r.load.at[len(loads)])
        copy.start()
        loads[name] = copy

    load("x", x_h, r.x)
    load("wk", wk_h, r.wqkv.at[1])
    load("wv", wv_h, r.wqkv.at[2])
    load("rf", rf_h, r.rf)
    load("wq", wq_h, r.wqkv.at[0])
    load("wo", wo_h, r.wo)
    for j in range(4):
        load("wup%d" % j, wup_h.at[:, pl.ds(j * 512, 512)], r.wup.at[j])
    load("cot", cot_h, r.cot)
    for j in range(4):
        load("wdown%d" % j, wdown_h.at[pl.ds(j * 512, 512)], r.wdown.at[j])
    barrier = pltpu.get_barrier_semaphore()
    for step in range(1, 16):
        pl.semaphore_signal(barrier, inc=1, device_id=(pack, lax.rem(seq + step, 16)), device_id_type=MESH)
    for step in range(1, 8):
        pl.semaphore_signal(barrier, inc=1, device_id=(lax.rem(pack + step, 8), seq), device_id_type=MESH)

    doc = doc_ref[...].astype(F32)
    doc_f, doc_l = doc[:, 0:1], doc[:, T - 1:T]
    in_f, in_l = doc == doc_f, doc == doc_l
    one_f, one_l = in_f.astype(F32), in_l.astype(F32)
    row16 = iota((16, T), 0)

    def ends(block, tail_f, tail_l):
        zero = jnp.zeros_like(block)
        tail = jnp.where(row16 == 0, tail_f, jnp.where(row16 == 1, tail_l, 0.0))
        return jnp.concatenate(
            [jnp.where(in_f, block, zero).astype(BF16), jnp.where(in_l, block, zero).astype(BF16), tail.astype(BF16)], axis=0)

    dcol = jnp.broadcast_to(doc, (128, T)).T
    for j in range(4):
        r.dcol[:, j * 128:(j + 1) * 128] = dcol
    live = jnp.broadcast_to(live_ref[...].astype(F32), (128, T)).T

    loads["x"].wait()

    def first_norm(rows, c):
        n, _ = layer_norm(r.x[rows, :].astype(F32))
        r.nb[rows, :] = (n * ga_ref[...]).astype(BF16)
        return c

    row_loop(64, first_norm)
    loads["rf"].wait()
    for p in range(4):
        lane, row = iota((256, 512), 1) // 256, iota((256, 512), 0)
        pick = (row >= 128) & (row < 152) & (row % 8 == 2 * p + lane)
        r.rx[p] = jnp.where(pick, 1.0, 0.0).astype(BF16)
        r.rx[p, 0:64, 0:256] = r.rf[2 * p]
        r.rx[p, 64:128, 256:512] = r.rf[2 * p + 1]
    for h in range(H):
        r.r80[h, 0:64] = r.rf[h]
        r.r80[h, 64:80] = jnp.where(iota((16, M), 0) == 0, 1.0, 0.0).astype(BF16)
    pick_heads = ((iota((D, 128), 1) % 8 == iota((D, 128), 0) // DH) & (iota((D, 128), 1) < 24)).astype(BF16)

    def features(w, low, transposed, phi, off, alive):
        flat = dot(r.nb[...], r.wqkv[w]).astype(BF16)
        transposed[...] = flat.T
        square = flat.astype(F32)
        square = square * square
        high = square.astype(BF16)
        rest = (square - high.astype(F32)).astype(BF16)
        size = dot(high, pick_heads) + dot(rest, pick_heads)
        shift = size * (-0.5 * C) - 4.0 / ALPHA
        if alive is not None:
            shift = shift + (alive - 1.0) * 1e30
        first = shift.astype(BF16).astype(F32)
        second = (shift - first).astype(BF16).astype(F32)
        third = shift - first - second
        at = iota((T, 128), 1)
        shift = jnp.where(at < 8, first, jnp.where(at < 16, second, jnp.where(at < 24, third, 0.0))).astype(BF16)
        for p in range(4):
            low[p, :, off:off + 128] = flat[:, p * 128:(p + 1) * 128]
            low[p, :, off + 128:off + 256] = shift

        def one_pair(p, c):
            y = dot(low[p, :, off:off + 256], r.rx[p])
            y = jnp.exp2(y * ALPHA).astype(BF16)
            phi[2 * p] = y[:, 0:256]
            phi[2 * p + 1] = y[:, 256:512]
            return c

        lax.fori_loop(0, 4, one_pair, 0)

    loads["wk"].wait()
    features(1, r.xb, r.kT, r.phik, 0, live)
    loads["wv"].wait()
    vT = dot(r.nb[...], r.wqkv[2]).astype(BF16).T
    for h in range(H):
        r.vext[h, 0:64] = vT[h * 64:(h + 1) * 64]
        r.vext[h, 64:80] = jnp.where(row16 == 0, 1.0, 0.0).astype(BF16)

    def put_slab(h, lhs, phi):
        s = dot(lhs, phi)
        row = iota((8, M), 0)
        tail = jnp.where(row == 2, doc_f, jnp.where(row == 3, doc_l, s[128:136]))
        for half in range(2):
            r.out[2 * h + half, 0:128] = s[0:128, half * 128:(half + 1) * 128]
            r.out[2 * h + half, 128:136] = tail[:, half * 128:(half + 1) * 128]

    def take_slab(h, sb):
        for half in range(2):
            lanes = pl.ds(half * 128, 128)
            sb[h, 0:128, lanes] = r.got[2 * h + half, 0:128].astype(BF16)
            sb[h, 128:144, lanes] = jnp.concatenate(
                [r.got[2 * h + half, 128:136], jnp.zeros((8, 128), F32)], axis=0).astype(BF16)

    def value_ends(h):
        return ends(r.vext[h, 0:64].astype(F32), one_f, one_l)

    head_loop(lambda h: put_slab(h, value_ends(h), r.phik[h]))
    pl.semaphore_wait(barrier, 22)
    exchange = Exchange(r, 0, pack, seq)
    exchange.begin()

    r.nT[...] = r.nb[...].T
    loads["wq"].wait()
    features(0, r.xb, r.qT, r.phiq, 256, None)
    exchange.turn()

    def same(block):
        return jnp.where(r.dcol[...] == doc, block, 0.0).astype(BF16)

    def attend(h):
        local = dot_nt(r.vext[h], same(dot_nt(r.phiq[h], r.phik[h])))
        r.num[h] = local[0:64]
        r.den[h] = local[64:72]

    head_loop(attend)
    exchange.wait()

    def join(h):
        take_slab(h, r.sb1)
        far = dot_nt(r.sb1[h], r.phiq[h])
        num = r.num[h] + jnp.where(in_f, far[0:64], 0.0) + jnp.where(in_l, far[64:128], 0.0)
        den = r.den[h, 0:1] + jnp.where(in_f, far[128:129], 0.0) + jnp.where(in_l, far[129:130], 0.0)
        inv = 1.0 / den
        att = num * inv
        r.num[h] = att
        r.den[h, 0:1] = inv
        r.attT[pl.ds(pl.multiple_of(h * 64, 64), 64)] = att.astype(BF16)

    head_loop(join)
    r.att[...] = r.attT[...].T
    loads["wo"].wait()
    r.mid[...] = dot(r.att[...], r.wo[...])

    def second_norm(rows, c):
        mid = r.x[rows, :].astype(F32) + r.mid[rows, :]
        r.mid[rows, :] = mid
        n, _ = layer_norm(mid)
        r.hid[rows, :] = (n * gf_ref[...]).astype(BF16)
        return c

    row_loop(64, second_norm)

    loads["cot"].wait()
    for j in range(4):
        loads["wup%d" % j].wait()
        loads["wdown%d" % j].wait()

    def feed(j, c):
        r.acc[...] = dot(r.hid[...], r.wup[j])
        r.acc2[...] = dot_nt(r.cot[...], r.wdown[j])

        def gelu(rows, c):
            u = r.acc[rows, :]
            ga = r.acc2[rows, :].astype(BF16).astype(F32)
            sq = u * u
            t = jnp.tanh(u * (GELU_A + GELU_A * GELU_B * sq))
            half = 0.5 * (1.0 + t)
            slope = half + 0.5 * u * (1.0 - t * t) * (GELU_A + 3.0 * GELU_A * GELU_B * sq)
            r.xb[j, rows, :] = (u * half).astype(BF16)
            r.gup[j, rows, :] = (ga * slope).astype(BF16)
            return c

        row_loop(16, gelu)
        back = dot_nt(r.gup[j], r.wup[j])

        @pl.when(j == 0)
        def _():
            r.gmid[...] = back

        @pl.when(j > 0)
        def _():
            r.gmid[...] += back

        r.g[pl.ds(pl.multiple_of(ROW_DOWN + j * 512, 512), 512), :] = dot_tn(r.xb[j], r.cot[...])
        return c

    lax.fori_loop(0, 4, feed, 0)
    waves = [
        Wave(r, where, ROW_DOWN, (512, 768, 768), 0),
        Wave(r, where, ROW_UP, (768, 768, 1024), 3),
        Wave(r, where, ROW_Q, (512, 512, 512), 6),
    ]
    waves[0].tick()

    def add_gain(which, p):
        total = r.gain_sum[which]
        for i in range(8):
            total = total + p[i * 8:(i + 1) * 8]
        r.gain_sum[which] = total

    r.gain_sum[...] = jnp.zeros((2, 8, D), F32)

    def second_back(rows, c):
        gh = r.gmid[rows, :].astype(BF16).astype(F32)
        n, scale = layer_norm(r.mid[rows, :])
        gm = r.cot[rows, :].astype(F32) + norm_back(n, scale, gh * gf_ref[...])
        r.gmid[rows, :] = gm
        r.gb[rows, :] = gm.astype(BF16)
        add_gain(1, gh * n)
        return c

    row_loop(64, second_back)
    waves[0].tick()
    r.acc[...] = dot_nt(r.wo[...], r.gb[...])

    def gates(h):
        ga = r.acc[pl.ds(pl.multiple_of(h * 64, 64), 64)].astype(BF16).astype(F32)
        inv = r.den[h, 0:1]
        gn = (ga * inv).astype(BF16)
        gd = -jnp.sum(ga * r.num[h], axis=0, keepdims=True) * inv
        r.gext[h, 0:64] = gn
        r.gext[h, 64:80] = jnp.where(row16 == 0, gd, 0.0).astype(BF16)
        put_slab(h, grad_ends(h), r.phiq[h])

    def grad_ends(h):
        gd = r.gext[h, 64:80].astype(F32)[0:1]
        return ends(r.gext[h, 0:64].astype(F32), one_f * gd, one_l * gd)

    head_loop(gates)
    exchange = Exchange(r, 1, pack, seq)
    exchange.begin()

    def block(row, value):
        r.g[row:row + 512, :] = value

    r.hidT[...] = r.hid[...].T
    for j in range(4):
        block(ROW_UP + j * 512, dot(r.hidT[...], r.gup[j]))
    block(ROW_O, dot(r.attT[...], r.gb[...]))
    waves[1].tick()

    def map_back(h, gphi, phi, flat, which):
        p = (gphi.astype(BF16).astype(F32) * phi.astype(F32)).astype(BF16)
        through = dot_nt(r.r80[h], p)
        rows = pl.ds(pl.multiple_of(h * 64, 64), 64)
        r.gT[which, rows] = (C * through[0:64] - (C * C) * through[64:65] * flat[rows].astype(F32)).astype(BF16)

    def query_back(h):
        gphi = dot(same(dot_tn(r.gext[h], r.vext[h])), r.phik[h]) + dot_tn(grad_ends(h), r.sb1[h])
        map_back(h, gphi, r.phiq[h], r.qT, 0)
        r.acc2[pl.ds(pl.multiple_of(h * 64, 64), 64)] = dot(r.gext[h, 0:64], same(dot_nt(r.phiq[h], r.phik[h])))

    head_loop(query_back, 0, 3)
    waves[1].tick()
    head_loop(query_back, 3, 6)
    waves[0].tick()
    exchange.turn()
    head_loop(query_back, 6, 8)
    block(ROW_Q, dot_nt(r.nT[...], r.gT[0]))
    r.acc[...] = dot(r.xb[0], r.wdown[0])
    for j in range(1, 4):
        r.acc[...] += dot(r.xb[j], r.wdown[j])

    def put_out(rows, c):
        r.obf[rows, :] = (r.mid[rows, :] + r.acc[rows, :]).astype(BF16)
        return c

    row_loop(64, put_out)
    waves[0].tick()
    exchange.wait()

    def key_back(h):
        take_slab(h, r.sb2)
        gphi = dot(same(dot_tn(r.vext[h], r.gext[h])), r.phiq[h]) + dot_tn(value_ends(h), r.sb2[h])
        map_back(h, gphi, r.phik[h], r.kT, 1)
        far = dot_nt(r.sb2[h, 0:128], r.phik[h])
        rows = pl.ds(pl.multiple_of(h * 64, 64), 64)
        r.gT[2, rows] = (r.acc2[rows] + jnp.where(in_f, far[0:64], 0.0) + jnp.where(in_l, far[64:128], 0.0)).astype(BF16)

    head_loop(key_back, 0, 4)
    waves[0].tick()
    waves[1].tick()
    head_loop(key_back, 4, 8)
    block(ROW_K, dot_nt(r.nT[...], r.gT[1]))
    block(ROW_V, dot_nt(r.nT[...], r.gT[2]))
    waves[2].tick()
    waves[0].tick()
    waves[1].tick()
    r.acc2[...] = dot(r.wqkv[0], r.gT[0])

    def normed_back(i, c):
        r.acc2[...] += dot(r.wqkv[i], r.gT[i])
        return c

    lax.fori_loop(1, 3, normed_back, 0)
    r.acc[...] = r.acc2[...].T
    waves[2].tick()

    def first_back(rows, c):
        gn = r.acc[rows, :].astype(BF16).astype(F32)
        n, scale = layer_norm(r.x[rows, :].astype(F32))
        r.gibf[rows, :] = (r.gmid[rows, :] + norm_back(n, scale, gn * ga_ref[...])).astype(BF16)
        add_gain(0, gn * n)
        return c

    row_loop(64, first_back)
    for which in range(2):
        total = r.gain_sum[which, 0:1]
        for i in range(1, 8):
            total = total + r.gain_sum[which, i:i + 1]
        for j in range(4):
            r.gain_here[4 * which + j:4 * which + j + 1] = total[:, j * 128:(j + 1) * 128]
    gains = Gains(r, pack, seq)
    gains.begin()
    order = (waves[1], waves[2], waves[0])
    for wave in order:
        wave.tick()
    gains.turn()
    while not all(wave.done for wave in waves):
        for wave in order:
            wave.tick()
    gain_ref[...] = gains.end()


def store_kernel(out, gin, g, gain, out_h, gin_h, gwq_h, gwk_h, gwv_h, gwo_h, gwup_h, gwdown_h, gain_h, sems):
    pieces = [(g.at[pl.ds(ROW_DOWN, FF)], gwdown_h)]
    pieces += [(g.at[pl.ds(ROW_UP + j * 512, 512)], gwup_h.at[:, pl.ds(j * 512, 512)]) for j in range(4)]
    pieces += [(g.at[pl.ds(row, 512)], dst) for row, dst in ((ROW_O, gwo_h), (ROW_Q, gwq_h), (ROW_K, gwk_h), (ROW_V, gwv_h))]
    pieces += [(out, out_h), (gin, gin_h), (gain, gain_h)]
    copies = [pltpu.make_async_copy(src, dst, sems.at[i]) for i, (src, dst) in enumerate(pieces)]
    for copy in copies:
        copy.start()
    for copy in copies:
        copy.wait()


def per_device(
    inputs, w_query, w_key, w_value, w_output, w_up, w_down, gain_attn, gain_ffn, random_features, doc_ids, live_rows, cotangent):
    hbm = pl.BlockSpec(memory_space=pltpu.HBM)
    vmem = pl.BlockSpec(memory_space=pltpu.VMEM)
    f32 = lambda *shape: jax.ShapeDtypeStruct(shape, F32)
    low = jax.ShapeDtypeStruct((T, D), BF16)
    held = pl.pallas_call(
        kernel,
        out_shape=(pltpu.VMEM((T, D), BF16), pltpu.VMEM((T, D), BF16), pltpu.VMEM((6144, 512), F32), pltpu.VMEM((8, 128), F32)),
        in_specs=[hbm] * 9 + [vmem] * 4,
        out_specs=(vmem,) * 4,
        scratch_shapes=[pltpu.VMEM(shape, dtype) for _, shape, dtype in SCRATCH] + [sem for _, sem in SEMS],
        compiler_params=pltpu.CompilerParams(collective_id=0, has_side_effects=True, vmem_limit_bytes=VMEM_LIMIT),
    )(
        *[pltpu.with_memory_space_constraint(v, pltpu.HBM) for v in (
            inputs[0], w_query, w_key, w_value, w_output, w_up, w_down, random_features, cotangent[0])],
        gain_attn[None], gain_ffn[None], doc_ids, live_rows)
    outs = pl.pallas_call(
        store_kernel,
        out_shape=(low, low, f32(D, D), f32(D, D), f32(D, D), f32(D, D), f32(D, FF), f32(FF, D), f32(8, 128)),
        in_specs=[vmem] * 4,
        out_specs=(hbm,) * 9,
        scratch_shapes=[pltpu.SemaphoreType.DMA((12,))],
        compiler_params=pltpu.CompilerParams(vmem_limit_bytes=1 * 2**20),
    )(*held)
    gain = outs[8].reshape(2 * D)
    return (outs[0][None], outs[1][None]) + tuple(outs[2:8]) + (gain[:D], gain[D:])


def solution(mesh):
    rows = P("pack", "seq", None)
    return jax.shard_map(
        per_device,
        mesh=mesh,
        in_specs=(rows,) + (P(),) * 9 + (P("pack", "seq"), P("pack", "seq"), rows),
        out_specs=(rows, rows) + (P(),) * 8,
        check_vma=False,
    )
```

```python
import functools
import math

import jax
import jax.numpy as jnp
from jax import lax
from jax.experimental import pallas as pl
from jax.experimental.pallas import tpu as pltpu
from jax.sharding import PartitionSpec as P

MESH = pl.DeviceIdType.MESH
F32, BF16 = jnp.float32, jnp.bfloat16
T, D, H, DH, M, FF = 512, 512, 8, 64, 256, 2048
SLAB = 136
EPS = 1e-05
VMEM_LIMIT = 47 * 2**20
C = DH ** -0.25
ALPHA = C * math.log2(math.e)
GELU_A, GELU_B = math.sqrt(2.0 / math.pi), 0.044715


def dot(a, b):
    return lax.dot_general(a, b, (((1,), (0,)), ((), ())), preferred_element_type=F32)


def dot_nt(a, b):
    return lax.dot_general(a, b, (((1,), (1,)), ((), ())), preferred_element_type=F32)


def dot_tn(a, b):
    return lax.dot_general(a, b, (((0,), (0,)), ((), ())), preferred_element_type=F32)


def iota(shape, dim):
    return lax.broadcasted_iota(jnp.int32, shape, dim)


def place():
    pack, seq = lax.axis_index("pack"), lax.axis_index("seq")
    return pack >> 1, pack & 1, seq >> 2, seq & 3


def layer_norm(v):
    centred = v - jnp.mean(v, axis=-1, keepdims=True)
    scale = lax.rsqrt(jnp.mean(centred * centred, axis=-1, keepdims=True) + EPS)
    return centred * scale, scale


def norm_back(n, scale, e):
    return scale * (e - jnp.mean(e, axis=-1, keepdims=True) - n * jnp.mean(e * n, axis=-1, keepdims=True))


def row_loop(step, body, carry=0):
    def run(i, c):
        return body(pl.ds(pl.multiple_of(i * step, step), step), c)

    return lax.fori_loop(0, T // step, run, carry)


def head_loop(body, start=0, stop=H):
    def run(h, c):
        body(h)
        return c

    lax.fori_loop(start, stop, run, 0)


def wait_all(like, send_sem, recv_sem, dev):
    pltpu.make_async_remote_copy(
        src_ref=like, dst_ref=like, send_sem=send_sem, recv_sem=recv_sem, device_id=dev, device_id_type=MESH).wait()


class Part:
    def __init__(self, r, where, number, row, rows, axes, down, up):
        self.r, self.where, self.row, self.n = r, where, row, rows // 2
        self.axes = dict(zip("oic", axes))
        self.down, self.up = down, up
        self.number = number
        self.at = row + where[1] * self.n
        self.buf = row // 2
        self.step, self.last = -1, len(down) + len(up) + 1
        self.flying, self.held, self.freed = 0, {}, set()

    def mine(self, role):
        z, core, x, y = self.where
        return (x, y, z)[self.axes[role]]

    def peers(self, roles):
        z, core, x, y = self.where
        out = []
        for far in range(1, 4 ** len(roles)):
            at = {role: (self.mine(role) + far // 4 ** k) & 3 for k, role in enumerate(roles)}
            spot = [x, y, z]
            for role, there in at.items():
                spot[self.axes[role]] = there
            out.append((at, (spot[2] * 2 + core, spot[0] * 4 + spot[1])))
        return out

    def behind(self, roles, d):
        return {role: (self.mine(role) - (d + 1) // 4 ** k) & 3 for k, role in enumerate(roles)}

    def sibling(self):
        z, core, x, y = self.where
        return (z * 2 + 1 - core, x * 4 + y)

    def block(self, at={}):
        at = {**self.held, **at}
        row, rows, lane, lanes = self.at, self.n, 0, 512
        if "o" in at:
            row, rows = row + at["o"] * (self.n // 4), self.n // 4
        if "i" in at:
            row, rows = row + at["i"] * (self.n // 16), self.n // 16
        if "c" in at:
            lane, lanes = pl.multiple_of(at["c"] * 128, 128), 128
        return row, rows, lane, lanes

    def view(self, block):
        row, rows, lane, lanes = block
        return self.r.g.at[pl.ds(pl.multiple_of(row, 8), rows), pl.ds(lane, lanes)]

    def landing(self, roles, d):
        n = self.n
        row, lane = {
            "o": (d * (n // 4), 0),
            "ic": (3 * n // 4 + d // 4 * (n // 16), d % 4 * 128),
            "c": (0, d * 128),
            "oi": (d * (n // 16), 384),
        }[roles]
        return self.buf + row, lane

    def send(self, src, dst, dev):
        pltpu.make_async_remote_copy(
            src_ref=src, dst_ref=dst, send_sem=self.r.ssem.at[self.number], recv_sem=self.r.rsem.at[self.number, self.step],
            device_id=dev, device_id_type=MESH).start()
        self.flying += 1
        self.piece = src.shape

    def add(self, block, buf, slots):
        r = self.r
        row, rows, lane, lanes = block
        step = min(16384 // lanes, rows)

        def body(i, c):
            at = pl.ds(pl.multiple_of(row + i * step, 8), step)
            total = r.g[at, pl.ds(lane, lanes)]
            for slot, column in slots:
                total = total + buf[pl.ds(pl.multiple_of(slot + i * step, 8), step), pl.ds(column, lanes)]
            r.g[at, pl.ds(lane, lanes)] = total
            return c

        lax.fori_loop(0, rows // step, body, 0)

    def finish(self):
        r, s, downs = self.r, self.step, len(self.down)
        if self.flying:
            rows, lanes = self.piece
            wait_all(r.from_chip.at[pl.ds(0, self.flying * rows), pl.ds(0, lanes)], r.ssem.at[self.number], r.rsem.at[self.number, s], self.sibling())
        self.flying = 0
        if s == 0:
            pl.semaphore_signal(r.free.at[self.number, 0], inc=1, device_id=self.sibling(), device_id_type=MESH)
            self.add(self.block(), r.from_core, [(self.buf, 0)])
        elif 1 <= s <= downs:
            roles = self.down[s - 1]
            self.held.update({role: self.mine(role) for role in roles})
            for k in range(1, len(self.up)):
                if k not in self.freed and set(self.up[k]) <= set(self.held):
                    self.freed.add(k)
                    for _, dev in self.peers(self.up[k]):
                        pl.semaphore_signal(r.free.at[self.number, k], inc=1, device_id=dev, device_id_type=MESH)
            self.add(self.block(), r.from_chip, [self.landing(roles, d) for d in range(4 ** len(roles) - 1)])
        elif downs < s < self.last:
            roles = self.up[s - downs - 1]
            if s == downs + 1:
                for d in range(4 ** len(roles) - 1):
                    row, rows, lane, lanes = self.block(self.behind(roles, d))
                    r.g[pl.ds(pl.multiple_of(row, 8), rows), pl.ds(lane, lanes)] = r.turn[d, pl.ds(self.buf // 16, rows)]
            for role in roles:
                del self.held[role]

    def start(self):
        r, n, downs = self.r, self.n, len(self.down)
        self.step = s = self.step + 1
        if s == 0:
            core = self.where[1]
            self.send(r.g.at[pl.ds(pl.multiple_of(self.row + (1 - core) * n, 8), n)], r.from_core.at[pl.ds(self.buf, n)], self.sibling())
        elif 1 <= s <= downs:
            roles = self.down[s - 1]
            for d, (at, dev) in enumerate(self.peers(roles)):
                block = self.block(at)
                row, lane = self.landing(roles, d)
                self.send(self.view(block), r.from_chip.at[pl.ds(row, block[1]), pl.ds(lane, block[3])], dev)
        elif downs < s < self.last:
            k = s - downs - 1
            roles = self.up[k]
            block = self.block()
            part = self.view(block)
            peers = self.peers(roles)
            if k > 0:
                pl.semaphore_wait(r.free.at[self.number, k], len(peers))
            for d, (at, dev) in enumerate(peers):
                self.send(part, part if k > 0 else r.turn.at[d, pl.ds(self.buf // 16, block[1])], dev)
        elif s == self.last:
            part = self.view(self.block())
            pl.semaphore_wait(r.free.at[self.number, 0], 1)
            self.send(part, part, self.sibling())

    def tick(self):
        if self.step <= self.last:
            self.finish()
            self.start()


def tick(*parts):
    for part in parts:
        part.tick()


class Exchange:
    def __init__(self, r, which, pack, seq):
        self.r, self.sems, self.pack, self.seq = r, r.esem.at[which], pack, seq

    def send(self, src, dst, way):
        for step in range(1, 16):
            peer = (self.seq + step) & 15
            pltpu.make_async_remote_copy(
                src_ref=src.at[peer], dst_ref=dst.at[self.seq], send_sem=self.sems.at[2], recv_sem=self.sems.at[way],
                device_id=(self.pack, peer), device_id_type=MESH).start()
        dst[self.seq] = src[self.seq]
        self.way = way

    def wait(self):
        wait_all(self.r.arrived.at[pl.ds(0, 15)], self.sems.at[2], self.sems.at[self.way], (self.pack, (self.seq + 1) & 15))

    def begin(self):
        self.send(self.r.out, self.r.arrived, 0)

    def turn(self, between=lambda: None):
        self.wait()
        between()
        arrived, back = self.r.arrived, self.r.back

        def left(dev, carry):
            total, small = carry
            tail, mine = arrived[dev - 1, 128:136], arrived[dev, 128:136]
            whole = tail[2:3] == tail[3:4]
            joins = tail[3:4] == mine[2:3]
            total = jnp.where(joins, arrived[dev - 1, 64:128] + jnp.where(whole, total, 0.0), 0.0)
            small = jnp.where(joins, tail[1:2] + jnp.where(whole, small, 0.0), 0.0)
            back[dev, 0:64] = total
            back[dev, 128:129] = small
            return total, small

        def right(i, carry):
            dev = 14 - i
            total, small = carry
            tail, mine = arrived[dev + 1, 128:136], arrived[dev, 128:136]
            whole = tail[2:3] == tail[3:4]
            joins = mine[3:4] == tail[2:3]
            total = jnp.where(joins, arrived[dev + 1, 0:64] + jnp.where(whole, total, 0.0), 0.0)
            small = jnp.where(joins, tail[0:1] + jnp.where(whole, small, 0.0), 0.0)
            back[dev, 64:128] = total
            back[dev, 129:130] = small
            return total, small

        none = (jnp.zeros((64, 128), F32), jnp.zeros((1, 128), F32))
        for dev in range(16):
            back[dev, 128:136] = jnp.zeros((8, 128), F32)
        back[0, 0:64] = none[0]
        back[15, 64:128] = none[0]
        lax.fori_loop(1, 16, left, none)
        lax.fori_loop(0, 15, right, none)
        self.send(back, self.r.got, 1)


class Gains:
    def __init__(self, r, pack, seq):
        self.r, self.pack, self.seq = r, pack, seq

    def send(self, src, dst, way, size):
        for step in range(1, size):
            dev = ((self.pack + step) & 7, self.seq) if way == 0 else (self.pack, (self.seq + step) & 15)
            pltpu.make_async_remote_copy(
                src_ref=src, dst_ref=dst.at[step - 1], send_sem=self.r.gsem.at[2], recv_sem=self.r.gsem.at[way],
                device_id=dev, device_id_type=MESH).start()

    def wait(self, like, way):
        wait_all(like, self.r.gsem.at[2], self.r.gsem.at[way], (self.pack, (self.seq + 1) & 15))

    def begin(self):
        self.send(self.r.gain_here, self.r.gain_pack, 0, 8)

    def turn(self):
        self.wait(self.r.gain_pack, 0)
        total = self.r.gain_here[...]
        for i in range(7):
            total = total + self.r.gain_pack[i]
        self.r.gain_mid[...] = total
        self.send(self.r.gain_mid, self.r.gain_seq, 1, 16)

    def end(self):
        self.wait(self.r.gain_seq, 1)
        total = self.r.gain_mid[...]
        for i in range(15):
            total = total + self.r.gain_seq[i]
        return total


class Refs:
    pass


SCRATCH = [
    ("x", (T, D), BF16), ("cot", (T, D), BF16),
    ("wqkv", (3, D, D), BF16), ("wo", (D, D), BF16),
    ("wup", (4, D, 512), BF16), ("wdown", (4, 512, D), BF16), ("rf", (H, DH, M), BF16),
    ("rx", (4, 256, 512), BF16), ("r80", (H, 80, M), BF16),
    ("nb", (T, D), BF16), ("nT", (D, T), BF16), ("qT", (D, T), BF16), ("kT", (D, T), BF16),
    ("xb", (4, T, 512), BF16),
    ("gup", (4, T, 512), BF16),
    ("vext", (H, 80, T), BF16), ("gext", (H, 80, T), BF16),
    ("phik", (H, T, M), BF16), ("phiq", (H, T, M), BF16),
    ("dcol", (T, T), F32),
    ("num", (H, DH, T), F32), ("den", (H, 8, T), F32),
    ("attT", (D, T), BF16), ("att", (T, D), BF16), ("mid", (T, D), F32), ("hid", (T, D), BF16),
    ("acc", (T, D), F32), ("acc2", (T, D), F32), ("gmid", (T, D), F32),
    ("sb1", (H, 144, M), BF16), ("sb2", (H, 144, M), BF16),
            ("out", (16, SLAB, 128), F32), ("arrived", (16, SLAB, 128), F32), ("got", (16, SLAB, 128), F32),
    ("from_core", (3072, 512), F32), ("from_chip", (3072, 512), F32), ("turn", (15, 192, 128), F32),
    ("gain_sum", (2, 8, D), F32), ("gain_here", (8, 128), F32), ("gain_pack", (7, 8, 128), F32), ("gain_mid", (8, 128), F32), ("gain_seq", (15, 8, 128), F32),
]
SEMS = [
    ("load", pltpu.SemaphoreType.DMA((9,))), ("esem", pltpu.SemaphoreType.DMA((2, 3))), ("gsem", pltpu.SemaphoreType.DMA((3,))),
    ("ssem", pltpu.SemaphoreType.DMA((11,))), ("rsem", pltpu.SemaphoreType.DMA((11, 6))), ("free", pltpu.SemaphoreType.REGULAR((11, 2))),
]
ROW_DOWN, ROW_UP, ROW_O, ROW_Q, ROW_K, ROW_V = 0, 2048, 4096, 4608, 5120, 5632


def kernel(
    x_h, wq_h, wk_h, wv_h, wo_h, wup_h, wdown_h, rf_h, cot_h, ga_ref, gf_ref, doc_ref, live_ref,
    obf, gibf, g, gain_ref, *scratch):
    r = Refs()
    r.obf, r.gibf, r.g = obf, gibf, g
    for (name, *_), ref in zip(SCRATCH + SEMS, scratch):
        setattr(r, name, ref)
    r.gb, r.hidT, r.gT, r.back = r.nb, r.att, r.gup, r.out
    where = place()
    z, core, px, py = where
    pack, seq = lax.axis_index("pack"), lax.axis_index("seq")

    loads = {}

    def load(name, src, dst):
        copy = pltpu.make_async_copy(src, dst, r.load.at[len(loads)])
        copy.start()
        loads[name] = copy

    load("x", x_h, r.x)
    load("wk", wk_h, r.wqkv.at[1])
    load("rf", rf_h, r.rf)
    load("wv", wv_h, r.wqkv.at[2])
    load("wq", wq_h, r.wqkv.at[0])
    barrier = pltpu.get_barrier_semaphore()
    for step in range(1, 16):
        pl.semaphore_signal(barrier, inc=1, device_id=(pack, (seq + step) & 15), device_id_type=MESH)
    for step in range(1, 8):
        pl.semaphore_signal(barrier, inc=1, device_id=((pack + step) & 7, seq), device_id_type=MESH)

    doc = doc_ref[...].astype(F32)
    doc_f, doc_l = doc[:, 0:1], doc[:, T - 1:T]
    in_f, in_l = doc == doc_f, doc == doc_l
    one_f, one_l = in_f.astype(F32), in_l.astype(F32)
    row16 = iota((16, T), 0)

    def ends(block, tail_f, tail_l):
        zero = jnp.zeros_like(block)
        tail = jnp.where(row16 == 0, tail_f, jnp.where(row16 == 1, tail_l, 0.0))
        return jnp.concatenate(
            [jnp.where(in_f, block, zero).astype(BF16), jnp.where(in_l, block, zero).astype(BF16), tail.astype(BF16)], axis=0)

    dcol = jnp.broadcast_to(doc, (128, T)).T
    for j in range(4):
        r.dcol[:, j * 128:(j + 1) * 128] = dcol
    live = jnp.broadcast_to(live_ref[...].astype(F32), (128, T)).T

    loads["x"].wait()

    def first_norm(rows, c):
        n, _ = layer_norm(r.x[rows, :].astype(F32))
        r.nb[rows, :] = (n * ga_ref[...]).astype(BF16)
        return c

    row_loop(64, first_norm)
    loads["rf"].wait()
    for p in range(4):
        lane, row = iota((256, 512), 1) // 256, iota((256, 512), 0)
        pick = (row >= 128) & (row < 152) & (row % 8 == 2 * p + lane)
        r.rx[p] = jnp.where(pick, 1.0, 0.0).astype(BF16)
        r.rx[p, 0:64, 0:256] = r.rf[2 * p]
        r.rx[p, 64:128, 256:512] = r.rf[2 * p + 1]
    for h in range(H):
        r.r80[h, 0:64] = r.rf[h]
        r.r80[h, 64:80] = jnp.where(iota((16, M), 0) == 0, 1.0, 0.0).astype(BF16)
    pick_heads = ((iota((D, 128), 1) % 8 == iota((D, 128), 0) // DH) & (iota((D, 128), 1) < 24)).astype(BF16)

    def features(w, low, transposed, phi, off, alive):
        flat = dot(r.nb[...], r.wqkv[w]).astype(BF16)
        transposed[...] = flat.T
        square = flat.astype(F32)
        square = square * square
        high = square.astype(BF16)
        rest = (square - high.astype(F32)).astype(BF16)
        size = dot(high, pick_heads) + dot(rest, pick_heads)
        shift = size * (-0.5 * C) - 4.0 / ALPHA
        if alive is not None:
            shift = shift + (alive - 1.0) * 1e30
        first = shift.astype(BF16).astype(F32)
        second = (shift - first).astype(BF16).astype(F32)
        third = shift - first - second
        at = iota((T, 128), 1)
        shift = jnp.where(at < 8, first, jnp.where(at < 16, second, jnp.where(at < 24, third, 0.0))).astype(BF16)
        for p in range(4):
            low[p, :, off:off + 128] = flat[:, p * 128:(p + 1) * 128]
            low[p, :, off + 128:off + 256] = shift

        def one_pair(p, c):
            y = dot(low[p, :, off:off + 256], r.rx[p])
            y = jnp.exp2(y * ALPHA).astype(BF16)
            phi[2 * p] = y[:, 0:256]
            phi[2 * p + 1] = y[:, 256:512]
            return c

        lax.fori_loop(0, 4, one_pair, 0)

    loads["wk"].wait()
    features(1, r.xb, r.kT, r.phik, 0, live)
    loads["wv"].wait()
    vT = dot(r.nb[...], r.wqkv[2]).astype(BF16).T
    for h in range(H):
        r.vext[h, 0:64] = vT[h * 64:(h + 1) * 64]
        r.vext[h, 64:80] = jnp.where(row16 == 0, 1.0, 0.0).astype(BF16)

    def put_slab(h, lhs, phi):
        s = dot(lhs, phi)
        row = iota((8, M), 0)
        tail = jnp.where(row == 2, doc_f, jnp.where(row == 3, doc_l, s[128:136]))
        for half in range(2):
            r.out[2 * h + half, 0:128] = s[0:128, half * 128:(half + 1) * 128]
            r.out[2 * h + half, 128:136] = tail[:, half * 128:(half + 1) * 128]

    def take_slab(h, sb):
        for half in range(2):
            lanes = pl.ds(half * 128, 128)
            sb[h, 0:128, lanes] = r.got[2 * h + half, 0:128].astype(BF16)
            sb[h, 128:144, lanes] = jnp.concatenate(
                [r.got[2 * h + half, 128:136], jnp.zeros((8, 128), F32)], axis=0).astype(BF16)

    def value_ends(h):
        return ends(r.vext[h, 0:64].astype(F32), one_f, one_l)

    head_loop(lambda h: put_slab(h, value_ends(h), r.phik[h]))
    pl.semaphore_wait(barrier, 22)
    exchange = Exchange(r, 0, pack, seq)
    exchange.begin()
    load("wo", wo_h, r.wo)
    load("cot", cot_h, r.cot)
    for j in range(4):
        pltpu.make_async_copy(wup_h.at[:, pl.ds(j * 512, 512)], r.wup.at[j], r.load.at[7]).start()
        pltpu.make_async_copy(wdown_h.at[pl.ds(j * 512, 512)], r.wdown.at[j], r.load.at[8]).start()

    r.nT[...] = r.nb[...].T
    loads["wq"].wait()
    features(0, r.xb, r.qT, r.phiq, 256, None)
    exchange.turn()

    def same(block):
        return jnp.where(r.dcol[...] == doc, block, 0.0).astype(BF16)

    def attend(h):
        local = dot_nt(r.vext[h], same(dot_nt(r.phiq[h], r.phik[h])))
        r.num[h] = local[0:64]
        r.den[h] = local[64:72]

    head_loop(attend)
    exchange.wait()

    def join(h):
        take_slab(h, r.sb1)
        far = dot_nt(r.sb1[h], r.phiq[h])
        num = r.num[h] + jnp.where(in_f, far[0:64], 0.0) + jnp.where(in_l, far[64:128], 0.0)
        den = r.den[h, 0:1] + jnp.where(in_f, far[128:129], 0.0) + jnp.where(in_l, far[129:130], 0.0)
        inv = 1.0 / den
        att = num * inv
        r.num[h] = att
        r.den[h, 0:1] = inv
        r.attT[pl.ds(pl.multiple_of(h * 64, 64), 64)] = att.astype(BF16)

    head_loop(join)
    r.att[...] = r.attT[...].T
    loads["wo"].wait()
    r.mid[...] = dot(r.att[...], r.wo[...])

    def second_norm(rows, c):
        mid = r.x[rows, :].astype(F32) + r.mid[rows, :]
        r.mid[rows, :] = mid
        n, _ = layer_norm(mid)
        r.hid[rows, :] = (n * gf_ref[...]).astype(BF16)
        return c

    row_loop(64, second_norm)

    loads["cot"].wait()
    pltpu.make_async_copy(r.wup, r.wup, r.load.at[7]).wait()
    pltpu.make_async_copy(r.wdown, r.wdown, r.load.at[8]).wait()

    def feed(j, c):
        r.acc[...] = dot(r.hid[...], r.wup[j])
        r.acc2[...] = dot_nt(r.cot[...], r.wdown[j])

        def gelu(rows, c):
            u = r.acc[rows, :]
            ga = r.acc2[rows, :].astype(BF16).astype(F32)
            sq = u * u
            t = jnp.tanh(u * (GELU_A + GELU_A * GELU_B * sq))
            half = 0.5 * (1.0 + t)
            slope = half + 0.5 * u * (1.0 - t * t) * (GELU_A + 3.0 * GELU_A * GELU_B * sq)
            r.xb[j, rows, :] = (u * half).astype(BF16)
            r.gup[j, rows, :] = (ga * slope).astype(BF16)
            return c

        row_loop(16, gelu)
        back = dot_nt(r.gup[j], r.wup[j])

        r.gmid[...] = back if j == 0 else r.gmid[...] + back
        r.g[ROW_DOWN + j * 512:ROW_DOWN + (j + 1) * 512, :] = dot_tn(r.xb[j], r.cot[...])
        return c

    X, Y, Z = 0, 1, 2
    early = [
        Part(r, where, k, ROW_DOWN + 512 * k, 512, axes, ("o", "ic"), ("ic", "o"))
        for k, axes in enumerate(((X, Y, Z), (Y, Z, X), (Z, X, Y), (Z, Y, X)))
    ]
    up = [
        Part(r, where, 4, ROW_UP, 1024, (X, Y, Z), ("c", "oi"), ("oi", "c")),
        Part(r, where, 5, ROW_UP + 1024, 512, (X, Y, Z), ("c", "oi"), ("ic", "o")),
        Part(r, where, 6, ROW_UP + 1536, 512, (Y, X, Z), ("c", "oi"), ("ic", "o")),
    ]
    branch = Part(r, where, 7, ROW_O, 512, (Z, X, Y), ("o", "ic"), ("ic", "o"))
    last = [
        Part(r, where, 8, ROW_Q, 512, (X, Y, Z), ("o", "ic"), ("ic", "o")),
        Part(r, where, 9, ROW_Q + 512, 512, (Y, Z, X), ("o", "ic"), ("ic", "o")),
        Part(r, where, 10, ROW_Q + 1024, 512, (Z, X, Y), ("o", "ic"), ("ic", "o")),
    ]

    for j in range(4):
        feed(j, 0)
        tick(*early[max(j - 1, 0):j + 1])

    def add_gain(which, p):
        total = r.gain_sum[which]
        for i in range(8):
            total = total + p[i * 8:(i + 1) * 8]
        r.gain_sum[which] = total

    r.gain_sum[...] = jnp.zeros((2, 8, D), F32)

    def second_back(rows, c):
        gh = r.gmid[rows, :].astype(BF16).astype(F32)
        n, scale = layer_norm(r.mid[rows, :])
        gm = r.cot[rows, :].astype(F32) + norm_back(n, scale, gh * gf_ref[...])
        r.gmid[rows, :] = gm
        r.gb[rows, :] = gm.astype(BF16)
        add_gain(1, gh * n)
        return c

    row_loop(64, second_back)
    tick(early[3])
    r.acc[...] = dot_nt(r.wo[...], r.gb[...])

    def gates(h):
        ga = r.acc[pl.ds(pl.multiple_of(h * 64, 64), 64)].astype(BF16).astype(F32)
        inv = r.den[h, 0:1]
        gn = (ga * inv).astype(BF16)
        gd = -jnp.sum(ga * r.num[h], axis=0, keepdims=True) * inv
        r.gext[h, 0:64] = gn
        r.gext[h, 64:80] = jnp.where(row16 == 0, gd, 0.0).astype(BF16)
        put_slab(h, grad_ends(h), r.phiq[h])

    def grad_ends(h):
        gd = r.gext[h, 64:80].astype(F32)[0:1]
        return ends(r.gext[h, 0:64].astype(F32), one_f * gd, one_l * gd)

    head_loop(gates)
    exchange = Exchange(r, 1, pack, seq)
    exchange.begin()

    def block(row, value):
        r.g[row:row + 512, :] = value

    r.hidT[...] = r.hid[...].T
    for j in range(4):
        block(ROW_UP + j * 512, dot(r.hidT[...], r.gup[j]))
    block(ROW_O, dot(r.attT[...], r.gb[...]))
    tick(*up, branch)

    def map_back(h, gphi, phi, flat, which):
        p = (gphi.astype(BF16).astype(F32) * phi.astype(F32)).astype(BF16)
        through = dot_nt(r.r80[h], p)
        rows = pl.ds(pl.multiple_of(h * 64, 64), 64)
        r.gT[which, rows] = (C * through[0:64] - (C * C) * through[64:65] * flat[rows].astype(F32)).astype(BF16)

    def query_back(h):
        gphi = dot(same(dot_tn(r.gext[h], r.vext[h])), r.phik[h]) + dot_tn(grad_ends(h), r.sb1[h])
        map_back(h, gphi, r.phiq[h], r.qT, 0)
        r.acc2[pl.ds(pl.multiple_of(h * 64, 64), 64)] = dot(r.gext[h, 0:64], same(dot_nt(r.phiq[h], r.phik[h])))

    head_loop(query_back, 0, 3)
    tick(*up, branch)
    head_loop(query_back, 3, 8)
    exchange.turn()
    tick(*early)
    block(ROW_Q, dot_nt(r.nT[...], r.gT[0]))
    r.acc[...] = dot(r.xb[0], r.wdown[0])
    for j in range(1, 4):
        r.acc[...] += dot(r.xb[j], r.wdown[j])

    def put_out(rows, c):
        r.obf[rows, :] = (r.mid[rows, :] + r.acc[rows, :]).astype(BF16)
        return c

    row_loop(64, put_out)

    def key_local(h):
        gphi = dot(same(dot_tn(r.vext[h], r.gext[h])), r.phiq[h]).astype(BF16)
        r.xb[h // 2, :, pl.ds(pl.multiple_of(h % 2 * 256, 256), 256)] = gphi

    head_loop(key_local)
    exchange.wait()
    tick(*early)

    def key_back(h):
        take_slab(h, r.sb2)
        gphi = r.xb[h // 2, :, pl.ds(pl.multiple_of(h % 2 * 256, 256), 256)].astype(F32) + dot_tn(value_ends(h), r.sb2[h])
        map_back(h, gphi, r.phik[h], r.kT, 1)
        far = dot_nt(r.sb2[h, 0:128], r.phik[h])
        rows = pl.ds(pl.multiple_of(h * 64, 64), 64)
        r.gT[2, rows] = (r.acc2[rows] + jnp.where(in_f, far[0:64], 0.0) + jnp.where(in_l, far[64:128], 0.0)).astype(BF16)

    head_loop(key_back, 0, 4)
    tick(*up)
    head_loop(key_back, 4, 8)
    block(ROW_K, dot_nt(r.nT[...], r.gT[1]))
    block(ROW_V, dot_nt(r.nT[...], r.gT[2]))
    tick(*last)
    r.acc2[...] = dot(r.wqkv[0], r.gT[0])

    def normed_back(i, c):
        r.acc2[...] += dot(r.wqkv[i], r.gT[i])
        return c

    lax.fori_loop(1, 3, normed_back, 0)
    r.acc[...] = r.acc2[...].T
    tick(*last)
    tick(*early, *up, branch)

    def first_back(rows, c):
        gn = r.acc[rows, :].astype(BF16).astype(F32)
        n, scale = layer_norm(r.x[rows, :].astype(F32))
        r.gibf[rows, :] = (r.gmid[rows, :] + norm_back(n, scale, gn * ga_ref[...])).astype(BF16)
        add_gain(0, gn * n)
        return c

    row_loop(64, first_back)
    for which in range(2):
        total = r.gain_sum[which, 0:1]
        for i in range(1, 8):
            total = total + r.gain_sum[which, i:i + 1]
        for j in range(4):
            r.gain_here[4 * which + j:4 * which + j + 1] = total[:, j * 128:(j + 1) * 128]
    gains = Gains(r, pack, seq)
    gains.begin()
    tick(*last)
    tick(*up, branch)
    tick(*last)
    tick(*early, branch)
    gains.turn()
    tick(*last)
    tick(*up)
    tick(*last)
    for part in early + up + [branch] + last:
        while part.step <= part.last:
            part.tick()
    total = gains.end()
    for j in range(4):
        gain_ref[0:1, j * 128:(j + 1) * 128] = total[j:j + 1]
        gain_ref[1:2, j * 128:(j + 1) * 128] = total[4 + j:5 + j]


def store_kernel(out, gin, g, gain, out_h, gin_h, gwq_h, gwk_h, gwv_h, gwo_h, gwup_h, gwdown_h, gga_h, ggf_h, sems):
    pieces = [(g.at[pl.ds(ROW_DOWN, FF)], gwdown_h)]
    pieces += [(g.at[pl.ds(ROW_UP + j * 512, 512)], gwup_h.at[:, pl.ds(j * 512, 512)]) for j in range(4)]
    pieces += [(g.at[pl.ds(row, 512)], dst) for row, dst in ((ROW_O, gwo_h), (ROW_Q, gwq_h), (ROW_K, gwk_h), (ROW_V, gwv_h))]
    pieces += [(out, out_h), (gin, gin_h), (gain.at[pl.ds(0, 1)], gga_h), (gain.at[pl.ds(1, 1)], ggf_h)]
    copies = [pltpu.make_async_copy(src, dst, sems.at[i]) for i, (src, dst) in enumerate(pieces)]
    for copy in copies:
        copy.start()
    for copy in copies:
        copy.wait()


def per_device(
    inputs, w_query, w_key, w_value, w_output, w_up, w_down, gain_attn, gain_ffn, random_features, doc_ids, live_rows, cotangent):
    hbm = pl.BlockSpec(memory_space=pltpu.HBM)
    vmem = pl.BlockSpec(memory_space=pltpu.VMEM)
    f32 = lambda *shape: jax.ShapeDtypeStruct(shape, F32)
    low = jax.ShapeDtypeStruct((T, D), BF16)
    held = pl.pallas_call(
        kernel,
        out_shape=(pltpu.VMEM((T, D), BF16), pltpu.VMEM((T, D), BF16), pltpu.VMEM((6144, 512), F32), pltpu.VMEM((8, D), F32)),
        in_specs=[hbm] * 9 + [vmem] * 4,
        out_specs=(vmem,) * 4,
        scratch_shapes=[pltpu.VMEM(shape, dtype) for _, shape, dtype in SCRATCH] + [sem for _, sem in SEMS],
        compiler_params=pltpu.CompilerParams(collective_id=0, has_side_effects=True, vmem_limit_bytes=VMEM_LIMIT),
    )(
        *[pltpu.with_memory_space_constraint(v, pltpu.HBM) for v in (
            inputs[0], w_query, w_key, w_value, w_output, w_up, w_down, random_features, cotangent[0])],
        gain_attn[None], gain_ffn[None], doc_ids, live_rows)
    outs = pl.pallas_call(
        store_kernel,
        out_shape=(low, low, f32(D, D), f32(D, D), f32(D, D), f32(D, D), f32(D, FF), f32(FF, D), f32(1, D), f32(1, D)),
        in_specs=[vmem] * 4,
        out_specs=(hbm,) * 10,
        scratch_shapes=[pltpu.SemaphoreType.DMA((13,))],
        compiler_params=pltpu.CompilerParams(vmem_limit_bytes=1 * 2**20),
    )(*held)
    return (outs[0][None], outs[1][None]) + tuple(outs[2:8]) + (outs[8][0], outs[9][0])


def solution(mesh):
    rows = P("pack", "seq", None)
    return jax.shard_map(
        per_device,
        mesh=mesh,
        in_specs=(rows,) + (P(),) * 9 + (P("pack", "seq"), P("pack", "seq"), rows),
        out_specs=(rows, rows) + (P(),) * 8,
        check_vma=False,
    )
```

```python
import functools
import math

import jax
import jax.numpy as jnp
from jax import lax
from jax.experimental import pallas as pl
from jax.experimental.pallas import tpu as pltpu
from jax.sharding import PartitionSpec as P

MESH = pl.DeviceIdType.MESH
F32, BF16 = jnp.float32, jnp.bfloat16
T, D, H, DH, M, FF = 512, 512, 8, 64, 256, 2048
SLAB = 136
EPS = 1e-05
VMEM_LIMIT = 47 * 2**20
C = DH ** -0.25
ALPHA = C * math.log2(math.e)
GELU_A, GELU_B = math.sqrt(2.0 / math.pi), 0.044715


def dot(a, b):
    return lax.dot_general(a, b, (((1,), (0,)), ((), ())), preferred_element_type=F32)


def dot_nt(a, b):
    return lax.dot_general(a, b, (((1,), (1,)), ((), ())), preferred_element_type=F32)


def dot_tn(a, b):
    return lax.dot_general(a, b, (((0,), (0,)), ((), ())), preferred_element_type=F32)


def iota(shape, dim):
    return lax.broadcasted_iota(jnp.int32, shape, dim)


def place():
    pack, seq = lax.axis_index("pack"), lax.axis_index("seq")
    return pack >> 1, pack & 1, seq >> 2, seq & 3


def layer_norm(v):
    centred = v - jnp.mean(v, axis=-1, keepdims=True)
    scale = lax.rsqrt(jnp.mean(centred * centred, axis=-1, keepdims=True) + EPS)
    return centred * scale, scale


def norm_back(n, scale, e):
    return scale * (e - jnp.mean(e, axis=-1, keepdims=True) - n * jnp.mean(e * n, axis=-1, keepdims=True))


def row_loop(step, body, carry=0):
    def run(i, c):
        return body(pl.ds(pl.multiple_of(i * step, step), step), c)

    return lax.fori_loop(0, T // step, run, carry)


def head_loop(body, start=0, stop=H):
    def run(h, c):
        body(h)
        return c

    lax.fori_loop(start, stop, run, 0)


def wait_all(like, send_sem, recv_sem, dev):
    pltpu.make_async_remote_copy(
        src_ref=like, dst_ref=like, send_sem=send_sem, recv_sem=recv_sem, device_id=dev, device_id_type=MESH).wait()


class Part:
    def __init__(self, r, where, number, row, rows, axes, down, up):
        self.r, self.where, self.row, self.n = r, where, row, rows // 2
        self.axes = dict(zip("oic", axes))
        self.down, self.up = down, up
        self.number = number
        self.at = row + where[1] * self.n
        self.buf = row // 2
        self.step, self.last = -1, len(down) + len(up) + 1
        self.flying, self.held, self.freed = 0, {}, set()

    def mine(self, role):
        z, core, x, y = self.where
        return (x, y, z)[self.axes[role]]

    def peers(self, roles):
        z, core, x, y = self.where
        out = []
        for far in range(1, 4 ** len(roles)):
            at = {role: (self.mine(role) + far // 4 ** k) & 3 for k, role in enumerate(roles)}
            spot = [x, y, z]
            for role, there in at.items():
                spot[self.axes[role]] = there
            out.append((at, (spot[2] * 2 + core, spot[0] * 4 + spot[1])))
        return out

    def behind(self, roles, d):
        return {role: (self.mine(role) - (d + 1) // 4 ** k) & 3 for k, role in enumerate(roles)}

    def sibling(self):
        z, core, x, y = self.where
        return (z * 2 + 1 - core, x * 4 + y)

    def block(self, at={}):
        at = {**self.held, **at}
        row, rows, lane, lanes = self.at, self.n, 0, 512
        if "o" in at:
            row, rows = row + at["o"] * (self.n // 4), self.n // 4
        if "i" in at:
            row, rows = row + at["i"] * (self.n // 16), self.n // 16
        if "c" in at:
            lane, lanes = pl.multiple_of(at["c"] * 128, 128), 128
        return row, rows, lane, lanes

    def view(self, block):
        row, rows, lane, lanes = block
        return self.r.g.at[pl.ds(pl.multiple_of(row, 8), rows), pl.ds(lane, lanes)]

    def landing(self, roles, d):
        n = self.n
        row, lane = {
            "o": (d * (n // 4), 0),
            "ic": (3 * n // 4 + d // 4 * (n // 16), d % 4 * 128),
            "c": (0, d * 128),
            "oi": (d * (n // 16), 384),
        }[roles]
        return self.buf + row, lane

    def send(self, src, dst, dev):
        pltpu.make_async_remote_copy(
            src_ref=src, dst_ref=dst, send_sem=self.r.ssem.at[self.number], recv_sem=self.r.rsem.at[self.number, self.step],
            device_id=dev, device_id_type=MESH).start()
        self.flying += 1
        self.piece = src.shape

    def add(self, block, buf, slots):
        r = self.r
        row, rows, lane, lanes = block
        step = min(16384 // lanes, rows)

        def body(i, c):
            at = pl.ds(pl.multiple_of(row + i * step, 8), step)
            total = r.g[at, pl.ds(lane, lanes)]
            for slot, column in slots:
                total = total + buf[pl.ds(pl.multiple_of(slot + i * step, 8), step), pl.ds(column, lanes)]
            r.g[at, pl.ds(lane, lanes)] = total
            return c

        lax.fori_loop(0, rows // step, body, 0)

    def finish(self):
        r, s, downs = self.r, self.step, len(self.down)
        if self.flying:
            rows, lanes = self.piece
            wait_all(r.from_chip.at[pl.ds(0, self.flying * rows), pl.ds(0, lanes)], r.ssem.at[self.number], r.rsem.at[self.number, s], self.sibling())
        self.flying = 0
        if s == 0:
            pl.semaphore_signal(r.free.at[self.number, 0], inc=1, device_id=self.sibling(), device_id_type=MESH)
            self.add(self.block(), r.from_core, [(self.buf, 0)])
        elif 1 <= s <= downs:
            roles = self.down[s - 1]
            self.held.update({role: self.mine(role) for role in roles})
            for k in range(1, len(self.up)):
                if k not in self.freed and set(self.up[k]) <= set(self.held):
                    self.freed.add(k)
                    for _, dev in self.peers(self.up[k]):
                        pl.semaphore_signal(r.free.at[self.number, k], inc=1, device_id=dev, device_id_type=MESH)
            self.add(self.block(), r.from_chip, [self.landing(roles, d) for d in range(4 ** len(roles) - 1)])
        elif downs < s < self.last:
            roles = self.up[s - downs - 1]
            if s == downs + 1:
                for d in range(4 ** len(roles) - 1):
                    row, rows, lane, lanes = self.block(self.behind(roles, d))
                    r.g[pl.ds(pl.multiple_of(row, 8), rows), pl.ds(lane, lanes)] = r.turn[d, pl.ds(self.buf // 16, rows)]
            for role in roles:
                del self.held[role]

    def start(self):
        r, n, downs = self.r, self.n, len(self.down)
        self.step = s = self.step + 1
        if s == 0:
            core = self.where[1]
            self.send(r.g.at[pl.ds(pl.multiple_of(self.row + (1 - core) * n, 8), n)], r.from_core.at[pl.ds(self.buf, n)], self.sibling())
        elif 1 <= s <= downs:
            roles = self.down[s - 1]
            for d, (at, dev) in enumerate(self.peers(roles)):
                block = self.block(at)
                row, lane = self.landing(roles, d)
                self.send(self.view(block), r.from_chip.at[pl.ds(row, block[1]), pl.ds(lane, block[3])], dev)
        elif downs < s < self.last:
            k = s - downs - 1
            roles = self.up[k]
            block = self.block()
            part = self.view(block)
            peers = self.peers(roles)
            if k > 0:
                pl.semaphore_wait(r.free.at[self.number, k], len(peers))
            for d, (at, dev) in enumerate(peers):
                self.send(part, part if k > 0 else r.turn.at[d, pl.ds(self.buf // 16, block[1])], dev)
        elif s == self.last:
            part = self.view(self.block())
            pl.semaphore_wait(r.free.at[self.number, 0], 1)
            self.send(part, part, self.sibling())

    def tick(self):
        if self.step <= self.last:
            self.finish()
            self.start()


def tick(*parts):
    for part in parts:
        part.tick()


class Exchange:
    PIECES = (pl.ds(64, SLAB - 64), pl.ds(0, 64))

    def __init__(self, r, which, pack, seq):
        self.r, self.sems, self.pack, self.seq = r, r.esem.at[which], pack, seq

    def send(self, src, dst, way, piece):
        rows = self.PIECES[piece]
        for step in range(1, 16):
            peer = (self.seq + step) & 15
            pltpu.make_async_remote_copy(
                src_ref=src.at[peer, rows], dst_ref=dst.at[self.seq, rows], send_sem=self.sems.at[4 + piece],
                recv_sem=self.sems.at[2 * way + piece], device_id=(self.pack, peer), device_id_type=MESH).start()
        dst[self.seq, rows] = src[self.seq, rows]

    def wait_piece(self, way, piece):
        wait_all(
            self.r.arrived.at[pl.ds(0, 15), self.PIECES[piece]], self.sems.at[4 + piece], self.sems.at[2 * way + piece],
            (self.pack, (self.seq + 1) & 15))

    def wait(self):
        self.wait_piece(1, 0)
        self.wait_piece(1, 1)

    def begin(self):
        self.send(self.r.out, self.r.arrived, 0, 0)
        self.send(self.r.out, self.r.arrived, 0, 1)

    def turn(self):
        arrived, back = self.r.arrived, self.r.back
        none, small_none = jnp.zeros((64, 128), F32), jnp.zeros((1, 128), F32)

        def left(dev, carry):
            total, small = carry
            tail, mine = arrived[dev - 1, 128:136], arrived[dev, 128:136]
            whole, joins = tail[2:3] == tail[3:4], tail[3:4] == mine[2:3]
            total = jnp.where(joins, arrived[dev - 1, 64:128] + jnp.where(whole, total, 0.0), 0.0)
            small = jnp.where(joins, tail[1:2] + jnp.where(whole, small, 0.0), 0.0)
            back[dev, 64:128] = total
            back[dev, 128:129] = small
            return total, small

        def right_small(i, small):
            dev = 14 - i
            tail, mine = arrived[dev + 1, 128:136], arrived[dev, 128:136]
            whole, joins = tail[2:3] == tail[3:4], mine[3:4] == tail[2:3]
            small = jnp.where(joins, tail[0:1] + jnp.where(whole, small, 0.0), 0.0)
            back[dev, 129:130] = small
            return small

        def right(i, total):
            dev = 14 - i
            tail, mine = arrived[dev + 1, 128:136], arrived[dev, 128:136]
            whole, joins = tail[2:3] == tail[3:4], mine[3:4] == tail[2:3]
            total = jnp.where(joins, arrived[dev + 1, 0:64] + jnp.where(whole, total, 0.0), 0.0)
            back[dev, 0:64] = total
            return total

        self.wait_piece(0, 0)
        for dev in range(16):
            back[dev, 128:136] = jnp.zeros((8, 128), F32)
        back[0, 64:128] = none
        lax.fori_loop(1, 16, left, (none, small_none))
        lax.fori_loop(0, 15, right_small, small_none)
        self.send(back, self.r.got, 1, 0)
        self.wait_piece(0, 1)
        back[15, 0:64] = none
        lax.fori_loop(0, 15, right, none)
        self.send(back, self.r.got, 1, 1)


class Gains:
    def __init__(self, r, pack, seq):
        self.r, self.pack, self.seq = r, pack, seq

    def send(self, src, dst, way, size):
        for step in range(1, size):
            dev = ((self.pack + step) & 7, self.seq) if way == 0 else (self.pack, (self.seq + step) & 15)
            pltpu.make_async_remote_copy(
                src_ref=src, dst_ref=dst.at[step - 1], send_sem=self.r.gsem.at[2], recv_sem=self.r.gsem.at[way],
                device_id=dev, device_id_type=MESH).start()

    def wait(self, like, way):
        wait_all(like, self.r.gsem.at[2], self.r.gsem.at[way], (self.pack, (self.seq + 1) & 15))

    def begin(self):
        self.send(self.r.gain_here, self.r.gain_pack, 0, 8)

    def turn(self):
        self.wait(self.r.gain_pack, 0)
        total = self.r.gain_here[...]
        for i in range(7):
            total = total + self.r.gain_pack[i]
        self.r.gain_mid[...] = total
        self.send(self.r.gain_mid, self.r.gain_seq, 1, 16)

    def end(self):
        self.wait(self.r.gain_seq, 1)
        total = self.r.gain_mid[...]
        for i in range(15):
            total = total + self.r.gain_seq[i]
        return total


class Refs:
    pass


SCRATCH = [
    ("x", (T, D), BF16), ("cot", (T, D), BF16),
    ("wqkv", (3, D, D), BF16), ("wo", (D, D), BF16),
    ("wup", (4, D, 512), BF16), ("wdown", (4, 512, D), BF16), ("rf", (H, DH, M), BF16),
    ("rx", (4, 256, 512), BF16), ("r80", (H, 80, M), BF16),
    ("nb", (T, D), BF16), ("nT", (D, T), BF16), ("qT", (D, T), BF16), ("kT", (D, T), BF16),
    ("xb", (4, T, 512), BF16),
    ("gup", (4, T, 512), BF16),
    ("vext", (H, 80, T), BF16), ("gext", (H, 80, T), BF16),
    ("phik", (H, T, M), BF16), ("phiq", (H, T, M), BF16),
    ("dcol", (T, T), F32),
    ("num", (H, DH, T), F32), ("den", (H, 8, T), F32),
    ("attT", (D, T), BF16), ("att", (T, D), BF16), ("mid", (T, D), F32), ("hid", (T, D), BF16),
    ("acc", (T, D), F32), ("acc2", (T, D), F32), ("gmid", (T, D), F32),
    ("sb1", (H, 144, M), BF16), ("sb2", (H, 144, M), BF16),
            ("out", (16, SLAB, 128), F32), ("arrived", (16, SLAB, 128), F32), ("got", (16, SLAB, 128), F32),
    ("from_core", (3072, 512), F32), ("from_chip", (3072, 512), F32), ("turn", (15, 192, 128), F32),
    ("gain_sum", (2, 8, D), F32), ("gain_here", (8, 128), F32), ("gain_pack", (7, 8, 128), F32), ("gain_mid", (8, 128), F32), ("gain_seq", (15, 8, 128), F32),
]
SEMS = [
    ("load", pltpu.SemaphoreType.DMA((9,))), ("esem", pltpu.SemaphoreType.DMA((2, 6))), ("gsem", pltpu.SemaphoreType.DMA((3,))),
    ("ssem", pltpu.SemaphoreType.DMA((11,))), ("rsem", pltpu.SemaphoreType.DMA((11, 6))), ("free", pltpu.SemaphoreType.REGULAR((11, 2))),
]
ROW_DOWN, ROW_UP, ROW_O, ROW_Q, ROW_K, ROW_V = 0, 2048, 4096, 4608, 5120, 5632


def kernel(
    x_h, wq_h, wk_h, wv_h, wo_h, wup_h, wdown_h, rf_h, cot_h, ga_ref, gf_ref, doc_ref, live_ref,
    obf, gibf, g, gain_ref, *scratch):
    r = Refs()
    r.obf, r.gibf, r.g = obf, gibf, g
    for (name, *_), ref in zip(SCRATCH + SEMS, scratch):
        setattr(r, name, ref)
    r.gb, r.hidT, r.gT, r.back = r.nb, r.att, r.gup, r.out
    where = place()
    z, core, px, py = where
    pack, seq = lax.axis_index("pack"), lax.axis_index("seq")

    loads = {}

    def load(name, src, dst):
        copy = pltpu.make_async_copy(src, dst, r.load.at[len(loads)])
        copy.start()
        loads[name] = copy

    load("x", x_h, r.x)
    load("wk", wk_h, r.wqkv.at[1])
    load("rf", rf_h, r.rf)
    load("wv", wv_h, r.wqkv.at[2])
    load("wq", wq_h, r.wqkv.at[0])
    barrier = pltpu.get_barrier_semaphore()
    for step in range(1, 16):
        pl.semaphore_signal(barrier, inc=1, device_id=(pack, (seq + step) & 15), device_id_type=MESH)
    for step in range(1, 8):
        pl.semaphore_signal(barrier, inc=1, device_id=((pack + step) & 7, seq), device_id_type=MESH)

    doc = doc_ref[...].astype(F32)
    doc_f, doc_l = doc[:, 0:1], doc[:, T - 1:T]
    in_f, in_l = doc == doc_f, doc == doc_l
    one_f, one_l = in_f.astype(F32), in_l.astype(F32)
    row16 = iota((16, T), 0)

    def ends(block, tail_f, tail_l):
        zero = jnp.zeros_like(block)
        tail = jnp.where(row16 == 0, tail_f, jnp.where(row16 == 1, tail_l, 0.0))
        return jnp.concatenate(
            [jnp.where(in_f, block, zero).astype(BF16), jnp.where(in_l, block, zero).astype(BF16), tail.astype(BF16)], axis=0)

    dcol = jnp.broadcast_to(doc, (128, T)).T
    for j in range(4):
        r.dcol[:, j * 128:(j + 1) * 128] = dcol
    live = jnp.broadcast_to(live_ref[...].astype(F32), (128, T)).T

    loads["x"].wait()

    def first_norm(rows, c):
        n, _ = layer_norm(r.x[rows, :].astype(F32))
        r.nb[rows, :] = (n * ga_ref[...]).astype(BF16)
        return c

    row_loop(64, first_norm)
    loads["rf"].wait()
    for p in range(4):
        lane, row = iota((256, 512), 1) // 256, iota((256, 512), 0)
        pick = (row >= 128) & (row < 152) & (row % 8 == 2 * p + lane)
        r.rx[p] = jnp.where(pick, 1.0, 0.0).astype(BF16)
        r.rx[p, 0:64, 0:256] = r.rf[2 * p]
        r.rx[p, 64:128, 256:512] = r.rf[2 * p + 1]
    for h in range(H):
        r.r80[h, 0:64] = r.rf[h]
        r.r80[h, 64:80] = jnp.where(iota((16, M), 0) == 0, 1.0, 0.0).astype(BF16)
    pick_heads = ((iota((D, 128), 1) % 8 == iota((D, 128), 0) // DH) & (iota((D, 128), 1) < 24)).astype(BF16)

    def features(w, low, transposed, phi, off, alive):
        flat = dot(r.nb[...], r.wqkv[w]).astype(BF16)
        transposed[...] = flat.T
        square = flat.astype(F32)
        square = square * square
        high = square.astype(BF16)
        rest = (square - high.astype(F32)).astype(BF16)
        size = dot(high, pick_heads) + dot(rest, pick_heads)
        shift = size * (-0.5 * C) - 4.0 / ALPHA
        if alive is not None:
            shift = shift + (alive - 1.0) * 1e30
        first = shift.astype(BF16).astype(F32)
        second = (shift - first).astype(BF16).astype(F32)
        third = shift - first - second
        at = iota((T, 128), 1)
        shift = jnp.where(at < 8, first, jnp.where(at < 16, second, jnp.where(at < 24, third, 0.0))).astype(BF16)
        for p in range(4):
            low[p, :, off:off + 128] = flat[:, p * 128:(p + 1) * 128]
            low[p, :, off + 128:off + 256] = shift

        def one_pair(p, c):
            y = dot(low[p, :, off:off + 256], r.rx[p])
            y = jnp.exp2(y * ALPHA).astype(BF16)
            phi[2 * p] = y[:, 0:256]
            phi[2 * p + 1] = y[:, 256:512]
            return c

        lax.fori_loop(0, 4, one_pair, 0)

    loads["wk"].wait()
    features(1, r.xb, r.kT, r.phik, 0, live)
    loads["wv"].wait()
    vT = dot(r.nb[...], r.wqkv[2]).astype(BF16).T
    for h in range(H):
        r.vext[h, 0:64] = vT[h * 64:(h + 1) * 64]
        r.vext[h, 64:80] = jnp.where(row16 == 0, 1.0, 0.0).astype(BF16)

    def put_slab(h, lhs, phi):
        s = dot(lhs, phi)
        row = iota((8, M), 0)
        tail = jnp.where(row == 2, doc_f, jnp.where(row == 3, doc_l, s[128:136]))
        for half in range(2):
            r.out[2 * h + half, 0:128] = s[0:128, half * 128:(half + 1) * 128]
            r.out[2 * h + half, 128:136] = tail[:, half * 128:(half + 1) * 128]

    def take_slab(h, sb):
        for half in range(2):
            lanes = pl.ds(half * 128, 128)
            sb[h, 0:64, lanes] = r.got[2 * h + half, 64:128].astype(BF16)
            sb[h, 64:128, lanes] = r.got[2 * h + half, 0:64].astype(BF16)
            sb[h, 128:144, lanes] = jnp.concatenate(
                [r.got[2 * h + half, 128:136], jnp.zeros((8, 128), F32)], axis=0).astype(BF16)

    def value_ends(h):
        return ends(r.vext[h, 0:64].astype(F32), one_f, one_l)

    head_loop(lambda h: put_slab(h, value_ends(h), r.phik[h]))
    pl.semaphore_wait(barrier, 22)
    exchange = Exchange(r, 0, pack, seq)
    exchange.begin()
    load("wo", wo_h, r.wo)
    load("cot", cot_h, r.cot)
    for j in range(4):
        pltpu.make_async_copy(wup_h.at[:, pl.ds(j * 512, 512)], r.wup.at[j], r.load.at[7]).start()
        pltpu.make_async_copy(wdown_h.at[pl.ds(j * 512, 512)], r.wdown.at[j], r.load.at[8]).start()

    r.nT[...] = r.nb[...].T
    loads["wq"].wait()
    features(0, r.xb, r.qT, r.phiq, 256, None)
    exchange.turn()

    def same(block):
        return jnp.where(r.dcol[...] == doc, block, 0.0).astype(BF16)

    def attend(h):
        local = dot_nt(r.vext[h], same(dot_nt(r.phiq[h], r.phik[h])))
        r.num[h] = local[0:64]
        r.den[h] = local[64:72]

    head_loop(attend)
    exchange.wait()

    def join(h):
        take_slab(h, r.sb1)
        far = dot_nt(r.sb1[h], r.phiq[h])
        num = r.num[h] + jnp.where(in_f, far[0:64], 0.0) + jnp.where(in_l, far[64:128], 0.0)
        den = r.den[h, 0:1] + jnp.where(in_f, far[128:129], 0.0) + jnp.where(in_l, far[129:130], 0.0)
        inv = 1.0 / den
        att = num * inv
        r.num[h] = att
        r.den[h, 0:1] = inv
        r.attT[pl.ds(pl.multiple_of(h * 64, 64), 64)] = att.astype(BF16)

    head_loop(join)
    r.att[...] = r.attT[...].T
    loads["wo"].wait()
    r.mid[...] = dot(r.att[...], r.wo[...])

    def second_norm(rows, c):
        mid = r.x[rows, :].astype(F32) + r.mid[rows, :]
        r.mid[rows, :] = mid
        n, _ = layer_norm(mid)
        r.hid[rows, :] = (n * gf_ref[...]).astype(BF16)
        return c

    row_loop(64, second_norm)

    loads["cot"].wait()
    pltpu.make_async_copy(r.wup, r.wup, r.load.at[7]).wait()
    pltpu.make_async_copy(r.wdown, r.wdown, r.load.at[8]).wait()

    def feed(j, c):
        r.acc[...] = dot(r.hid[...], r.wup[j])
        r.acc2[...] = dot_nt(r.cot[...], r.wdown[j])

        def gelu(rows, c):
            u = r.acc[rows, :]
            ga = r.acc2[rows, :].astype(BF16).astype(F32)
            sq = u * u
            t = jnp.tanh(u * (GELU_A + GELU_A * GELU_B * sq))
            half = 0.5 * (1.0 + t)
            slope = half + 0.5 * u * (1.0 - t * t) * (GELU_A + 3.0 * GELU_A * GELU_B * sq)
            r.xb[j, rows, :] = (u * half).astype(BF16)
            r.gup[j, rows, :] = (ga * slope).astype(BF16)
            return c

        row_loop(16, gelu)
        back = dot_nt(r.gup[j], r.wup[j])

        r.gmid[...] = back if j == 0 else r.gmid[...] + back
        block(ROW_DOWN + j * 512, dot_tn(r.xb[j], r.cot[...]))
        block(ROW_UP + j * 512, dot(r.hidT[...], r.gup[j]))
        return c

    X, Y, Z = 0, 1, 2
    early = [
        Part(r, where, k, ROW_DOWN + 512 * k, 512, axes, ("o", "ic"), ("ic", "o"))
        for k, axes in enumerate(((X, Y, Z), (Y, X, Z), (X, Y, Z), (Y, X, Z)))
    ]
    up = [
        Part(r, where, 4, ROW_UP, 1024, (X, Y, Z), ("c", "oi"), ("oi", "c")),
        Part(r, where, 5, ROW_UP + 1024, 512, (X, Y, Z), ("c", "oi"), ("ic", "o")),
        Part(r, where, 6, ROW_UP + 1536, 512, (Y, X, Z), ("c", "oi"), ("ic", "o")),
    ]
    branch = Part(r, where, 7, ROW_O, 512, (Z, X, Y), ("o", "ic"), ("ic", "o"))
    query = Part(r, where, 8, ROW_Q, 512, (Z, Y, X), ("o", "ic"), ("ic", "o"))
    last = [
        Part(r, where, 9, ROW_K, 512, (X, Y, Z), ("o", "ic"), ("ic", "o")),
        Part(r, where, 10, ROW_V, 512, (Y, X, Z), ("o", "ic"), ("ic", "o")),
    ]

    def block(row, value):
        r.g[row:row + 512, :] = value

    r.hidT[...] = r.hid[...].T
    for j, moves in enumerate((early[:1], early[:2] + up[:1], early[1:3] + up[:2], early[2:4] + up[1:3])):
        feed(j, 0)
        tick(*moves)

    def add_gain(which, p):
        total = r.gain_sum[which]
        for i in range(8):
            total = total + p[i * 8:(i + 1) * 8]
        r.gain_sum[which] = total

    r.gain_sum[...] = jnp.zeros((2, 8, D), F32)

    def second_back(rows, c):
        gh = r.gmid[rows, :].astype(BF16).astype(F32)
        n, scale = layer_norm(r.mid[rows, :])
        gm = r.cot[rows, :].astype(F32) + norm_back(n, scale, gh * gf_ref[...])
        r.gmid[rows, :] = gm
        r.gb[rows, :] = gm.astype(BF16)
        add_gain(1, gh * n)
        return c

    row_loop(64, second_back)
    tick(early[3], up[2])
    block(ROW_O, dot(r.attT[...], r.gb[...]))
    tick(branch)
    r.acc[...] = dot_nt(r.wo[...], r.gb[...])

    def gates(h):
        ga = r.acc[pl.ds(pl.multiple_of(h * 64, 64), 64)].astype(BF16).astype(F32)
        inv = r.den[h, 0:1]
        gn = (ga * inv).astype(BF16)
        gd = -jnp.sum(ga * r.num[h], axis=0, keepdims=True) * inv
        r.gext[h, 0:64] = gn
        r.gext[h, 64:80] = jnp.where(row16 == 0, gd, 0.0).astype(BF16)
        put_slab(h, grad_ends(h), r.phiq[h])

    def grad_ends(h):
        gd = r.gext[h, 64:80].astype(F32)[0:1]
        return ends(r.gext[h, 0:64].astype(F32), one_f * gd, one_l * gd)

    head_loop(gates)
    tick(branch)
    exchange = Exchange(r, 1, pack, seq)
    exchange.begin()

    def map_back(h, gphi, phi, flat, which):
        p = (gphi.astype(BF16).astype(F32) * phi.astype(F32)).astype(BF16)
        through = dot_nt(r.r80[h], p)
        rows = pl.ds(pl.multiple_of(h * 64, 64), 64)
        r.gT[which, rows] = (C * through[0:64] - (C * C) * through[64:65] * flat[rows].astype(F32)).astype(BF16)

    def query_back(h):
        gphi = dot(same(dot_tn(r.gext[h], r.vext[h])), r.phik[h]) + dot_tn(grad_ends(h), r.sb1[h])
        map_back(h, gphi, r.phiq[h], r.qT, 0)
        r.acc2[pl.ds(pl.multiple_of(h * 64, 64), 64)] = dot(r.gext[h, 0:64], same(dot_nt(r.phiq[h], r.phik[h])))

    head_loop(query_back)
    exchange.turn()
    tick(*early)
    block(ROW_Q, dot_nt(r.nT[...], r.gT[0]))
    tick(query)
    r.acc[...] = dot(r.xb[0], r.wdown[0])
    for j in range(1, 4):
        r.acc[...] += dot(r.xb[j], r.wdown[j])

    def put_out(rows, c):
        r.obf[rows, :] = (r.mid[rows, :] + r.acc[rows, :]).astype(BF16)
        return c

    row_loop(64, put_out)
    tick(query)

    def key_local(h):
        gphi = dot(same(dot_tn(r.vext[h], r.gext[h])), r.phiq[h]).astype(BF16)
        r.xb[h // 2, :, pl.ds(pl.multiple_of(h % 2 * 256, 256), 256)] = gphi

    head_loop(key_local)
    tick(*up, branch)
    exchange.wait()
    tick(*early, query)

    def key_back(h):
        take_slab(h, r.sb2)
        gphi = r.xb[h // 2, :, pl.ds(pl.multiple_of(h % 2 * 256, 256), 256)].astype(F32) + dot_tn(value_ends(h), r.sb2[h])
        map_back(h, gphi, r.phik[h], r.kT, 1)
        far = dot_nt(r.sb2[h, 0:128], r.phik[h])
        rows = pl.ds(pl.multiple_of(h * 64, 64), 64)
        r.gT[2, rows] = (r.acc2[rows] + jnp.where(in_f, far[0:64], 0.0) + jnp.where(in_l, far[64:128], 0.0)).astype(BF16)

    head_loop(key_back, 0, 4)
    tick(*up, branch)
    head_loop(key_back, 4, 8)
    block(ROW_K, dot_nt(r.nT[...], r.gT[1]))
    block(ROW_V, dot_nt(r.nT[...], r.gT[2]))
    tick(*last)
    tick(*early, query)
    r.acc2[...] = dot(r.wqkv[0], r.gT[0])

    def normed_back(i, c):
        r.acc2[...] += dot(r.wqkv[i], r.gT[i])
        return c

    lax.fori_loop(1, 3, normed_back, 0)
    r.acc[...] = r.acc2[...].T
    tick(*last)
    tick(*up, branch, query)

    def first_back(rows, c):
        gn = r.acc[rows, :].astype(BF16).astype(F32)
        n, scale = layer_norm(r.x[rows, :].astype(F32))
        r.gibf[rows, :] = (r.gmid[rows, :] + norm_back(n, scale, gn * ga_ref[...])).astype(BF16)
        add_gain(0, gn * n)
        return c

    row_loop(64, first_back)
    for which in range(2):
        total = r.gain_sum[which, 0:1]
        for i in range(1, 8):
            total = total + r.gain_sum[which, i:i + 1]
        for j in range(4):
            r.gain_here[4 * which + j:4 * which + j + 1] = total[:, j * 128:(j + 1) * 128]
    gains = Gains(r, pack, seq)
    gains.begin()
    tick(*last)
    tick(*early)
    tick(*last)
    gains.turn()
    tick(*last)
    tick(*up, branch, query)
    tick(*last)
    for part in early + up + [branch, query] + last:
        while part.step <= part.last:
            part.tick()
    total = gains.end()
    for j in range(4):
        gain_ref[0:1, j * 128:(j + 1) * 128] = total[j:j + 1]
        gain_ref[1:2, j * 128:(j + 1) * 128] = total[4 + j:5 + j]


def store_kernel(out, gin, g, gain, out_h, gin_h, gwq_h, gwk_h, gwv_h, gwo_h, gwup_h, gwdown_h, gga_h, ggf_h, sems):
    pieces = [(g.at[pl.ds(ROW_DOWN, FF)], gwdown_h)]
    pieces += [(g.at[pl.ds(ROW_UP + j * 512, 512)], gwup_h.at[:, pl.ds(j * 512, 512)]) for j in range(4)]
    pieces += [(g.at[pl.ds(row, 512)], dst) for row, dst in ((ROW_O, gwo_h), (ROW_Q, gwq_h), (ROW_K, gwk_h), (ROW_V, gwv_h))]
    pieces += [(out, out_h), (gin, gin_h), (gain.at[pl.ds(0, 1)], gga_h), (gain.at[pl.ds(1, 1)], ggf_h)]
    copies = [pltpu.make_async_copy(src, dst, sems.at[i]) for i, (src, dst) in enumerate(pieces)]
    for copy in copies:
        copy.start()
    for copy in copies:
        copy.wait()


def per_device(
    inputs, w_query, w_key, w_value, w_output, w_up, w_down, gain_attn, gain_ffn, random_features, doc_ids, live_rows, cotangent):
    hbm = pl.BlockSpec(memory_space=pltpu.HBM)
    vmem = pl.BlockSpec(memory_space=pltpu.VMEM)
    f32 = lambda *shape: jax.ShapeDtypeStruct(shape, F32)
    low = jax.ShapeDtypeStruct((T, D), BF16)
    held = pl.pallas_call(
        kernel,
        out_shape=(pltpu.VMEM((T, D), BF16), pltpu.VMEM((T, D), BF16), pltpu.VMEM((6144, 512), F32), pltpu.VMEM((8, D), F32)),
        in_specs=[hbm] * 9 + [vmem] * 4,
        out_specs=(vmem,) * 4,
        scratch_shapes=[pltpu.VMEM(shape, dtype) for _, shape, dtype in SCRATCH] + [sem for _, sem in SEMS],
        compiler_params=pltpu.CompilerParams(collective_id=0, has_side_effects=True, vmem_limit_bytes=VMEM_LIMIT),
    )(
        *[pltpu.with_memory_space_constraint(v, pltpu.HBM) for v in (
            inputs[0], w_query, w_key, w_value, w_output, w_up, w_down, random_features, cotangent[0])],
        gain_attn[None], gain_ffn[None], doc_ids, live_rows)
    outs = pl.pallas_call(
        store_kernel,
        out_shape=(low, low, f32(D, D), f32(D, D), f32(D, D), f32(D, D), f32(D, FF), f32(FF, D), f32(1, D), f32(1, D)),
        in_specs=[vmem] * 4,
        out_specs=(hbm,) * 10,
        scratch_shapes=[pltpu.SemaphoreType.DMA((13,))],
        compiler_params=pltpu.CompilerParams(vmem_limit_bytes=1 * 2**20),
    )(*held)
    return (outs[0][None], outs[1][None]) + tuple(outs[2:8]) + (outs[8][0], outs[9][0])


def solution(mesh):
    rows = P("pack", "seq", None)
    return jax.shard_map(
        per_device,
        mesh=mesh,
        in_specs=(rows,) + (P(),) * 9 + (P("pack", "seq"), P("pack", "seq"), rows),
        out_specs=(rows, rows) + (P(),) * 8,
        check_vma=False,
    )
```

```python
import functools
import math

import jax
import jax.numpy as jnp
from jax import lax
from jax.experimental import pallas as pl
from jax.experimental.pallas import tpu as pltpu
from jax.sharding import PartitionSpec as P

MESH = pl.DeviceIdType.MESH
F32, BF16 = jnp.float32, jnp.bfloat16
T, D, H, DH, M, FF = 512, 512, 8, 64, 256, 2048
SLAB = 136
EPS = 1e-05
VMEM_LIMIT = 50 * 2**20
C = DH ** -0.25
ALPHA = C * math.log2(math.e)
GELU_A, GELU_B = math.sqrt(2.0 / math.pi), 0.044715


def dot(a, b):
    return lax.dot_general(a, b, (((1,), (0,)), ((), ())), preferred_element_type=F32)


def dot_nt(a, b):
    return lax.dot_general(a, b, (((1,), (1,)), ((), ())), preferred_element_type=F32)


def dot_tn(a, b):
    return lax.dot_general(a, b, (((0,), (0,)), ((), ())), preferred_element_type=F32)


def iota(shape, dim):
    return lax.broadcasted_iota(jnp.int32, shape, dim)


def place():
    pack, seq = lax.axis_index("pack"), lax.axis_index("seq")
    return pack >> 1, pack & 1, seq >> 2, seq & 3


def layer_norm(v):
    centred = v - jnp.mean(v, axis=-1, keepdims=True)
    scale = lax.rsqrt(jnp.mean(centred * centred, axis=-1, keepdims=True) + EPS)
    return centred * scale, scale


def norm_back(n, scale, e):
    return scale * (e - jnp.mean(e, axis=-1, keepdims=True) - n * jnp.mean(e * n, axis=-1, keepdims=True))


def row_loop(step, body, carry=0):
    def run(i, c):
        return body(pl.ds(pl.multiple_of(i * step, step), step), c)

    return lax.fori_loop(0, T // step, run, carry, unroll=2)


def head_loop(body, start=0, stop=H):
    def run(h, c):
        body(h)
        return c

    lax.fori_loop(start, stop, run, 0, unroll=4 if (stop - start) % 4 == 0 else 2)


def wait_all(like, send_sem, recv_sem, dev):
    pltpu.make_async_remote_copy(
        src_ref=like, dst_ref=like, send_sem=send_sem, recv_sem=recv_sem, device_id=dev, device_id_type=MESH).wait()


class Part:
    def __init__(self, r, where, number, row, rows, axes, down, up):
        self.r, self.where, self.row, self.n = r, where, row, rows // 2
        self.axes = dict(zip("oic", axes))
        self.down, self.up = down, up
        self.number = number
        self.at = row + where[1] * self.n
        self.buf = row // 2
        self.step, self.last = -1, len(down) + len(up) + 1
        self.flying, self.held, self.freed = 0, {}, set()

    def mine(self, role):
        z, core, x, y = self.where
        return (x, y, z)[self.axes[role]]

    def peers(self, roles):
        z, core, x, y = self.where
        out = []
        for far in range(1, 4 ** len(roles)):
            at = {role: (self.mine(role) + far // 4 ** k) & 3 for k, role in enumerate(roles)}
            spot = [x, y, z]
            for role, there in at.items():
                spot[self.axes[role]] = there
            out.append((at, (spot[2] * 2 + core, spot[0] * 4 + spot[1])))
        return out

    def behind(self, roles, d):
        return {role: (self.mine(role) - (d + 1) // 4 ** k) & 3 for k, role in enumerate(roles)}

    def sibling(self):
        z, core, x, y = self.where
        return (z * 2 + 1 - core, x * 4 + y)

    def block(self, at={}):
        at = {**self.held, **at}
        row, rows, lane, lanes = self.at, self.n, 0, 512
        if "o" in at:
            row, rows = row + at["o"] * (self.n // 4), self.n // 4
        if "i" in at:
            row, rows = row + at["i"] * (self.n // 16), self.n // 16
        if "c" in at:
            lane, lanes = pl.multiple_of(at["c"] * 128, 128), 128
        return row, rows, lane, lanes

    def view(self, block):
        row, rows, lane, lanes = block
        return self.r.g.at[pl.ds(pl.multiple_of(row, 8), rows), pl.ds(lane, lanes)]

    def landing(self, roles, d):
        n = self.n
        row, lane = {
            "o": (d * (n // 4), 0),
            "ic": (3 * n // 4 + d // 4 * (n // 16), d % 4 * 128),
            "c": (0, d * 128),
            "oi": (d * (n // 16), 384),
        }[roles]
        return self.buf + row, lane

    def send(self, src, dst, dev):
        pltpu.make_async_remote_copy(
            src_ref=src, dst_ref=dst, send_sem=self.r.ssem.at[self.number], recv_sem=self.r.rsem.at[self.number, self.step],
            device_id=dev, device_id_type=MESH).start()
        self.flying += 1
        self.piece = src.shape

    def add(self, block, buf, slots):
        r = self.r
        row, rows, lane, lanes = block
        step = min(16384 // lanes, rows)

        def body(i, c):
            at = pl.ds(pl.multiple_of(row + i * step, 8), step)
            total = r.g[at, pl.ds(lane, lanes)]
            for slot, column in slots:
                total = total + buf[pl.ds(pl.multiple_of(slot + i * step, 8), step), pl.ds(column, lanes)]
            r.g[at, pl.ds(lane, lanes)] = total
            return c

        lax.fori_loop(0, rows // step, body, 0)

    def finish(self):
        r, s, downs = self.r, self.step, len(self.down)
        if self.flying:
            rows, lanes = self.piece
            wait_all(r.from_chip.at[pl.ds(0, self.flying * rows), pl.ds(0, lanes)], r.ssem.at[self.number], r.rsem.at[self.number, s], self.sibling())
        self.flying = 0
        if s == 0:
            pl.semaphore_signal(r.free.at[self.number, 0], inc=1, device_id=self.sibling(), device_id_type=MESH)
            self.add(self.block(), r.from_core, [(self.buf, 0)])
        elif 1 <= s <= downs:
            roles = self.down[s - 1]
            self.held.update({role: self.mine(role) for role in roles})
            for k in range(1, len(self.up)):
                if k not in self.freed and set(self.up[k]) <= set(self.held):
                    self.freed.add(k)
                    for _, dev in self.peers(self.up[k]):
                        pl.semaphore_signal(r.free.at[self.number, k], inc=1, device_id=dev, device_id_type=MESH)
            self.add(self.block(), r.from_chip, [self.landing(roles, d) for d in range(4 ** len(roles) - 1)])
        elif downs < s < self.last:
            roles = self.up[s - downs - 1]
            if s == downs + 1:
                for d in range(4 ** len(roles) - 1):
                    row, rows, lane, lanes = self.block(self.behind(roles, d))
                    r.g[pl.ds(pl.multiple_of(row, 8), rows), pl.ds(lane, lanes)] = r.turn[d, pl.ds(self.buf // 16, rows)]
            for role in roles:
                del self.held[role]

    def start(self):
        r, n, downs = self.r, self.n, len(self.down)
        self.step = s = self.step + 1
        if s == 0:
            core = self.where[1]
            self.send(r.g.at[pl.ds(pl.multiple_of(self.row + (1 - core) * n, 8), n)], r.from_core.at[pl.ds(self.buf, n)], self.sibling())
        elif 1 <= s <= downs:
            roles = self.down[s - 1]
            for d, (at, dev) in enumerate(self.peers(roles)):
                block = self.block(at)
                row, lane = self.landing(roles, d)
                self.send(self.view(block), r.from_chip.at[pl.ds(row, block[1]), pl.ds(lane, block[3])], dev)
        elif downs < s < self.last:
            k = s - downs - 1
            roles = self.up[k]
            block = self.block()
            part = self.view(block)
            peers = self.peers(roles)
            if k > 0:
                pl.semaphore_wait(r.free.at[self.number, k], len(peers))
            for d, (at, dev) in enumerate(peers):
                self.send(part, part if k > 0 else r.turn.at[d, pl.ds(self.buf // 16, block[1])], dev)
        elif s == self.last:
            part = self.view(self.block())
            pl.semaphore_wait(r.free.at[self.number, 0], 1)
            self.send(part, part, self.sibling())

    def tick(self):
        if self.step <= self.last:
            self.finish()
            self.start()


def tick(*parts):
    for part in parts:
        part.tick()


class Exchange:
    PIECES = (pl.ds(64, SLAB - 64), pl.ds(0, 64))

    def __init__(self, r, which, pack, seq):
        self.r, self.sems, self.pack, self.seq = r, r.esem.at[which], pack, seq

    def send(self, src, dst, way, piece):
        rows = self.PIECES[piece]
        for step in range(1, 16):
            peer = (self.seq + step) & 15
            pltpu.make_async_remote_copy(
                src_ref=src.at[peer, rows], dst_ref=dst.at[self.seq, rows], send_sem=self.sems.at[4 + piece],
                recv_sem=self.sems.at[2 * way + piece], device_id=(self.pack, peer), device_id_type=MESH).start()
        dst[self.seq, rows] = src[self.seq, rows]

    def wait_piece(self, way, piece):
        wait_all(
            self.r.arrived.at[pl.ds(0, 15), self.PIECES[piece]], self.sems.at[4 + piece], self.sems.at[2 * way + piece],
            (self.pack, (self.seq + 1) & 15))

    def wait(self):
        self.wait_piece(1, 0)
        self.wait_piece(1, 1)

    def begin(self):
        self.send(self.r.out, self.r.arrived, 0, 0)
        self.send(self.r.out, self.r.arrived, 0, 1)

    def turn(self):
        arrived, back = self.r.arrived, self.r.back
        none, small_none = jnp.zeros((64, 128), F32), jnp.zeros((1, 128), F32)

        def left(dev, carry):
            total, small = carry
            tail, mine = arrived[dev - 1, 128:136], arrived[dev, 128:136]
            whole, joins = tail[2:3] == tail[3:4], tail[3:4] == mine[2:3]
            total = jnp.where(joins, arrived[dev - 1, 64:128] + jnp.where(whole, total, 0.0), 0.0)
            small = jnp.where(joins, tail[1:2] + jnp.where(whole, small, 0.0), 0.0)
            back[dev, 64:128] = total
            back[dev, 128:129] = small
            return total, small

        def right_small(i, small):
            dev = 14 - i
            tail, mine = arrived[dev + 1, 128:136], arrived[dev, 128:136]
            whole, joins = tail[2:3] == tail[3:4], mine[3:4] == tail[2:3]
            small = jnp.where(joins, tail[0:1] + jnp.where(whole, small, 0.0), 0.0)
            back[dev, 129:130] = small
            return small

        def right(i, total):
            dev = 14 - i
            tail, mine = arrived[dev + 1, 128:136], arrived[dev, 128:136]
            whole, joins = tail[2:3] == tail[3:4], mine[3:4] == tail[2:3]
            total = jnp.where(joins, arrived[dev + 1, 0:64] + jnp.where(whole, total, 0.0), 0.0)
            back[dev, 0:64] = total
            return total

        self.wait_piece(0, 0)
        for dev in range(16):
            back[dev, 128:136] = jnp.zeros((8, 128), F32)
        back[0, 64:128] = none
        lax.fori_loop(1, 16, left, (none, small_none))
        lax.fori_loop(0, 15, right_small, small_none)
        self.send(back, self.r.got, 1, 0)
        self.wait_piece(0, 1)
        back[15, 0:64] = none
        lax.fori_loop(0, 15, right, none)
        self.send(back, self.r.got, 1, 1)


class Gains:
    def __init__(self, r, pack, seq):
        self.r, self.pack, self.seq = r, pack, seq

    def send(self, src, dst, way, size):
        for step in range(1, size):
            dev = ((self.pack + step) & 7, self.seq) if way == 0 else (self.pack, (self.seq + step) & 15)
            pltpu.make_async_remote_copy(
                src_ref=src, dst_ref=dst.at[step - 1], send_sem=self.r.gsem.at[2], recv_sem=self.r.gsem.at[way],
                device_id=dev, device_id_type=MESH).start()

    def wait(self, like, way):
        wait_all(like, self.r.gsem.at[2], self.r.gsem.at[way], (self.pack, (self.seq + 1) & 15))

    def begin(self):
        self.send(self.r.gain_here, self.r.gain_pack, 0, 8)

    def turn(self):
        self.wait(self.r.gain_pack, 0)
        total = self.r.gain_here[...]
        for i in range(7):
            total = total + self.r.gain_pack[i]
        self.r.gain_mid[...] = total
        self.send(self.r.gain_mid, self.r.gain_seq, 1, 16)

    def end(self):
        self.wait(self.r.gain_seq, 1)
        total = self.r.gain_mid[...]
        for i in range(15):
            total = total + self.r.gain_seq[i]
        return total


class Refs:
    pass


SCRATCH = [
    ("x", (T, D), BF16), ("cot", (T, D), BF16),
    ("wqkv", (3, D, D), BF16), ("wo", (D, D), BF16),
    ("wup", (4, D, 512), BF16), ("wdown", (4, 512, D), BF16), ("rf", (H, DH, M), BF16),
    ("rx", (4, 256, 512), BF16), ("r80", (H, 80, M), BF16),
    ("nb", (T, D), BF16), ("nT", (D, T), BF16), ("qT", (D, T), BF16), ("kT", (D, T), BF16),
    ("xb", (4, T, 512), BF16),
    ("gup", (4, T, 512), BF16),
    ("vext", (H, 80, T), BF16), ("gext", (H, 80, T), BF16),
    ("phik", (H, T, M), BF16), ("phiq", (H, T, M), BF16),
    ("dcol", (T, T), F32),
    ("num", (H, DH, T), F32), ("den", (H, 8, T), F32),
    ("attT", (D, T), BF16), ("att", (T, D), BF16), ("mid", (T, D), F32), ("hid", (T, D), BF16),
    ("acc", (T, D), F32), ("acc2", (T, D), F32), ("gmid", (T, D), F32),
    ("sb1", (H, 144, M), BF16), ("sb2", (H, 144, M), BF16),
            ("out", (16, SLAB, 128), F32), ("arrived", (16, SLAB, 128), F32), ("got", (16, SLAB, 128), F32),
    ("from_core", (3072, 512), F32), ("from_chip", (3072, 512), F32), ("turn", (15, 192, 128), F32),
    ("gain_sum", (2, 8, D), F32), ("gain_here", (8, 128), F32), ("gain_pack", (7, 8, 128), F32), ("gain_mid", (8, 128), F32), ("gain_seq", (15, 8, 128), F32),
]
SEMS = [
    ("load", pltpu.SemaphoreType.DMA((9,))), ("esem", pltpu.SemaphoreType.DMA((2, 6))), ("gsem", pltpu.SemaphoreType.DMA((3,))),
    ("ssem", pltpu.SemaphoreType.DMA((11,))), ("rsem", pltpu.SemaphoreType.DMA((11, 6))), ("free", pltpu.SemaphoreType.REGULAR((11, 2))),
]
ROW_DOWN, ROW_UP, ROW_O, ROW_Q, ROW_K, ROW_V = 0, 2048, 4096, 4608, 5120, 5632


def kernel(
    x_h, wq_h, wk_h, wv_h, wo_h, wup_h, wdown_h, rf_h, cot_h, ga_ref, gf_ref, doc_ref, live_ref,
    obf, gibf, g, gain_ref, *scratch):
    r = Refs()
    r.obf, r.gibf, r.g = obf, gibf, g
    for (name, *_), ref in zip(SCRATCH + SEMS, scratch):
        setattr(r, name, ref)
    r.gb, r.hidT, r.gT, r.back = r.nb, r.att, r.gup, r.out
    where = place()
    z, core, px, py = where
    pack, seq = lax.axis_index("pack"), lax.axis_index("seq")

    loads = {}

    def load(name, src, dst):
        copy = pltpu.make_async_copy(src, dst, r.load.at[len(loads)])
        copy.start()
        loads[name] = copy

    load("x", x_h, r.x)
    load("wk", wk_h, r.wqkv.at[1])
    load("rf", rf_h, r.rf)
    load("wv", wv_h, r.wqkv.at[2])
    load("wq", wq_h, r.wqkv.at[0])
    barrier = pltpu.get_barrier_semaphore()
    for step in range(1, 16):
        pl.semaphore_signal(barrier, inc=1, device_id=(pack, (seq + step) & 15), device_id_type=MESH)
    for step in range(1, 8):
        pl.semaphore_signal(barrier, inc=1, device_id=((pack + step) & 7, seq), device_id_type=MESH)

    doc = doc_ref[...].astype(F32)
    doc_f, doc_l = doc[:, 0:1], doc[:, T - 1:T]
    in_f, in_l = doc == doc_f, doc == doc_l
    one_f, one_l = in_f.astype(F32), in_l.astype(F32)
    row16 = iota((16, T), 0)

    def ends(block, tail_f, tail_l):
        zero = jnp.zeros_like(block)
        tail = jnp.where(row16 == 0, tail_f, jnp.where(row16 == 1, tail_l, 0.0))
        return jnp.concatenate(
            [jnp.where(in_f, block, zero).astype(BF16), jnp.where(in_l, block, zero).astype(BF16), tail.astype(BF16)], axis=0)

    dcol = jnp.broadcast_to(doc, (128, T)).T
    for j in range(4):
        r.dcol[:, j * 128:(j + 1) * 128] = dcol
    live = jnp.broadcast_to(live_ref[...].astype(F32), (128, T)).T

    loads["x"].wait()

    def first_norm(rows, c):
        n, _ = layer_norm(r.x[rows, :].astype(F32))
        r.nb[rows, :] = (n * ga_ref[...]).astype(BF16)
        return c

    row_loop(64, first_norm)
    loads["rf"].wait()
    for p in range(4):
        lane, row = iota((256, 512), 1) // 256, iota((256, 512), 0)
        pick = (row >= 128) & (row < 152) & (row % 8 == 2 * p + lane)
        r.rx[p] = jnp.where(pick, 1.0, 0.0).astype(BF16)
        r.rx[p, 0:64, 0:256] = r.rf[2 * p]
        r.rx[p, 64:128, 256:512] = r.rf[2 * p + 1]
    for h in range(H):
        r.r80[h, 0:64] = r.rf[h]
        r.r80[h, 64:80] = jnp.where(iota((16, M), 0) == 0, 1.0, 0.0).astype(BF16)
    pick_heads = ((iota((D, 128), 1) % 8 == iota((D, 128), 0) // DH) & (iota((D, 128), 1) < 24)).astype(BF16)

    def features(w, low, transposed, phi, off, alive):
        flat = dot(r.nb[...], r.wqkv[w]).astype(BF16)
        transposed[...] = flat.T
        square = flat.astype(F32)
        square = square * square
        high = square.astype(BF16)
        rest = (square - high.astype(F32)).astype(BF16)
        size = dot(high, pick_heads) + dot(rest, pick_heads)
        shift = size * (-0.5 * C) - 4.0 / ALPHA
        if alive is not None:
            shift = shift + (alive - 1.0) * 1e30
        first = shift.astype(BF16).astype(F32)
        second = (shift - first).astype(BF16).astype(F32)
        third = shift - first - second
        at = iota((T, 128), 1)
        shift = jnp.where(at < 8, first, jnp.where(at < 16, second, jnp.where(at < 24, third, 0.0))).astype(BF16)
        for p in range(4):
            low[p, :, off:off + 128] = flat[:, p * 128:(p + 1) * 128]
            low[p, :, off + 128:off + 256] = shift

        def one_pair(p, c):
            y = dot(low[p, :, off:off + 256], r.rx[p])
            y = jnp.exp2(y * ALPHA).astype(BF16)
            phi[2 * p] = y[:, 0:256]
            phi[2 * p + 1] = y[:, 256:512]
            return c

        lax.fori_loop(0, 4, one_pair, 0)

    loads["wk"].wait()
    features(1, r.xb, r.kT, r.phik, 0, live)
    loads["wv"].wait()
    vT = dot(r.nb[...], r.wqkv[2]).astype(BF16).T
    for h in range(H):
        r.vext[h, 0:64] = vT[h * 64:(h + 1) * 64]
        r.vext[h, 64:80] = jnp.where(row16 == 0, 1.0, 0.0).astype(BF16)

    def put_slab(h, lhs, phi):
        s = dot(lhs, phi)
        row = iota((8, M), 0)
        tail = jnp.where(row == 2, doc_f, jnp.where(row == 3, doc_l, s[128:136]))
        for half in range(2):
            r.out[2 * h + half, 0:128] = s[0:128, half * 128:(half + 1) * 128]
            r.out[2 * h + half, 128:136] = tail[:, half * 128:(half + 1) * 128]

    def take_slab(h, sb):
        for half in range(2):
            lanes = pl.ds(half * 128, 128)
            sb[h, 0:64, lanes] = r.got[2 * h + half, 64:128].astype(BF16)
            sb[h, 64:128, lanes] = r.got[2 * h + half, 0:64].astype(BF16)
            sb[h, 128:144, lanes] = jnp.concatenate(
                [r.got[2 * h + half, 128:136], jnp.zeros((8, 128), F32)], axis=0).astype(BF16)

    def value_ends(h):
        return ends(r.vext[h, 0:64].astype(F32), one_f, one_l)

    head_loop(lambda h: put_slab(h, value_ends(h), r.phik[h]))
    pl.semaphore_wait(barrier, 22)
    exchange = Exchange(r, 0, pack, seq)
    exchange.begin()
    load("wo", wo_h, r.wo)
    load("cot", cot_h, r.cot)
    for j in range(4):
        pltpu.make_async_copy(wup_h.at[:, pl.ds(j * 512, 512)], r.wup.at[j], r.load.at[7]).start()
        pltpu.make_async_copy(wdown_h.at[pl.ds(j * 512, 512)], r.wdown.at[j], r.load.at[8]).start()

    r.nT[...] = r.nb[...].T
    loads["wq"].wait()
    features(0, r.xb, r.qT, r.phiq, 256, None)
    exchange.turn()

    def same(block):
        return jnp.where(r.dcol[...] == doc, block, 0.0).astype(BF16)

    def attend(h):
        local = dot_nt(r.vext[h], same(dot_nt(r.phiq[h], r.phik[h])))
        r.num[h] = local[0:64]
        r.den[h] = local[64:72]

    head_loop(attend)
    exchange.wait()

    def join(h):
        take_slab(h, r.sb1)
        far = dot_nt(r.sb1[h], r.phiq[h])
        num = r.num[h] + jnp.where(in_f, far[0:64], 0.0) + jnp.where(in_l, far[64:128], 0.0)
        den = r.den[h, 0:1] + jnp.where(in_f, far[128:129], 0.0) + jnp.where(in_l, far[129:130], 0.0)
        inv = 1.0 / den
        att = num * inv
        r.num[h] = att
        r.den[h, 0:1] = inv
        r.attT[pl.ds(pl.multiple_of(h * 64, 64), 64)] = att.astype(BF16)

    head_loop(join)
    r.att[...] = r.attT[...].T
    loads["wo"].wait()
    r.mid[...] = dot(r.att[...], r.wo[...])

    def second_norm(rows, c):
        mid = r.x[rows, :].astype(F32) + r.mid[rows, :]
        r.mid[rows, :] = mid
        n, _ = layer_norm(mid)
        r.hid[rows, :] = (n * gf_ref[...]).astype(BF16)
        return c

    row_loop(64, second_norm)

    loads["cot"].wait()
    pltpu.make_async_copy(r.wup, r.wup, r.load.at[7]).wait()
    pltpu.make_async_copy(r.wdown, r.wdown, r.load.at[8]).wait()

    def feed(j, c):
        r.acc[...] = dot(r.hid[...], r.wup[j])
        r.acc2[...] = dot_nt(r.cot[...], r.wdown[j])

        def gelu(rows, c):
            u = r.acc[rows, :]
            ga = r.acc2[rows, :].astype(BF16).astype(F32)
            sq = u * u
            t = jnp.tanh(u * (GELU_A + GELU_A * GELU_B * sq))
            half = 0.5 * (1.0 + t)
            slope = half + 0.5 * u * (1.0 - t * t) * (GELU_A + 3.0 * GELU_A * GELU_B * sq)
            r.xb[j, rows, :] = (u * half).astype(BF16)
            r.gup[j, rows, :] = (ga * slope).astype(BF16)
            return c

        row_loop(32, gelu)
        back = dot_nt(r.gup[j], r.wup[j])

        r.gmid[...] = back if j == 0 else r.gmid[...] + back
        block(ROW_DOWN + j * 512, dot_tn(r.xb[j], r.cot[...]))
        block(ROW_UP + j * 512, dot(r.hidT[...], r.gup[j]))
        return c

    X, Y, Z = 0, 1, 2
    early = [
        Part(r, where, k, ROW_DOWN + 512 * k, 512, axes, ("o", "ic"), ("ic", "o"))
        for k, axes in enumerate(((X, Y, Z), (Y, X, Z), (X, Y, Z), (Y, X, Z)))
    ]
    up = [
        Part(r, where, 4, ROW_UP, 1024, (X, Y, Z), ("c", "oi"), ("oi", "c")),
        Part(r, where, 5, ROW_UP + 1024, 512, (X, Y, Z), ("c", "oi"), ("ic", "o")),
        Part(r, where, 6, ROW_UP + 1536, 512, (Y, X, Z), ("c", "oi"), ("ic", "o")),
    ]
    branch = Part(r, where, 7, ROW_O, 512, (Z, X, Y), ("o", "ic"), ("ic", "o"))
    query = Part(r, where, 8, ROW_Q, 512, (Z, Y, X), ("o", "ic"), ("ic", "o"))
    last = [
        Part(r, where, 9, ROW_K, 512, (X, Y, Z), ("o", "ic"), ("ic", "o")),
        Part(r, where, 10, ROW_V, 512, (Y, X, Z), ("o", "ic"), ("ic", "o")),
    ]

    def block(row, value):
        r.g[row:row + 512, :] = value

    r.hidT[...] = r.hid[...].T
    for j, moves in enumerate((early[:1], early[:2] + up[:1], early[1:3] + up[:2], early[2:4] + up[1:3])):
        feed(j, 0)
        tick(*moves)

    def add_gain(which, p):
        total = r.gain_sum[which]
        for i in range(8):
            total = total + p[i * 8:(i + 1) * 8]
        r.gain_sum[which] = total

    r.gain_sum[...] = jnp.zeros((2, 8, D), F32)

    def second_back(rows, c):
        gh = r.gmid[rows, :].astype(BF16).astype(F32)
        n, scale = layer_norm(r.mid[rows, :])
        gm = r.cot[rows, :].astype(F32) + norm_back(n, scale, gh * gf_ref[...])
        r.gmid[rows, :] = gm
        r.gb[rows, :] = gm.astype(BF16)
        add_gain(1, gh * n)
        return c

    row_loop(64, second_back)
    tick(early[3], up[2])
    block(ROW_O, dot(r.attT[...], r.gb[...]))
    tick(branch)
    r.acc[...] = dot_nt(r.wo[...], r.gb[...])

    def gates(h):
        ga = r.acc[pl.ds(pl.multiple_of(h * 64, 64), 64)].astype(BF16).astype(F32)
        inv = r.den[h, 0:1]
        gn = (ga * inv).astype(BF16)
        gd = -jnp.sum(ga * r.num[h], axis=0, keepdims=True) * inv
        r.gext[h, 0:64] = gn
        r.gext[h, 64:80] = jnp.where(row16 == 0, gd, 0.0).astype(BF16)
        put_slab(h, grad_ends(h), r.phiq[h])

    def grad_ends(h):
        gd = r.gext[h, 64:80].astype(F32)[0:1]
        return ends(r.gext[h, 0:64].astype(F32), one_f * gd, one_l * gd)

    head_loop(gates)
    tick(branch)
    exchange = Exchange(r, 1, pack, seq)
    exchange.begin()

    def map_back(h, gphi, phi, flat, which):
        p = (gphi.astype(BF16).astype(F32) * phi.astype(F32)).astype(BF16)
        through = dot_nt(r.r80[h], p)
        rows = pl.ds(pl.multiple_of(h * 64, 64), 64)
        r.gT[which, rows] = (C * through[0:64] - (C * C) * through[64:65] * flat[rows].astype(F32)).astype(BF16)

    def query_back(h):
        gphi = dot(same(dot_tn(r.gext[h], r.vext[h])), r.phik[h]) + dot_tn(grad_ends(h), r.sb1[h])
        map_back(h, gphi, r.phiq[h], r.qT, 0)
        r.acc2[pl.ds(pl.multiple_of(h * 64, 64), 64)] = dot(r.gext[h, 0:64], same(dot_nt(r.phiq[h], r.phik[h])))

    head_loop(query_back)
    exchange.turn()
    tick(*early)
    block(ROW_Q, dot_nt(r.nT[...], r.gT[0]))
    tick(query)
    r.acc[...] = dot(r.xb[0], r.wdown[0])
    for j in range(1, 4):
        r.acc[...] += dot(r.xb[j], r.wdown[j])

    def put_out(rows, c):
        r.obf[rows, :] = (r.mid[rows, :] + r.acc[rows, :]).astype(BF16)
        return c

    row_loop(64, put_out)
    tick(query)

    def key_local(h):
        gphi = dot(same(dot_tn(r.vext[h], r.gext[h])), r.phiq[h]).astype(BF16)
        r.xb[h // 2, :, pl.ds(pl.multiple_of(h % 2 * 256, 256), 256)] = gphi

    head_loop(key_local)
    tick(*up, branch)
    exchange.wait()
    tick(*early, query)

    def key_back(h):
        take_slab(h, r.sb2)
        gphi = r.xb[h // 2, :, pl.ds(pl.multiple_of(h % 2 * 256, 256), 256)].astype(F32) + dot_tn(value_ends(h), r.sb2[h])
        map_back(h, gphi, r.phik[h], r.kT, 1)
        far = dot_nt(r.sb2[h, 0:128], r.phik[h])
        rows = pl.ds(pl.multiple_of(h * 64, 64), 64)
        r.gT[2, rows] = (r.acc2[rows] + jnp.where(in_f, far[0:64], 0.0) + jnp.where(in_l, far[64:128], 0.0)).astype(BF16)

    head_loop(key_back, 0, 4)
    tick(*up, branch)
    head_loop(key_back, 4, 8)
    block(ROW_K, dot_nt(r.nT[...], r.gT[1]))
    block(ROW_V, dot_nt(r.nT[...], r.gT[2]))
    tick(*last)
    tick(*early, up[0], branch, query)
    r.acc2[...] = dot(r.wqkv[0], r.gT[0])

    def normed_back(i, c):
        r.acc2[...] += dot(r.wqkv[i], r.gT[i])
        return c

    lax.fori_loop(1, 3, normed_back, 0)
    r.acc[...] = r.acc2[...].T
    tick(*last)

    def first_back(rows, c):
        gn = r.acc[rows, :].astype(BF16).astype(F32)
        n, scale = layer_norm(r.x[rows, :].astype(F32))
        r.gibf[rows, :] = (r.gmid[rows, :] + norm_back(n, scale, gn * ga_ref[...])).astype(BF16)
        add_gain(0, gn * n)
        return c

    row_loop(64, first_back)
    for which in range(2):
        total = r.gain_sum[which, 0:1]
        for i in range(1, 8):
            total = total + r.gain_sum[which, i:i + 1]
        for j in range(4):
            r.gain_here[4 * which + j:4 * which + j + 1] = total[:, j * 128:(j + 1) * 128]
    gains = Gains(r, pack, seq)
    gains.begin()
    tick(*last)
    tick(*early)
    tick(*last)
    tick(*up[1:], query)
    gains.turn()
    tick(*last)
    tick(up[0], branch, *up[1:], query)
    tick(*last)
    for part in early + up + [branch, query] + last:
        while part.step <= part.last:
            part.tick()
    total = gains.end()
    for j in range(4):
        gain_ref[0:1, j * 128:(j + 1) * 128] = total[j:j + 1]
        gain_ref[1:2, j * 128:(j + 1) * 128] = total[4 + j:5 + j]


def store_kernel(out, gin, g, gain, out_h, gin_h, gwq_h, gwk_h, gwv_h, gwo_h, gwup_h, gwdown_h, gga_h, ggf_h, sems):
    pieces = [(g.at[pl.ds(ROW_DOWN, FF)], gwdown_h)]
    pieces += [(g.at[pl.ds(ROW_UP + j * 512, 512)], gwup_h.at[:, pl.ds(j * 512, 512)]) for j in range(4)]
    pieces += [(g.at[pl.ds(row, 512)], dst) for row, dst in ((ROW_O, gwo_h), (ROW_Q, gwq_h), (ROW_K, gwk_h), (ROW_V, gwv_h))]
    pieces += [(out, out_h), (gin, gin_h), (gain.at[pl.ds(0, 1)], gga_h), (gain.at[pl.ds(1, 1)], ggf_h)]
    copies = [pltpu.make_async_copy(src, dst, sems.at[i]) for i, (src, dst) in enumerate(pieces)]
    for copy in copies:
        copy.start()
    for copy in copies:
        copy.wait()


def per_device(
    inputs, w_query, w_key, w_value, w_output, w_up, w_down, gain_attn, gain_ffn, random_features, doc_ids, live_rows, cotangent):
    hbm = pl.BlockSpec(memory_space=pltpu.HBM)
    vmem = pl.BlockSpec(memory_space=pltpu.VMEM)
    f32 = lambda *shape: jax.ShapeDtypeStruct(shape, F32)
    low = jax.ShapeDtypeStruct((T, D), BF16)
    held = pl.pallas_call(
        kernel,
        out_shape=(pltpu.VMEM((T, D), BF16), pltpu.VMEM((T, D), BF16), pltpu.VMEM((6144, 512), F32), pltpu.VMEM((8, D), F32)),
        in_specs=[hbm] * 9 + [vmem] * 4,
        out_specs=(vmem,) * 4,
        scratch_shapes=[pltpu.VMEM(shape, dtype) for _, shape, dtype in SCRATCH] + [sem for _, sem in SEMS],
        compiler_params=pltpu.CompilerParams(collective_id=0, has_side_effects=True, vmem_limit_bytes=VMEM_LIMIT),
    )(
        *[pltpu.with_memory_space_constraint(v, pltpu.HBM) for v in (
            inputs[0], w_query, w_key, w_value, w_output, w_up, w_down, random_features, cotangent[0])],
        gain_attn[None], gain_ffn[None], doc_ids, live_rows)
    outs = pl.pallas_call(
        store_kernel,
        out_shape=(low, low, f32(D, D), f32(D, D), f32(D, D), f32(D, D), f32(D, FF), f32(FF, D), f32(1, D), f32(1, D)),
        in_specs=[vmem] * 4,
        out_specs=(hbm,) * 10,
        scratch_shapes=[pltpu.SemaphoreType.DMA((13,))],
        compiler_params=pltpu.CompilerParams(vmem_limit_bytes=1 * 2**20),
    )(*held)
    return (outs[0][None], outs[1][None]) + tuple(outs[2:8]) + (outs[8][0], outs[9][0])


def solution(mesh):
    rows = P("pack", "seq", None)
    return jax.shard_map(
        per_device,
        mesh=mesh,
        in_specs=(rows,) + (P(),) * 9 + (P("pack", "seq"), P("pack", "seq"), rows),
        out_specs=(rows, rows) + (P(),) * 8,
        check_vma=False,
    )
```

```python
import functools
import math

import jax
import jax.numpy as jnp
from jax import lax
from jax.experimental import pallas as pl
from jax.experimental.pallas import tpu as pltpu
from jax.sharding import PartitionSpec as P

MESH = pl.DeviceIdType.MESH
F32, BF16 = jnp.float32, jnp.bfloat16
T, D, H, DH, M, FF = 512, 512, 8, 64, 256, 2048
SLAB = 136
EPS = 1e-05
VMEM_LIMIT = 50 * 2**20
C = DH ** -0.25
ALPHA = C * math.log2(math.e)
GELU_A, GELU_B = math.sqrt(2.0 / math.pi), 0.044715


def dot(a, b):
    return lax.dot_general(a, b, (((1,), (0,)), ((), ())), preferred_element_type=F32)


def dot_nt(a, b):
    return lax.dot_general(a, b, (((1,), (1,)), ((), ())), preferred_element_type=F32)


def dot_tn(a, b):
    return lax.dot_general(a, b, (((0,), (0,)), ((), ())), preferred_element_type=F32)


def iota(shape, dim):
    return lax.broadcasted_iota(jnp.int32, shape, dim)


def place():
    pack, seq = lax.axis_index("pack"), lax.axis_index("seq")
    return pack >> 1, pack & 1, seq >> 2, seq & 3


def layer_norm(v):
    centred = v - jnp.mean(v, axis=-1, keepdims=True)
    scale = lax.rsqrt(jnp.mean(centred * centred, axis=-1, keepdims=True) + EPS)
    return centred * scale, scale


def norm_back(n, scale, e):
    return scale * (e - jnp.mean(e, axis=-1, keepdims=True) - n * jnp.mean(e * n, axis=-1, keepdims=True))


def row_loop(step, body, carry=0):
    def run(i, c):
        return body(pl.ds(pl.multiple_of(i * step, step), step), c)

    return lax.fori_loop(0, T // step, run, carry, unroll=2)


def head_loop(body, start=0, stop=H):
    def run(h, c):
        body(h)
        return c

    lax.fori_loop(start, stop, run, 0, unroll=4 if (stop - start) % 4 == 0 else 2)


def wait_all(like, send_sem, recv_sem, dev):
    pltpu.make_async_remote_copy(
        src_ref=like, dst_ref=like, send_sem=send_sem, recv_sem=recv_sem, device_id=dev, device_id_type=MESH).wait()


class Part:
    def __init__(self, r, where, number, row, rows, axes, down, up):
        self.r, self.where, self.row, self.n = r, where, row, rows // 2
        self.axes = dict(zip("oic", axes))
        self.down, self.up = down, up
        self.number = number
        self.at = row + where[1] * self.n
        self.buf = row // 2
        self.step, self.last = -1, len(down) + len(up) + 1
        self.flying, self.held, self.freed = 0, {}, set()

    def mine(self, role):
        z, core, x, y = self.where
        return (x, y, z)[self.axes[role]]

    def peers(self, roles):
        z, core, x, y = self.where
        out = []
        for far in range(1, 4 ** len(roles)):
            at = {role: (self.mine(role) + far // 4 ** k) & 3 for k, role in enumerate(roles)}
            spot = [x, y, z]
            for role, there in at.items():
                spot[self.axes[role]] = there
            out.append((at, (spot[2] * 2 + core, spot[0] * 4 + spot[1])))
        return out

    def behind(self, roles, d):
        return {role: (self.mine(role) - (d + 1) // 4 ** k) & 3 for k, role in enumerate(roles)}

    def sibling(self):
        z, core, x, y = self.where
        return (z * 2 + 1 - core, x * 4 + y)

    def block(self, at={}):
        at = {**self.held, **at}
        row, rows, lane, lanes = self.at, self.n, 0, 512
        if "o" in at:
            row, rows = row + at["o"] * (self.n // 4), self.n // 4
        if "i" in at:
            row, rows = row + at["i"] * (self.n // 16), self.n // 16
        if "c" in at:
            lane, lanes = pl.multiple_of(at["c"] * 128, 128), 128
        return row, rows, lane, lanes

    def view(self, block):
        row, rows, lane, lanes = block
        return self.r.g.at[pl.ds(pl.multiple_of(row, 8), rows), pl.ds(lane, lanes)]

    def landing(self, roles, d):
        n = self.n
        row, lane = {
            "o": (d * (n // 4), 0),
            "ic": (3 * n // 4 + d // 4 * (n // 16), d % 4 * 128),
            "c": (0, d * 128),
            "oi": (d * (n // 16), 384),
        }[roles]
        return self.buf + row, lane

    def send(self, src, dst, dev):
        pltpu.make_async_remote_copy(
            src_ref=src, dst_ref=dst, send_sem=self.r.ssem.at[self.number], recv_sem=self.r.rsem.at[self.number, self.step],
            device_id=dev, device_id_type=MESH).start()
        self.flying += 1
        self.piece = src.shape

    def add(self, block, buf, slots):
        r = self.r
        row, rows, lane, lanes = block
        step = min(16384 // lanes, rows)

        def body(i, c):
            at = pl.ds(pl.multiple_of(row + i * step, 8), step)
            total = r.g[at, pl.ds(lane, lanes)]
            for slot, column in slots:
                total = total + buf[pl.ds(pl.multiple_of(slot + i * step, 8), step), pl.ds(column, lanes)]
            r.g[at, pl.ds(lane, lanes)] = total
            return c

        lax.fori_loop(0, rows // step, body, 0)

    def finish(self):
        r, s, downs = self.r, self.step, len(self.down)
        if self.flying:
            rows, lanes = self.piece
            wait_all(r.from_chip.at[pl.ds(0, self.flying * rows), pl.ds(0, lanes)], r.ssem.at[self.number], r.rsem.at[self.number, s], self.sibling())
        self.flying = 0
        if s == 0:
            pl.semaphore_signal(r.free.at[self.number, 0], inc=1, device_id=self.sibling(), device_id_type=MESH)
            self.add(self.block(), r.from_core, [(self.buf, 0)])
        elif 1 <= s <= downs:
            roles = self.down[s - 1]
            self.held.update({role: self.mine(role) for role in roles})
            for k in range(1, len(self.up)):
                if k not in self.freed and set(self.up[k]) <= set(self.held):
                    self.freed.add(k)
                    for _, dev in self.peers(self.up[k]):
                        pl.semaphore_signal(r.free.at[self.number, k], inc=1, device_id=dev, device_id_type=MESH)
            self.add(self.block(), r.from_chip, [self.landing(roles, d) for d in range(4 ** len(roles) - 1)])
        elif downs < s < self.last:
            roles = self.up[s - downs - 1]
            if s == downs + 1:
                for d in range(4 ** len(roles) - 1):
                    row, rows, lane, lanes = self.block(self.behind(roles, d))
                    r.g[pl.ds(pl.multiple_of(row, 8), rows), pl.ds(lane, lanes)] = r.turn[d, pl.ds(self.buf // 16, rows)]
            for role in roles:
                del self.held[role]

    def start(self):
        r, n, downs = self.r, self.n, len(self.down)
        self.step = s = self.step + 1
        if s == 0:
            core = self.where[1]
            self.send(r.g.at[pl.ds(pl.multiple_of(self.row + (1 - core) * n, 8), n)], r.from_core.at[pl.ds(self.buf, n)], self.sibling())
        elif 1 <= s <= downs:
            roles = self.down[s - 1]
            for d, (at, dev) in enumerate(self.peers(roles)):
                block = self.block(at)
                row, lane = self.landing(roles, d)
                self.send(self.view(block), r.from_chip.at[pl.ds(row, block[1]), pl.ds(lane, block[3])], dev)
        elif downs < s < self.last:
            k = s - downs - 1
            roles = self.up[k]
            block = self.block()
            part = self.view(block)
            peers = self.peers(roles)
            if k > 0:
                pl.semaphore_wait(r.free.at[self.number, k], len(peers))
            for d, (at, dev) in enumerate(peers):
                self.send(part, part if k > 0 else r.turn.at[d, pl.ds(self.buf // 16, block[1])], dev)
        elif s == self.last:
            part = self.view(self.block())
            pl.semaphore_wait(r.free.at[self.number, 0], 1)
            self.send(part, part, self.sibling())

    def tick(self):
        if self.step <= self.last:
            self.finish()
            self.start()


def tick(*parts):
    for part in parts:
        part.tick()


class Exchange:
    PIECES = (pl.ds(64, SLAB - 64), pl.ds(0, 64))

    def __init__(self, r, which, pack, seq):
        self.r, self.sems, self.pack, self.seq = r, r.esem.at[which], pack, seq

    def send(self, src, dst, way, piece):
        rows = self.PIECES[piece]
        for step in range(1, 16):
            peer = (self.seq + step) & 15
            pltpu.make_async_remote_copy(
                src_ref=src.at[peer, rows], dst_ref=dst.at[self.seq, rows], send_sem=self.sems.at[4 + piece],
                recv_sem=self.sems.at[2 * way + piece], device_id=(self.pack, peer), device_id_type=MESH).start()
        dst[self.seq, rows] = src[self.seq, rows]

    def wait_piece(self, way, piece):
        wait_all(
            self.r.arrived.at[pl.ds(0, 15), self.PIECES[piece]], self.sems.at[4 + piece], self.sems.at[2 * way + piece],
            (self.pack, (self.seq + 1) & 15))

    def wait(self):
        self.wait_piece(1, 0)
        self.wait_piece(1, 1)

    def begin(self):
        self.send(self.r.out, self.r.arrived, 0, 0)
        self.send(self.r.out, self.r.arrived, 0, 1)

    def turn(self):
        arrived, back = self.r.arrived, self.r.back
        none, small_none = jnp.zeros((64, 128), F32), jnp.zeros((1, 128), F32)

        def left(dev, carry):
            total, small = carry
            tail, mine = arrived[dev - 1, 128:136], arrived[dev, 128:136]
            whole, joins = tail[2:3] == tail[3:4], tail[3:4] == mine[2:3]
            total = jnp.where(joins, arrived[dev - 1, 64:128] + jnp.where(whole, total, 0.0), 0.0)
            small = jnp.where(joins, tail[1:2] + jnp.where(whole, small, 0.0), 0.0)
            back[dev, 64:128] = total
            back[dev, 128:129] = small
            return total, small

        def right_small(i, small):
            dev = 14 - i
            tail, mine = arrived[dev + 1, 128:136], arrived[dev, 128:136]
            whole, joins = tail[2:3] == tail[3:4], mine[3:4] == tail[2:3]
            small = jnp.where(joins, tail[0:1] + jnp.where(whole, small, 0.0), 0.0)
            back[dev, 129:130] = small
            return small

        def right(i, total):
            dev = 14 - i
            tail, mine = arrived[dev + 1, 128:136], arrived[dev, 128:136]
            whole, joins = tail[2:3] == tail[3:4], mine[3:4] == tail[2:3]
            total = jnp.where(joins, arrived[dev + 1, 0:64] + jnp.where(whole, total, 0.0), 0.0)
            back[dev, 0:64] = total
            return total

        self.wait_piece(0, 0)
        for dev in range(16):
            back[dev, 128:136] = jnp.zeros((8, 128), F32)
        back[0, 64:128] = none
        lax.fori_loop(1, 16, left, (none, small_none))
        lax.fori_loop(0, 15, right_small, small_none)
        self.send(back, self.r.got, 1, 0)
        self.wait_piece(0, 1)
        back[15, 0:64] = none
        lax.fori_loop(0, 15, right, none)
        self.send(back, self.r.got, 1, 1)


class Gains:
    def __init__(self, r, pack, seq):
        self.r, self.pack, self.seq = r, pack, seq

    def send(self, src, dst, way, size):
        for step in range(1, size):
            dev = ((self.pack + step) & 7, self.seq) if way == 0 else (self.pack, (self.seq + step) & 15)
            pltpu.make_async_remote_copy(
                src_ref=src, dst_ref=dst.at[step - 1], send_sem=self.r.gsem.at[2], recv_sem=self.r.gsem.at[way],
                device_id=dev, device_id_type=MESH).start()

    def wait(self, like, way):
        wait_all(like, self.r.gsem.at[2], self.r.gsem.at[way], (self.pack, (self.seq + 1) & 15))

    def begin(self):
        self.send(self.r.gain_here, self.r.gain_pack, 0, 8)

    def turn(self):
        self.wait(self.r.gain_pack, 0)
        total = self.r.gain_here[...]
        for i in range(7):
            total = total + self.r.gain_pack[i]
        self.r.gain_mid[...] = total
        self.send(self.r.gain_mid, self.r.gain_seq, 1, 16)

    def end(self):
        self.wait(self.r.gain_seq, 1)
        total = self.r.gain_mid[...]
        for i in range(15):
            total = total + self.r.gain_seq[i]
        return total


class Refs:
    pass


SCRATCH = [
    ("x", (T, D), BF16), ("cot", (T, D), BF16),
    ("wqkv", (3, D, D), BF16), ("wo", (D, D), BF16),
    ("wup", (4, D, 512), BF16), ("wdown", (4, 512, D), BF16), ("rf", (H, DH, M), BF16),
    ("rx", (4, 256, 512), BF16), ("r80", (H, 80, M), BF16),
    ("nb", (T, D), BF16), ("nT", (D, T), BF16), ("qT", (D, T), BF16), ("kT", (D, T), BF16),
    ("xb", (4, T, 512), BF16),
    ("gup", (4, T, 512), BF16),
    ("vext", (H, 80, T), BF16), ("gext", (H, 80, T), BF16),
    ("phik", (H, T, M), BF16), ("phiq", (H, T, M), BF16),
    ("dcol", (T, T), F32),
    ("num", (H, DH, T), F32), ("den", (H, 8, T), F32),
    ("attT", (D, T), BF16), ("att", (T, D), BF16), ("mid", (T, D), F32), ("hid", (T, D), BF16),
    ("acc", (T, D), F32), ("acc2", (T, D), F32), ("gmid", (T, D), F32),
    ("sb1", (H, 144, M), BF16), ("sb2", (H, 144, M), BF16),
            ("out", (16, SLAB, 128), F32), ("arrived", (16, SLAB, 128), F32), ("got", (16, SLAB, 128), F32),
    ("from_core", (3072, 512), F32), ("from_chip", (3072, 512), F32), ("turn", (15, 192, 128), F32),
    ("gain_sum", (2, 8, D), F32), ("gain_here", (8, 128), F32), ("gain_pack", (7, 8, 128), F32), ("gain_mid", (8, 128), F32), ("gain_seq", (15, 8, 128), F32),
]
SEMS = [
    ("load", pltpu.SemaphoreType.DMA((9,))), ("esem", pltpu.SemaphoreType.DMA((2, 6))), ("gsem", pltpu.SemaphoreType.DMA((3,))),
    ("ssem", pltpu.SemaphoreType.DMA((11,))), ("rsem", pltpu.SemaphoreType.DMA((11, 6))), ("free", pltpu.SemaphoreType.REGULAR((11, 2))),
]
ROW_DOWN, ROW_UP, ROW_O, ROW_Q, ROW_K, ROW_V = 0, 2048, 4096, 4608, 5120, 5632


def kernel(
    x_h, wq_h, wk_h, wv_h, wo_h, wup_h, wdown_h, rf_h, cot_h, ga_ref, gf_ref, doc_ref, live_ref,
    obf, gibf, g, gain_ref, *scratch):
    r = Refs()
    r.obf, r.gibf, r.g = obf, gibf, g
    for (name, *_), ref in zip(SCRATCH + SEMS, scratch):
        setattr(r, name, ref)
    r.gb, r.hidT, r.gT, r.back = r.nb, r.att, r.gup, r.out
    where = place()
    z, core, px, py = where
    pack, seq = lax.axis_index("pack"), lax.axis_index("seq")

    loads = {}

    def load(name, src, dst):
        copy = pltpu.make_async_copy(src, dst, r.load.at[len(loads)])
        copy.start()
        loads[name] = copy

    load("x", x_h, r.x)
    load("wk", wk_h, r.wqkv.at[1])
    load("rf", rf_h, r.rf)
    load("wv", wv_h, r.wqkv.at[2])
    load("wq", wq_h, r.wqkv.at[0])
    barrier = pltpu.get_barrier_semaphore()
    for step in range(1, 16):
        pl.semaphore_signal(barrier, inc=1, device_id=(pack, (seq + step) & 15), device_id_type=MESH)
    for step in range(1, 8):
        pl.semaphore_signal(barrier, inc=1, device_id=((pack + step) & 7, seq), device_id_type=MESH)

    doc = doc_ref[...].astype(F32)
    doc_f, doc_l = doc[:, 0:1], doc[:, T - 1:T]
    in_f, in_l = doc == doc_f, doc == doc_l
    one_f, one_l = in_f.astype(F32), in_l.astype(F32)
    row16 = iota((16, T), 0)

    def ends(block, tail_f, tail_l):
        zero = jnp.zeros_like(block)
        tail = jnp.where(row16 == 0, tail_f, jnp.where(row16 == 1, tail_l, 0.0))
        return jnp.concatenate(
            [jnp.where(in_f, block, zero).astype(BF16), jnp.where(in_l, block, zero).astype(BF16), tail.astype(BF16)], axis=0)

    live = jnp.broadcast_to(live_ref[...].astype(F32), (128, T)).T

    loads["x"].wait()

    def first_norm(rows, c):
        n, _ = layer_norm(r.x[rows, :].astype(F32))
        r.nb[rows, :] = (n * ga_ref[...]).astype(BF16)
        return c

    row_loop(64, first_norm)
    loads["rf"].wait()
    for p in range(4):
        lane, row = iota((256, 512), 1) // 256, iota((256, 512), 0)
        pick = (row >= 128) & (row < 152) & (row % 8 == 2 * p + lane)
        r.rx[p] = jnp.where(pick, 1.0, 0.0).astype(BF16)
        r.rx[p, 0:64, 0:256] = r.rf[2 * p]
        r.rx[p, 64:128, 256:512] = r.rf[2 * p + 1]
    pick_heads = ((iota((D, 128), 1) % 8 == iota((D, 128), 0) // DH) & (iota((D, 128), 1) < 24)).astype(BF16)

    def features(w, low, transposed, phi, off, alive):
        flat = dot(r.nb[...], r.wqkv[w]).astype(BF16)
        if transposed is not None:
            transposed[...] = flat.T
        square = flat.astype(F32)
        square = square * square
        high = square.astype(BF16)
        rest = (square - high.astype(F32)).astype(BF16)
        size = dot(high, pick_heads) + dot(rest, pick_heads)
        shift = size * (-0.5 * C) - 4.0 / ALPHA
        if alive is not None:
            shift = shift + (alive - 1.0) * 1e30
        first = shift.astype(BF16).astype(F32)
        second = (shift - first).astype(BF16).astype(F32)
        third = shift - first - second
        at = iota((T, 128), 1)
        shift = jnp.where(at < 8, first, jnp.where(at < 16, second, jnp.where(at < 24, third, 0.0))).astype(BF16)
        for p in range(4):
            low[p, :, off:off + 128] = flat[:, p * 128:(p + 1) * 128]
            low[p, :, off + 128:off + 256] = shift

        def one_pair(p, c):
            y = dot(low[p, :, off:off + 256], r.rx[p])
            y = jnp.exp2(y * ALPHA).astype(BF16)
            phi[2 * p] = y[:, 0:256]
            phi[2 * p + 1] = y[:, 256:512]
            return c

        lax.fori_loop(0, 4, one_pair, 0)

    loads["wk"].wait()
    features(1, r.xb, None, r.phik, 0, live)
    loads["wv"].wait()
    vT = dot(r.nb[...], r.wqkv[2]).astype(BF16).T
    for h in range(H):
        r.vext[h, 0:64] = vT[h * 64:(h + 1) * 64]
        r.vext[h, 64:80] = jnp.where(row16 == 0, 1.0, 0.0).astype(BF16)

    def put_slab(h, lhs, phi):
        s = dot(lhs, phi)
        row = iota((8, M), 0)
        tail = jnp.where(row == 2, doc_f, jnp.where(row == 3, doc_l, s[128:136]))
        for half in range(2):
            r.out[2 * h + half, 0:128] = s[0:128, half * 128:(half + 1) * 128]
            r.out[2 * h + half, 128:136] = tail[:, half * 128:(half + 1) * 128]

    def take_slab(h, sb):
        for half in range(2):
            lanes = pl.ds(half * 128, 128)
            sb[h, 0:64, lanes] = r.got[2 * h + half, 64:128].astype(BF16)
            sb[h, 64:128, lanes] = r.got[2 * h + half, 0:64].astype(BF16)
            sb[h, 128:144, lanes] = jnp.concatenate(
                [r.got[2 * h + half, 128:136], jnp.zeros((8, 128), F32)], axis=0).astype(BF16)

    def value_ends(h):
        return ends(r.vext[h, 0:64].astype(F32), one_f, one_l)

    head_loop(lambda h: put_slab(h, value_ends(h), r.phik[h]))
    pl.semaphore_wait(barrier, 22)
    exchange = Exchange(r, 0, pack, seq)
    exchange.begin()
    load("wo", wo_h, r.wo)
    load("cot", cot_h, r.cot)
    for j in range(4):
        pltpu.make_async_copy(wup_h.at[:, pl.ds(j * 512, 512)], r.wup.at[j], r.load.at[7]).start()
        pltpu.make_async_copy(wdown_h.at[pl.ds(j * 512, 512)], r.wdown.at[j], r.load.at[8]).start()

    r.nT[...] = r.nb[...].T
    dcol = jnp.broadcast_to(doc, (128, T)).T
    for j in range(4):
        r.dcol[:, j * 128:(j + 1) * 128] = dcol
    for h in range(H):
        r.r80[h, 0:64] = r.rf[h]
        r.r80[h, 64:80] = jnp.where(iota((16, M), 0) == 0, 1.0, 0.0).astype(BF16)
    for p in range(4):
        r.kT[p * 128:(p + 1) * 128] = r.xb[p, :, 0:128].T
    loads["wq"].wait()
    features(0, r.xb, r.qT, r.phiq, 256, None)
    exchange.turn()

    def same(block):
        return jnp.where(r.dcol[...] == doc, block, 0.0).astype(BF16)

    def attend(h):
        local = dot_nt(r.vext[h], same(dot_nt(r.phiq[h], r.phik[h])))
        r.num[h] = local[0:64]
        r.den[h] = local[64:72]

    head_loop(attend)
    exchange.wait()

    def join(h):
        take_slab(h, r.sb1)
        far = dot_nt(r.sb1[h], r.phiq[h])
        num = r.num[h] + jnp.where(in_f, far[0:64], 0.0) + jnp.where(in_l, far[64:128], 0.0)
        den = r.den[h, 0:1] + jnp.where(in_f, far[128:129], 0.0) + jnp.where(in_l, far[129:130], 0.0)
        inv = 1.0 / den
        att = num * inv
        r.num[h] = att
        r.den[h, 0:1] = inv
        r.attT[pl.ds(pl.multiple_of(h * 64, 64), 64)] = att.astype(BF16)

    head_loop(join)
    r.att[...] = r.attT[...].T
    loads["wo"].wait()
    r.mid[...] = dot(r.att[...], r.wo[...])

    def second_norm(rows, c):
        mid = r.x[rows, :].astype(F32) + r.mid[rows, :]
        r.mid[rows, :] = mid
        n, _ = layer_norm(mid)
        r.hid[rows, :] = (n * gf_ref[...]).astype(BF16)
        return c

    row_loop(64, second_norm)

    loads["cot"].wait()
    pltpu.make_async_copy(r.wup, r.wup, r.load.at[7]).wait()
    pltpu.make_async_copy(r.wdown, r.wdown, r.load.at[8]).wait()

    def feed(j, c):
        r.acc[...] = dot(r.hid[...], r.wup[j])
        r.acc2[...] = dot_nt(r.cot[...], r.wdown[j])

        def gelu(rows, c):
            u = r.acc[rows, :]
            ga = r.acc2[rows, :].astype(BF16).astype(F32)
            sq = u * u
            t = jnp.tanh(u * (GELU_A + GELU_A * GELU_B * sq))
            half = 0.5 * (1.0 + t)
            slope = half + 0.5 * u * (1.0 - t * t) * (GELU_A + 3.0 * GELU_A * GELU_B * sq)
            r.xb[j, rows, :] = (u * half).astype(BF16)
            r.gup[j, rows, :] = (ga * slope).astype(BF16)
            return c

        row_loop(32, gelu)
        back = dot_nt(r.gup[j], r.wup[j])

        r.gmid[...] = back if j == 0 else r.gmid[...] + back
        block(ROW_DOWN + j * 512, dot_tn(r.xb[j], r.cot[...]))
        block(ROW_UP + j * 512, dot(r.hidT[...], r.gup[j]))
        return c

    X, Y, Z = 0, 1, 2
    early = [
        Part(r, where, k, ROW_DOWN + 512 * k, 512, axes, ("o", "ic"), ("ic", "o"))
        for k, axes in enumerate(((X, Y, Z), (Y, X, Z), (X, Y, Z), (Y, X, Z)))
    ]
    up = [
        Part(r, where, 4, ROW_UP, 1024, (X, Y, Z), ("c", "oi"), ("oi", "c")),
        Part(r, where, 5, ROW_UP + 1024, 512, (X, Y, Z), ("c", "oi"), ("ic", "o")),
        Part(r, where, 6, ROW_UP + 1536, 512, (Y, X, Z), ("c", "oi"), ("ic", "o")),
    ]
    branch = Part(r, where, 7, ROW_O, 512, (Z, X, Y), ("o", "ic"), ("ic", "o"))
    query = Part(r, where, 8, ROW_Q, 512, (Z, Y, X), ("o", "ic"), ("ic", "o"))
    last = [
        Part(r, where, 9, ROW_K, 512, (X, Y, Z), ("o", "ic"), ("ic", "o")),
        Part(r, where, 10, ROW_V, 512, (Y, X, Z), ("o", "ic"), ("ic", "o")),
    ]

    def block(row, value):
        r.g[row:row + 512, :] = value

    r.hidT[...] = r.hid[...].T
    for j, moves in enumerate((early[:1], early[:2] + up[:1], early[1:3] + up[:2], early[2:4] + up[1:3])):
        feed(j, 0)
        tick(*moves)

    def add_gain(which, p):
        total = r.gain_sum[which]
        for i in range(8):
            total = total + p[i * 8:(i + 1) * 8]
        r.gain_sum[which] = total

    r.gain_sum[...] = jnp.zeros((2, 8, D), F32)

    def second_back(rows, c):
        gh = r.gmid[rows, :].astype(BF16).astype(F32)
        n, scale = layer_norm(r.mid[rows, :])
        gm = r.cot[rows, :].astype(F32) + norm_back(n, scale, gh * gf_ref[...])
        r.gmid[rows, :] = gm
        r.gb[rows, :] = gm.astype(BF16)
        add_gain(1, gh * n)
        return c

    row_loop(64, second_back)
    tick(early[3], up[2])
    block(ROW_O, dot(r.attT[...], r.gb[...]))
    tick(branch)
    r.acc[...] = dot_nt(r.wo[...], r.gb[...])

    def gates(h):
        ga = r.acc[pl.ds(pl.multiple_of(h * 64, 64), 64)].astype(BF16).astype(F32)
        inv = r.den[h, 0:1]
        gn = (ga * inv).astype(BF16)
        gd = -jnp.sum(ga * r.num[h], axis=0, keepdims=True) * inv
        r.gext[h, 0:64] = gn
        r.gext[h, 64:80] = jnp.where(row16 == 0, gd, 0.0).astype(BF16)
        put_slab(h, grad_ends(h), r.phiq[h])

    def grad_ends(h):
        gd = r.gext[h, 64:80].astype(F32)[0:1]
        return ends(r.gext[h, 0:64].astype(F32), one_f * gd, one_l * gd)

    head_loop(gates)
    tick(branch)
    exchange = Exchange(r, 1, pack, seq)
    exchange.begin()

    def map_back(h, gphi, phi, flat, which):
        p = (gphi.astype(BF16).astype(F32) * phi.astype(F32)).astype(BF16)
        through = dot_nt(r.r80[h], p)
        rows = pl.ds(pl.multiple_of(h * 64, 64), 64)
        r.gT[which, rows] = (C * through[0:64] - (C * C) * through[64:65] * flat[rows].astype(F32)).astype(BF16)

    def query_back(h):
        gphi = dot(same(dot_tn(r.gext[h], r.vext[h])), r.phik[h]) + dot_tn(grad_ends(h), r.sb1[h])
        map_back(h, gphi, r.phiq[h], r.qT, 0)
        r.acc2[pl.ds(pl.multiple_of(h * 64, 64), 64)] = dot(r.gext[h, 0:64], same(dot_nt(r.phiq[h], r.phik[h])))

    head_loop(query_back)
    exchange.turn()
    tick(*early)
    block(ROW_Q, dot_nt(r.nT[...], r.gT[0]))
    tick(query)
    r.acc[...] = dot(r.xb[0], r.wdown[0])
    for j in range(1, 4):
        r.acc[...] += dot(r.xb[j], r.wdown[j])

    def put_out(rows, c):
        r.obf[rows, :] = (r.mid[rows, :] + r.acc[rows, :]).astype(BF16)
        return c

    row_loop(64, put_out)
    tick(query)

    def key_local(h):
        gphi = dot(same(dot_tn(r.vext[h], r.gext[h])), r.phiq[h]).astype(BF16)
        r.xb[h // 2, :, pl.ds(pl.multiple_of(h % 2 * 256, 256), 256)] = gphi

    head_loop(key_local)
    tick(*up, branch)
    exchange.wait()
    tick(*early, query)

    def key_back(h):
        take_slab(h, r.sb2)
        gphi = r.xb[h // 2, :, pl.ds(pl.multiple_of(h % 2 * 256, 256), 256)].astype(F32) + dot_tn(value_ends(h), r.sb2[h])
        map_back(h, gphi, r.phik[h], r.kT, 1)
        far = dot_nt(r.sb2[h, 0:128], r.phik[h])
        rows = pl.ds(pl.multiple_of(h * 64, 64), 64)
        r.gT[2, rows] = (r.acc2[rows] + jnp.where(in_f, far[0:64], 0.0) + jnp.where(in_l, far[64:128], 0.0)).astype(BF16)

    head_loop(key_back, 0, 4)
    tick(*up, branch)
    head_loop(key_back, 4, 8)
    block(ROW_K, dot_nt(r.nT[...], r.gT[1]))
    block(ROW_V, dot_nt(r.nT[...], r.gT[2]))
    tick(*last)
    tick(*early, up[0], branch, query)
    r.acc2[...] = dot(r.wqkv[0], r.gT[0])

    def normed_back(i, c):
        r.acc2[...] += dot(r.wqkv[i], r.gT[i])
        return c

    lax.fori_loop(1, 3, normed_back, 0)
    r.acc[...] = r.acc2[...].T
    tick(*last)

    def first_back(rows, c):
        gn = r.acc[rows, :].astype(BF16).astype(F32)
        n, scale = layer_norm(r.x[rows, :].astype(F32))
        r.gibf[rows, :] = (r.gmid[rows, :] + norm_back(n, scale, gn * ga_ref[...])).astype(BF16)
        add_gain(0, gn * n)
        return c

    row_loop(64, first_back)
    for which in range(2):
        total = r.gain_sum[which, 0:1]
        for i in range(1, 8):
            total = total + r.gain_sum[which, i:i + 1]
        for j in range(4):
            r.gain_here[4 * which + j:4 * which + j + 1] = total[:, j * 128:(j + 1) * 128]
    gains = Gains(r, pack, seq)
    gains.begin()
    tick(*last)
    tick(*early)
    tick(*last)
    tick(*up[1:], query)
    gains.turn()
    tick(*last)
    tick(up[0], branch, *up[1:], query)
    tick(*last)
    for part in early + up + [branch, query] + last:
        while part.step <= part.last:
            part.tick()
    total = gains.end()
    for j in range(4):
        gain_ref[0:1, j * 128:(j + 1) * 128] = total[j:j + 1]
        gain_ref[1:2, j * 128:(j + 1) * 128] = total[4 + j:5 + j]


def store_kernel(out, gin, g, gain, out_h, gin_h, gwq_h, gwk_h, gwv_h, gwo_h, gwup_h, gwdown_h, gga_h, ggf_h, sems):
    pieces = [(g.at[pl.ds(ROW_DOWN, FF)], gwdown_h)]
    pieces += [(g.at[pl.ds(ROW_UP + j * 512, 512)], gwup_h.at[:, pl.ds(j * 512, 512)]) for j in range(4)]
    pieces += [(g.at[pl.ds(row, 512)], dst) for row, dst in ((ROW_O, gwo_h), (ROW_Q, gwq_h), (ROW_K, gwk_h), (ROW_V, gwv_h))]
    pieces += [(out, out_h), (gin, gin_h), (gain.at[pl.ds(0, 1)], gga_h), (gain.at[pl.ds(1, 1)], ggf_h)]
    copies = [pltpu.make_async_copy(src, dst, sems.at[i]) for i, (src, dst) in enumerate(pieces)]
    for copy in copies:
        copy.start()
    for copy in copies:
        copy.wait()


def per_device(
    inputs, w_query, w_key, w_value, w_output, w_up, w_down, gain_attn, gain_ffn, random_features, doc_ids, live_rows, cotangent):
    hbm = pl.BlockSpec(memory_space=pltpu.HBM)
    vmem = pl.BlockSpec(memory_space=pltpu.VMEM)
    f32 = lambda *shape: jax.ShapeDtypeStruct(shape, F32)
    low = jax.ShapeDtypeStruct((T, D), BF16)
    held = pl.pallas_call(
        kernel,
        out_shape=(pltpu.VMEM((T, D), BF16), pltpu.VMEM((T, D), BF16), pltpu.VMEM((6144, 512), F32), pltpu.VMEM((8, D), F32)),
        in_specs=[hbm] * 9 + [vmem] * 4,
        out_specs=(vmem,) * 4,
        scratch_shapes=[pltpu.VMEM(shape, dtype) for _, shape, dtype in SCRATCH] + [sem for _, sem in SEMS],
        compiler_params=pltpu.CompilerParams(collective_id=0, has_side_effects=True, vmem_limit_bytes=VMEM_LIMIT),
    )(
        *[pltpu.with_memory_space_constraint(v, pltpu.HBM) for v in (
            inputs[0], w_query, w_key, w_value, w_output, w_up, w_down, random_features, cotangent[0])],
        gain_attn[None], gain_ffn[None], doc_ids, live_rows)
    outs = pl.pallas_call(
        store_kernel,
        out_shape=(low, low, f32(D, D), f32(D, D), f32(D, D), f32(D, D), f32(D, FF), f32(FF, D), f32(1, D), f32(1, D)),
        in_specs=[vmem] * 4,
        out_specs=(hbm,) * 10,
        scratch_shapes=[pltpu.SemaphoreType.DMA((13,))],
        compiler_params=pltpu.CompilerParams(vmem_limit_bytes=1 * 2**20),
    )(*held)
    return (outs[0][None], outs[1][None]) + tuple(outs[2:8]) + (outs[8][0], outs[9][0])


def solution(mesh):
    rows = P("pack", "seq", None)
    return jax.shard_map(
        per_device,
        mesh=mesh,
        in_specs=(rows,) + (P(),) * 9 + (P("pack", "seq"), P("pack", "seq"), rows),
        out_specs=(rows, rows) + (P(),) * 8,
        check_vma=False,
    )
```
